256 devices in a mesh: grid: 4 (over y), gx: 8 (over x, core), gy: 8 (over z).
Axes of the slice: x: 4, y: 4, z: 8, core: 2. Of those that a mesh axis runs over, the one named last changes fastest.
Arguments:
- deck_fields: float32 [3, 32, 512, 384], P(None, None, ('grid', 'gx', 'gy')), may hold values from -6 to 6
- back_fields: float32 [3, 32, 512, 1024], P(None, None, ('grid', 'gx'), 'gy'), may hold values from -6 to 6
- metrics: float32 [4, 512, 384], P(None, ('grid', 'gx', 'gy'))
- donors: int32 [256, 512, 1], P(('grid', 'gx', 'gy')), may hold values from 0 to 63; in each aligned block of 512 rows (0 to 511, 512 to 1023, ..., all dimensions but the last counted through in order) at most 16 rows name the same one
- stencil: int32 [256, 512, 4], P(('grid', 'gx', 'gy')), may hold values from 0 to 382, as said below
- fringe_cells: int32 [256, 508], P(('grid', 'gx', 'gy')), may hold values from 0 to 2047, as said below
Outputs:
- deck_final: float32 [3, 32, 512, 384], P(None, None, ('grid', 'gx', 'gy'))
- back_final: float32 [3, 32, 512, 1024], P(None, None, ('grid', 'gx'), 'gy')
The draws below stay inside these ranges and needn't reach their ends.
Inputs may be any that keep to these rules, and one draw needn't show every extreme that they name: `donors`: at most 16 rows of one tile name the same donor, and some tile's rows reach that in every draw. `stencil`: the first 4 rows of each tile have base row below 15 and base column below 127, the others base row below 1 and base column below 383; fractions 0 to 16. `fringe_cells`: distinct within a tile; the block's last cell is always among them.
All inputs are finite; a program needn't handle non-finite values.
Results may differ from the reference program's by a relative error of at most 0.0001.
Values sent between devices are 32-bit elements; how exact they have to be, the bound alone decides.
No kernel may reach another device: no remote copies, remote signals or barrier semaphores. Data moves between devices by JAX's collectives and lax.ppermute only.
A program may use at most 64 MiB of HBM per device.

```python
import math
import jax
import jax.numpy as jnp
import numpy as np
from jax import lax

SPAN = 32
DY = 384
FRL = 2
DX_DEV = 2
BX_DEV = 16
BY_DEV = 128
FR_DEV = 512
TILES = 256
NDX = 512
NBX = 512
NBY = 1024
FRD = 4
FRB = 508
CAP = 16
N_GX = 8
N_GY = 8


def draw_metrics(key, part):
    key = jax.random.fold_in(key, 23)
    first, second = jax.random.split(key)
    diagonal = jnp.exp(jax.random.uniform(first, (2, NDX, DY), jnp.float32, math.log(0.5), math.log(2.0)))
    offside = jax.random.uniform(second, (2, NDX, DY), jnp.float32, -0.5, 0.5)
    return jnp.stack([diagonal[0], offside[0], offside[1], diagonal[1]], axis=0).astype(jnp.float32)


def draw_stencil(key, part):
    key = jax.random.fold_in(key, 11)
    key_list = jax.random.split(key, 4)
    grid_shape = (TILES, FR_DEV)
    on_back = jnp.arange(FR_DEV) < FRD
    row_limit = jnp.where(on_back, BX_DEV - 1, DX_DEV - 1)
    col_limit = jnp.where(on_back, BY_DEV - 1, DY - 1)
    row_values = jax.random.randint(key_list[0], grid_shape, 0, row_limit)
    col_values = jax.random.randint(key_list[1], grid_shape, 0, col_limit)
    frac_first = jax.random.randint(key_list[2], grid_shape, 0, 17)
    frac_second = jax.random.randint(key_list[3], grid_shape, 0, 17)
    col_values = col_values.at[0, FR_DEV - 1].set(DY - 2)
    frac_first = frac_first.at[0, 0].set(16)
    return jnp.stack([row_values, col_values, frac_first, frac_second], axis=-1).astype(jnp.int32)


def draw_fringe_cells(key, part):
    key = jax.random.fold_in(key, 37)
    key_list = jax.random.split(key, TILES)
    last_cell = BX_DEV * BY_DEV - 1

    def pick(subkey):
        chosen = jax.random.permutation(subkey, last_cell)[:FRB - 1]
        return jnp.concatenate([chosen, jnp.full((1,), last_cell, jnp.int32)])
    return jax.vmap(pick)(key_list).astype(jnp.int32)


def levels(stream_key, dims, shards, low, high):
    gain = 1.0
    for axis_at, parts in shards:
        steps = jax.random.uniform(jax.random.fold_in(jax.random.fold_in(stream_key, 6), axis_at), (parts,), jnp.float32, low / len(shards), high / len(shards))
        gain = gain * jnp.repeat(jnp.exp(steps), dims[axis_at] // parts).reshape((-1,) + (1,) * (len(dims) - 1 - axis_at))
    return gain


def routed_block(stream_key, own, number, rows, amount, top, bound, slope):
    ranking = jax.random.permutation(stream_key, amount)
    crowded, common = load_shares(amount, rows * top, bound, slope, True), load_shares(amount, rows * top, bound, slope, False)
    places = jnp.arange(amount)

    def named(lengths, turn):
        used = int((lengths > 0).sum())
        fixed = max(1, used // 4)
        moved = fixed + (places - fixed + turn * (used - fixed)) % max(1, amount - fixed)
        return jnp.zeros((amount,), jnp.int32).at[ranking[jnp.where(places < fixed, places, moved)]].set(jnp.asarray(lengths, jnp.int32))

    lengths = jnp.where(number % 4 == 0, named(crowded, number // 4), named(common, number - number // 4 - 1))
    mixed = jax.random.permutation(jax.random.fold_in(own, 3), amount)
    giver, taker = mixed[0:amount // 2 * 2:2], mixed[1:amount // 2 * 2:2]
    slack = jnp.minimum(lengths[giver] - 1, bound - lengths[taker]) // 2
    slack = jnp.where((giver == ranking[0]) | (taker == ranking[0]) | (lengths[taker] == 0), 0, jnp.maximum(slack, 0))
    moved = jax.random.randint(jax.random.fold_in(own, 4), (amount // 2,), 0, 1 << 20) % (slack + 1)
    lengths = lengths.at[giver].add(-moved).at[taker].add(moved)
    labels = jnp.searchsorted(jnp.cumsum(lengths), jnp.arange(rows * top), side="right").astype(jnp.int32)
    listing = labels.reshape(top, rows).T
    listing = listing[jax.random.permutation(jax.random.fold_in(own, 1), rows)]
    turn = jax.random.randint(jax.random.fold_in(own, 2), (rows, 1), 0, top)
    return jnp.take_along_axis(listing, (jnp.arange(top)[None, :] + turn) % top, axis=1)


def load_shares(count, total, limit, lean, full):
    loads = [(1 << 20) // math.isqrt(grade ** lean) + 1 for grade in range(1, count + 1)]
    largest = limit if full else min(limit, max(-(-total // count), total * loads[0] // sum(loads)))
    least = 1 if total - largest >= count - 1 else 0
    counts, spare = [largest] + [least] * (count - 1), total - largest - least * (count - 1)
    while spare > 0:
        movable = [i for i in range(1, count) if counts[i] < largest] or [i for i in range(1, count) if counts[i] < limit]
        whole, left = sum([loads[i] for i in movable]), spare
        for i in movable:
            more = min(limit - counts[i], max(1, left * loads[i] // whole), spare)
            counts[i] = counts[i] + more
            spare = spare - more
    return np.array(counts)


def bell_draw(stream_key, extent, scale, limit, shards=(), kind=jnp.bfloat16):
    loudness = levels(stream_key, extent, shards, -0.22, 0.18) if shards else 1.0
    entries = jax.random.normal(stream_key, extent, jnp.float32) * scale * loudness
    return jnp.minimum(jnp.maximum(entries, -limit), limit).astype(kind)


def setup_inputs(seed: int = 0) -> dict:
    splits = jax.random.split(jax.random.key(seed), 7)
    deck_fields = bell_draw(splits[0], (3, SPAN, NDX, DY), 1.0, 6.0, ((2, 256),), jnp.float32)
    back_fields = bell_draw(splits[1], (3, SPAN, NBX, NBY), 1.0, 6.0, ((2, 32), (3, 8)), jnp.float32)
    metrics = draw_metrics(jax.random.fold_in(splits[6], 71), 0)
    donors_keys = jax.random.split(jax.random.fold_in(splits[3], 1), TILES * FR_DEV // FR_DEV)
    donors_turns = jax.random.permutation(jax.random.fold_in(splits[3], 3), TILES * FR_DEV // FR_DEV)
    donors = jax.vmap(lambda own, number: routed_block(jax.random.fold_in(splits[3], 2), own, number, FR_DEV, N_GX * N_GY, 1, CAP, 2))(donors_keys, donors_turns).reshape((TILES, FR_DEV, 1))
    stencil = draw_stencil(jax.random.fold_in(splits[6], 71), 0)
    fringe_cells = draw_fringe_cells(jax.random.fold_in(splits[6], 71), 0)
    return dict(deck_fields=deck_fields, back_fields=back_fields, metrics=metrics, donors=donors, stencil=stencil, fringe_cells=fringe_cells)


time_step = 0.05
smagorinsky = 0.02

def tendency(fields, padded, metric):
    plus_xi = padded[:, :, 2:, 1:-1]
    minus_xi = padded[:, :, :-2, 1:-1]
    plus_eta = padded[:, :, 1:-1, 2:]
    minus_eta = padded[:, :, 1:-1, :-2]
    plus_span = jnp.roll(fields, -1, axis=1)
    minus_span = jnp.roll(fields, 1, axis=1)
    along_xi = 0.5 * (plus_xi - minus_xi)
    along_eta = 0.5 * (plus_eta - minus_eta)
    along_span = 0.5 * (plus_span - minus_span)
    strain = lax.optimization_barrier(jnp.sum(along_xi * along_xi + along_eta * along_eta + along_span * along_span, axis=0))
    viscosity = smagorinsky * jnp.sqrt(1.0 + strain)
    if metric is None:
        speed_xi = fields[0]
        speed_eta = fields[1]
        scale_xi = 1.0
        scale_eta = 1.0
    else:
        speed_xi = metric[0] * fields[0] + metric[1] * fields[1]
        speed_eta = metric[2] * fields[0] + metric[3] * fields[1]
        scale_xi = metric[0] * metric[0] + metric[1] * metric[1]
        scale_eta = metric[2] * metric[2] + metric[3] * metric[3]
    advection = speed_xi * along_xi + speed_eta * along_eta + fields[2] * along_span
    doubled = 2.0 * fields
    diffusion = scale_xi * (plus_xi - doubled + minus_xi) + scale_eta * (plus_eta - doubled + minus_eta) + (plus_span - doubled + minus_span)
    return viscosity * diffusion - advection

def bilinear(values_flat, position, stride, frac_row, frac_col):
    low_low = values_flat[:, position]
    high_low = values_flat[:, position + stride]
    low_high = values_flat[:, position + 1]
    high_high = values_flat[:, position + stride + 1]
    return (1.0 - frac_row) * (1.0 - frac_col) * low_low + frac_row * (1.0 - frac_col) * high_low + (1.0 - frac_row) * frac_col * low_high + frac_row * frac_col * high_high

def reference(deck_fields, back_fields, metrics, donors, stencil, fringe_cells):
    members = N_GX * N_GY
    planes = 3 * SPAN
    nearby = DX_DEV * FRL
    tile_ids = jnp.arange(TILES, dtype=jnp.int32)
    grid_block = tile_ids // members
    own_member = tile_ids % members
    donor_ids = donors[:, :, 0]
    donor_tile = grid_block[:, None] * members + donor_ids
    donor_gx = donor_ids // N_GY
    donor_gy = donor_ids % N_GY
    base_row = stencil[:, :, 0]
    base_col = stencil[:, :, 1]
    frac_row = stencil[:, :, 2].astype(jnp.float32) / 16.0
    frac_col = stencil[:, :, 3].astype(jnp.float32) / 16.0
    back_start = (grid_block[:, None] * N_GX + donor_gx) * BX_DEV
    back_position = ((back_start + base_row) * NBY + donor_gy * BY_DEV + base_col)[:, :nearby].reshape(-1)
    deck_position = ((donor_tile * DX_DEV + base_row) * DY + base_col)[:, nearby:].reshape(-1)
    near_row = frac_row[:, :nearby].reshape(-1)
    near_col = frac_col[:, :nearby].reshape(-1)
    far_row = frac_row[:, nearby:].reshape(-1)
    far_col = frac_col[:, nearby:].reshape(-1)
    own_gx = own_member // N_GY
    own_gy = own_member % N_GY
    cell_row = fringe_cells // BY_DEV
    cell_col = fringe_cells % BY_DEV
    targets = ((((grid_block * N_GX + own_gx) * BX_DEV)[:, None] + cell_row) * NBY + (own_gy * BY_DEV)[:, None] + cell_col).reshape(-1)
    keep_back = 1.0 - jnp.zeros((NBX * NBY,), jnp.float32).at[targets].set(1.0).reshape(NBX, NBY)
    keep_deck = (jnp.arange(DY) < DY - FRL).astype(jnp.float32)
    metric = (metrics[0], metrics[1], metrics[2], metrics[3])

    def fill(deck_state, back_state):
        deck_flat = deck_state.reshape(planes, NDX * DY)
        back_flat = back_state.reshape(planes, NBX * NBY)
        to_deck = bilinear(back_flat, back_position, NBY, near_row, near_col)
        to_back = bilinear(deck_flat, deck_position, DY, far_row, far_col)
        deck_state = deck_state.at[:, :, :, DY - FRL:].set(to_deck.reshape(3, SPAN, NDX, FRL))
        back_state = back_flat.at[:, targets].set(to_back).reshape(back_state.shape)
        return (deck_state, back_state)
    deck_state, back_state = (deck_fields, back_fields)
    base_deck, base_back = (deck_fields, back_fields)
    for section_index in range(3):
        deck_state, back_state = fill(deck_state, back_state)
        if section_index == 0:
            base_deck, base_back = (deck_state, back_state)
        wrapped = jnp.concatenate([deck_state[:, :, -1:], deck_state, deck_state[:, :, :1]], axis=2)
        deck_padded = jnp.pad(wrapped, ((0, 0), (0, 0), (0, 0), (1, 1)))
        back_padded = jnp.pad(back_state, ((0, 0), (0, 0), (1, 1), (1, 1)))
        deck_next = deck_state + time_step * keep_deck * tendency(deck_state, deck_padded, metric)
        back_next = back_state + time_step * keep_back * tendency(back_state, back_padded, None)
        if section_index == 1:
            deck_next = 0.75 * base_deck + 0.25 * deck_next
            back_next = 0.75 * base_back + 0.25 * back_next
        elif section_index == 2:
            deck_next = base_deck / 3.0 + 2.0 / 3.0 * deck_next
            back_next = base_back / 3.0 + 2.0 / 3.0 * back_next
        deck_state, back_state = (deck_next, back_next)
    return (deck_state, back_state)
```

```python
import functools

import jax
import jax.numpy as jnp
from jax import lax
from jax.experimental import pallas as pl
from jax.experimental.pallas import tpu as pltpu
from jax.sharding import PartitionSpec as P

SPAN = 32
PLANES = 96
MEMBERS = 64
CAP = 16
SLOTS = MEMBERS * CAP
ROWS = 16
COLS = 128
DROWS = 2
DCOLS = 384
FRINGE = 512
NEAR = 4
TIME_STEP = 0.05
SMAGORINSKY = 0.02
F32 = jnp.float32
BF16 = jnp.bfloat16
NT = (((1,), (1,)), ((), ()))
NN = (((1,), (0,)), ((), ()))
VMEM_LIMIT = 48 * 1024 * 1024
PACKED = CAP * PLANES
R_ROW, R_COL, R_FX, R_FY, R_GRID = range(5)


def dot(a, b, dims):
    return lax.dot_general(a, b, dims, preferred_element_type=F32)


def iota(shape, dim):
    return lax.broadcasted_iota(jnp.int32, shape, dim)


def call(kernel, outs, ins, scratch=(), any_at=(), name=None):
    def spec(i):
        return pl.BlockSpec(memory_space=pl.ANY if i in any_at else pltpu.VMEM)

    return pl.pallas_call(
        kernel,
        out_shape=tuple(jax.ShapeDtypeStruct(s, d) for s, d in outs),
        in_specs=[spec(i) for i in range(len(ins))],
        out_specs=tuple(pl.BlockSpec(memory_space=pltpu.VMEM) for _ in outs),
        scratch_shapes=list(scratch),
        compiler_params=pltpu.CompilerParams(vmem_limit_bytes=VMEM_LIMIT),
        name=name,
    )(*ins)


def route_kernel(donors_ref, stencil_ref, cells_ref, request_ref, local_ref):
    donors = donors_ref[...]
    member = (iota((MEMBERS, FRINGE), 0) == donors).astype(F32)
    before = (iota((FRINGE, FRINGE), 0) < iota((FRINGE, FRINGE), 1)).astype(BF16)
    member_b = member.astype(BF16)
    earlier = dot(member_b, before, NN)
    rank = jnp.sum(member * earlier, axis=0, keepdims=True).astype(jnp.int32)
    at_rank = (iota((CAP, FRINGE), 0) == rank).astype(F32)

    def place(values):
        stacked = jnp.concatenate([at_rank * v.astype(F32) for v in values], axis=0)
        return dot(member_b, stacked.astype(BF16), NT)

    row = stencil_ref[0:1, :]
    col = stencil_ref[1:2, :]
    lane = iota((1, FRINGE), 1)
    grid = jnp.where(lane < NEAR, 1, 2)
    half = col >> 1
    sent = place([row, half, col - 2 * half, stencil_ref[2:3, :], stencil_ref[3:4, :], grid])
    request_ref[:, 0, :] = jnp.zeros((MEMBERS, 128), F32)
    request_ref[:, 0, 0:16] = sent[:, 0:16]
    request_ref[:, 0, 16:32] = 2.0 * sent[:, 16:32] + sent[:, 32:48]
    request_ref[:, 0, 32:80] = sent[:, 48:96]
    cells = cells_ref[...]
    far = lane >= NEAR
    local_ref[...] = place(
        [
            jnp.where(far, (cells >> 7) + 1, 0),
            jnp.where(far, cells & 127, 0),
            jnp.where(far, 0, lane + 1),
        ]
    )


def prepare_kernel(local_ref, deck_ref, back_ref, fill_ref, near_ref, keep_ref, deck_out, back_out):
    for r in range(ROWS):
        back_out[r] = back_ref[:, r, :]
    for r in range(DROWS):
        deck_out[r] = deck_ref[:, r, :]
    lane = iota((MEMBERS, COLS), 1)
    lane2 = iota((MEMBERS, 2 * COLS), 1)
    listed = [jnp.zeros((1, COLS), F32) for _ in range(ROWS)]
    for s in range(CAP):
        row = local_ref[:, s : s + 1].astype(jnp.int32) - 1
        col = local_ref[:, CAP + s : CAP + s + 1].astype(jnp.int32)
        hit = jnp.where(lane == col, 1.0, 0.0)
        for r in range(ROWS):
            here = jnp.where(row == r, hit, 0.0)
            fill_ref[s * MEMBERS : (s + 1) * MEMBERS, r * COLS : (r + 1) * COLS] = here.astype(BF16)
            listed[r] = listed[r] + jnp.sum(here, axis=0, keepdims=True)
        if s < NEAR:
            near = local_ref[:, 2 * CAP + s : 2 * CAP + s + 1].astype(jnp.int32) - 1
            place = jnp.where(near >= 0, (near >> 1) * COLS + COLS - 2 + (near & 1), -1)
            near_ref[s * MEMBERS : (s + 1) * MEMBERS, :] = jnp.where(lane2 == place, 1.0, 0.0).astype(BF16)
    for r in range(ROWS):
        keep_ref[r] = 1.0 - jnp.broadcast_to(listed[r], (8, COLS))


def split(x):
    high = x.astype(BF16)
    return high, (x - high.astype(F32)).astype(BF16)


def weights(request_ref, far_ref, near_ref):
    wide = iota((MEMBERS, DCOLS), 1)
    lane = iota((MEMBERS, COLS), 1)
    for s in range(CAP):

        def field(f):
            at = f * CAP + s
            return request_ref[:, 0, at : at + 1]

        col = field(R_COL).astype(jnp.int32)
        fx = field(R_FX) / 16.0
        fy = field(R_FY) / 16.0
        grid = field(R_GRID)
        at = slice(s * MEMBERS, (s + 1) * MEMBERS)
        on_deck = jnp.where(grid == 2.0, 1.0, 0.0)
        low, high = on_deck * (1.0 - fy), on_deck * fy
        across = jnp.where(wide == col, low, jnp.where(wide == col + 1, high, 0.0))
        far_ref[at, 0:DCOLS] = ((1.0 - fx) * across).astype(BF16)
        far_ref[at, DCOLS : 2 * DCOLS] = (fx * across).astype(BF16)
        if s < NEAR:
            row = field(R_ROW).astype(jnp.int32)
            on_back = jnp.where(grid == 1.0, 1.0, 0.0)
            low, high = on_back * (1.0 - fy), on_back * fy
            across = jnp.where(lane == col, low, jnp.where(lane == col + 1, high, 0.0))
            for r in range(ROWS):
                share = jnp.where(row == r, 1.0 - fx, jnp.where(row + 1 == r, fx, 0.0))
                near_ref[at, r * COLS : (r + 1) * COLS] = (share * across).astype(BF16)


def stack_deck(pieces, r, value):
    high, low = split(value)
    pieces[0:PLANES, r * DCOLS : (r + 1) * DCOLS] = high
    pieces[128 : 128 + PLANES, r * DCOLS : (r + 1) * DCOLS] = low


def stack_back(pieces, r, value):
    high, low = split(value)
    pieces[0:PLANES, r * COLS : (r + 1) * COLS] = high
    pieces[128 : 128 + PLANES, r * COLS : (r + 1) * COLS] = low


def clear_pieces(deck_pieces, back_pieces):
    for pieces in (deck_pieces, back_pieces):
        gap = jnp.zeros((128 - PLANES, pieces.shape[1]), BF16)
        pieces[PLANES:128, :] = gap
        pieces[128 + PLANES : 256, :] = gap


def answer(far_ref, near_ref, deck_pieces, back_pieces, out_ref):
    lane = iota((MEMBERS, 128), 1)
    for q in range(CAP // 4):
        got = dot(far_ref[q * 256 : (q + 1) * 256, :], deck_pieces[...], NT)
        if q == 0:
            got = got + dot(near_ref[...], back_pieces[...], NT)
        got = got[:, 0:128] + got[:, 128:256]
        a = [got[i * MEMBERS : (i + 1) * MEMBERS, :] for i in range(4)]
        base = q * 4 * PLANES
        out_ref[:, 0, base : base + 128] = jnp.where(lane < 96, a[0], pltpu.roll(a[1], 96, 1))
        out_ref[:, 0, base + 128 : base + 256] = jnp.where(
            lane < 64, pltpu.roll(a[1], 96, 1), pltpu.roll(a[2], 64, 1)
        )
        out_ref[:, 0, base + 256 : base + 384] = jnp.where(
            lane < 32, pltpu.roll(a[2], 64, 1), pltpu.roll(a[3], 32, 1)
        )


def first_answer_kernel(request_ref, deck_ref, back_ref, far_ref, near_ref, out_ref, deck_pieces, back_pieces):
    weights(request_ref, far_ref, near_ref)
    clear_pieces(deck_pieces, back_pieces)
    for r in range(DROWS):
        stack_deck(deck_pieces, r, deck_ref[r])
    for r in range(ROWS):
        stack_back(back_pieces, r, back_ref[r])
    answer(far_ref, near_ref, deck_pieces, back_pieces, out_ref)


def fill_kernel(
    got_ref, fill_hbm, near_ref, keep_ref, deck_ref, back_ref,
    deck_out, back_out, north_out, south_out, west_out, east_out,
    fill_ref, got_pieces, sems,
):
    chunks = ROWS // 2
    copies = []
    for c in range(chunks):
        at = pl.ds(c * 256, 256)
        copies.append(pltpu.make_async_copy(fill_hbm.at[:, at], fill_ref.at[:, at], sems.at[c]))
        copies[c].start()
    lane = iota((MEMBERS, 128), 1)
    for q in range(CAP // 4):
        base = q * 4 * PLANES
        c0 = got_ref[:, 0, base : base + 128]
        c1 = got_ref[:, 0, base + 128 : base + 256]
        c2 = got_ref[:, 0, base + 256 : base + 384]
        a0 = jnp.where(lane < 96, c0, 0.0)
        a1 = jnp.where(lane < 32, pltpu.roll(c0, 32, 1), jnp.where(lane < 96, pltpu.roll(c1, 32, 1), 0.0))
        a2 = jnp.where(lane < 64, pltpu.roll(c1, 64, 1), jnp.where(lane < 96, pltpu.roll(c2, 64, 1), 0.0))
        a3 = jnp.where(lane < 96, pltpu.roll(c2, 96, 1), 0.0)
        across = jnp.concatenate([a0, a1, a2, a3], axis=0).T
        high, low = split(across[0:PLANES, :])
        got_pieces[0:PLANES, q * 256 : (q + 1) * 256] = high
        got_pieces[PLANES : 2 * PLANES, q * 256 : (q + 1) * 256] = low
    near = dot(got_pieces[:, 0:256], near_ref[...], NN)
    near = near[0:PLANES] + near[PLANES : 2 * PLANES]
    lane = iota((PLANES, 128), 1)
    for r in range(DROWS):
        side = west_out if r == 0 else east_out
        outer = jnp.where(lane >= 126, near[:, r * 128 : (r + 1) * 128], deck_ref[r, :, 256:384])
        deck_out[r, :, 0:256] = deck_ref[r, :, 0:256]
        deck_out[r, :, 256:384] = outer
        side[:, 0:256] = deck_ref[r, :, 0:256]
        side[:, 256:384] = outer
    west = jnp.zeros((PLANES, 128), F32)
    east = jnp.zeros((PLANES, 128), F32)
    for c in range(chunks):
        copies[c].wait()
        new = dot(got_pieces[...], fill_ref[:, c * 256 : (c + 1) * 256], NN)
        new = new[0:PLANES] + new[PLANES : 2 * PLANES]
        for half in range(2):
            r = 2 * c + half
            state = back_ref[r] * keep_ref[r, 0:1, :] + new[:, half * 128 : (half + 1) * 128]
            back_out[r] = state
            if r == 0:
                north_out[...] = state
            if r == ROWS - 1:
                south_out[...] = state
            west = jnp.where(lane == r, state[:, 0:1], west)
            east = jnp.where(lane == r, state[:, 127:128], east)
    west_out[:, 384:512] = west
    east_out[:, 384:512] = east


def update(here, minus_xi, plus_xi, minus_eta, plus_eta, metric, keep, base, section):
    d_xi, d_eta, d_span, lap = [], [], [], []
    strain = None
    for c in range(3):
        f = here[c]
        plus_span = jnp.concatenate([f[1:], f[:1]], axis=0)
        minus_span = jnp.concatenate([f[-1:], f[:-1]], axis=0)
        a = plus_xi[c] - minus_xi[c]
        b = plus_eta[c] - minus_eta[c]
        s = plus_span - minus_span
        square = a * a + b * b + s * s
        strain = square if strain is None else strain + square
        doubled = 2.0 * f
        l_xi = plus_xi[c] - doubled + minus_xi[c]
        l_eta = plus_eta[c] - doubled + minus_eta[c]
        if metric is not None:
            l_xi, l_eta = metric[4] * l_xi, metric[5] * l_eta
        lap.append(l_xi + l_eta + (plus_span - doubled + minus_span))
        d_xi.append(a)
        d_eta.append(b)
        d_span.append(s)
    viscosity = SMAGORINSKY * jnp.sqrt(1.0 + 0.25 * strain)
    if metric is None:
        speed_xi, speed_eta = here[0], here[1]
    else:
        speed_xi = metric[0] * here[0] + metric[1] * here[1]
        speed_eta = metric[2] * here[0] + metric[3] * here[1]
    out = []
    for c in range(3):
        advection = 0.5 * (speed_xi * d_xi[c] + speed_eta * d_eta[c] + here[2] * d_span[c])
        tendency = viscosity * lap[c] - advection
        if section == 0:
            out.append(here[c] + (TIME_STEP * keep) * tendency)
        elif section == 1:
            out.append(0.75 * base[c] + 0.25 * here[c] + (0.25 * TIME_STEP * keep) * tendency)
        else:
            out.append(base[c] * (1.0 / 3.0) + (2.0 / 3.0) * here[c] + (2.0 / 3.0 * TIME_STEP * keep) * tendency)
    return out


def fields(ref, at):
    return [ref[at + (slice(c * SPAN, (c + 1) * SPAN), slice(None))] for c in range(3)]


def section_kernel(section, *refs):
    refs = list(refs)
    deck_ref, back_ref, north_ref, south_ref, west_ref, east_ref, ends_ref, metric_ref, keep_ref = refs[:9]
    del refs[:9]
    base_deck = base_back = None
    if section > 0:
        base_deck, base_back = refs[:2]
        del refs[:2]
    last = section == 2
    if last:
        deck_out, back_out = refs
    else:
        far_hbm, near_hbm, deck_out, back_out, answer_out, deck_pieces, back_pieces, far_ref, near_ref, sems = refs
        copies = [
            pltpu.make_async_copy(far_hbm, far_ref, sems.at[0]),
            pltpu.make_async_copy(near_hbm, near_ref, sems.at[1]),
        ]
        for c in copies:
            c.start()
        clear_pieces(deck_pieces, back_pieces)
    lane = iota((SPAN, DCOLS), 1)
    keep_deck = jnp.where(iota((1, DCOLS), 1) < DCOLS - 2, 1.0, 0.0)
    for r in range(DROWS):
        here = fields(deck_ref, (r,))
        if r == 0:
            minus = [east_ref[c * SPAN : (c + 1) * SPAN, 0:DCOLS] for c in range(3)]
            plus = fields(deck_ref, (1,))
        else:
            minus = fields(deck_ref, (0,))
            plus = [west_ref[c * SPAN : (c + 1) * SPAN, 0:DCOLS] for c in range(3)]
        m = [metric_ref[i, r : r + 1, :] for i in range(4)]
        metric = m + [m[0] * m[0] + m[1] * m[1], m[2] * m[2] + m[3] * m[3]]
        plus_eta = [jnp.where(lane == DCOLS - 1, 0.0, pltpu.roll(f, DCOLS - 1, 1)) for f in here]
        minus_eta = [jnp.where(lane == 0, 0.0, pltpu.roll(f, 1, 1)) for f in here]
        base = fields(base_deck, (r,)) if section > 0 else None
        new = update(here, minus, plus, minus_eta, plus_eta, metric, keep_deck, base, section)
        for c in range(3):
            if last:
                deck_out[c * SPAN : (c + 1) * SPAN, r, :] = new[c]
            else:
                deck_out[r, c * SPAN : (c + 1) * SPAN, :] = new[c]
        if not last:
            stack_deck(deck_pieces, r, jnp.concatenate(new, axis=0))
    lane = iota((SPAN, COLS), 1)
    west_end = ends_ref[0]
    east_end = ends_ref[1]
    for r in range(ROWS):
        here = fields(back_ref, (r,))
        minus = fields(back_ref, (r - 1,)) if r > 0 else fields(south_ref, ())
        plus = fields(back_ref, (r + 1,)) if r < ROWS - 1 else fields(north_ref, ())
        plus_eta, minus_eta = [], []
        for c in range(3):
            at = slice(c * SPAN, (c + 1) * SPAN)
            from_east = west_ref[at, DCOLS + r : DCOLS + r + 1] * east_end
            from_west = east_ref[at, DCOLS + r : DCOLS + r + 1] * west_end
            plus_eta.append(jnp.where(lane == COLS - 1, from_east, pltpu.roll(here[c], COLS - 1, 1)))
            minus_eta.append(jnp.where(lane == 0, from_west, pltpu.roll(here[c], 1, 1)))
        base = fields(base_back, (r,)) if section > 0 else None
        new = update(here, minus, plus, minus_eta, plus_eta, None, keep_ref[r, 0:1, :], base, section)
        for c in range(3):
            if last:
                back_out[c * SPAN : (c + 1) * SPAN, r, :] = new[c]
            else:
                back_out[r, c * SPAN : (c + 1) * SPAN, :] = new[c]
        if not last:
            stack_back(back_pieces, r, jnp.concatenate(new, axis=0))
    if not last:
        for c in copies:
            c.wait()
        answer(far_ref, near_ref, deck_pieces, back_pieces, answer_out)


def local(deck_fields, back_fields, metrics, donors, stencil, fringe_cells):
    group = ("gx", "gy")
    everyone = ("grid", "gx", "gy")

    def exchange(x):
        return lax.all_to_all(x, group, split_axis=0, concat_axis=0, tiled=True)

    count = lax.axis_size("grid") * lax.axis_size("gx") * lax.axis_size("gy")
    across_y = lax.axis_size("gy")
    onward = [(i, (i + 1) % count) for i in range(count)]
    back = [(j, i) for i, j in onward]
    down = [(i, i + across_y) for i in range(count - across_y)]
    up = [(j, i) for i, j in down]

    deck_in = deck_fields.reshape(PLANES, DROWS, DCOLS)
    back_in = back_fields.reshape(PLANES, ROWS, COLS)
    cells = jnp.pad(fringe_cells, ((0, 0), (NEAR, 0)))
    request, placing = call(
        route_kernel,
        [((MEMBERS, 1, 128), F32), ((MEMBERS, 3 * CAP), F32)],
        [donors.reshape(1, FRINGE), stencil.reshape(FRINGE, 4).T, cells],
        name="route",
    )
    request = exchange(request)
    fill_map, near_map, keep, deck, back_state = call(
        prepare_kernel,
        [
            ((SLOTS, ROWS * COLS), BF16),
            ((NEAR * MEMBERS, 2 * COLS), BF16),
            ((ROWS, 8, COLS), F32),
            ((DROWS, PLANES, DCOLS), F32),
            ((ROWS, PLANES, COLS), F32),
        ],
        [placing, deck_in, back_in],
        name="prepare",
    )
    pieces = [pltpu.VMEM((256, DROWS * DCOLS), BF16), pltpu.VMEM((256, ROWS * COLS), BF16)]
    far, near, answers = call(
        first_answer_kernel,
        [
            ((SLOTS, DROWS * DCOLS), BF16),
            ((NEAR * MEMBERS, ROWS * COLS), BF16),
            ((MEMBERS, 1, PACKED), F32),
        ],
        [request, deck, back_state],
        scratch=pieces,
        name="first_answer",
    )
    column = lax.axis_index("gy")
    ends = jnp.stack([column > 0, column < across_y - 1]).astype(F32)
    base = None
    for section in range(3):
        got = exchange(answers)
        deck, back_state, north, south, west, east = call(
            fill_kernel,
            [
                ((DROWS, PLANES, DCOLS), F32),
                ((ROWS, PLANES, COLS), F32),
                ((PLANES, COLS), F32),
                ((PLANES, COLS), F32),
                ((PLANES, 512), F32),
                ((PLANES, 512), F32),
            ],
            [got, fill_map, near_map, keep, deck, back_state],
            scratch=[
                pltpu.VMEM((SLOTS, ROWS * COLS), BF16),
                pltpu.VMEM((2 * PLANES, SLOTS), BF16),
                pltpu.SemaphoreType.DMA((ROWS // 2,)),
            ],
            any_at=(1,),
            name="fill",
        )
        if section == 0:
            base = [deck, back_state]
        east = lax.ppermute(east, everyone, onward)
        west = lax.ppermute(west, everyone, back)
        south = lax.ppermute(south, everyone, down)
        north = lax.ppermute(north, everyone, up)
        ins = [deck, back_state, north, south, west, east, ends, metrics, keep]
        if section > 0:
            ins += base
        if section < 2:
            at = len(ins)
            ins += [far, near]
            deck, back_state, answers = section_call(
                section,
                [
                    ((DROWS, PLANES, DCOLS), F32),
                    ((ROWS, PLANES, COLS), F32),
                    ((MEMBERS, 1, PACKED), F32),
                ],
                ins,
                pieces
                + [
                    pltpu.VMEM((SLOTS, DROWS * DCOLS), BF16),
                    pltpu.VMEM((NEAR * MEMBERS, ROWS * COLS), BF16),
                    pltpu.SemaphoreType.DMA((2,)),
                ],
                (at, at + 1),
            )
        else:
            deck, back_state = section_call(
                section, [((PLANES, DROWS, DCOLS), F32), ((PLANES, ROWS, COLS), F32)], ins, [], ()
            )
    return deck.reshape(deck_fields.shape), back_state.reshape(back_fields.shape)


def section_call(section, outs, ins, scratch, any_at):
    def spec(i):
        if i == 6:
            return pl.BlockSpec(memory_space=pltpu.SMEM)
        return pl.BlockSpec(memory_space=pl.ANY if i in any_at else pltpu.VMEM)

    return pl.pallas_call(
        functools.partial(section_kernel, section),
        out_shape=tuple(jax.ShapeDtypeStruct(s, d) for s, d in outs),
        in_specs=[spec(i) for i in range(len(ins))],
        out_specs=tuple(pl.BlockSpec(memory_space=pltpu.VMEM) for _ in outs),
        scratch_shapes=scratch,
        compiler_params=pltpu.CompilerParams(vmem_limit_bytes=VMEM_LIMIT),
        name="section",
    )(*ins)


def solution(mesh):
    return jax.shard_map(
        local,
        mesh=mesh,
        in_specs=(
            P(None, None, ("grid", "gx", "gy"), None),
            P(None, None, ("grid", "gx"), "gy"),
            P(None, ("grid", "gx", "gy"), None),
            P(("grid", "gx", "gy"), None, None),
            P(("grid", "gx", "gy"), None, None),
            P(("grid", "gx", "gy"), None),
        ),
        out_specs=(P(None, None, ("grid", "gx", "gy"), None), P(None, None, ("grid", "gx"), "gy")),
        check_vma=False,
    )
```

```python
import functools

import jax
import jax.numpy as jnp
from jax import lax
from jax.experimental import pallas as pl
from jax.experimental.pallas import tpu as pltpu
from jax.sharding import PartitionSpec as P

SPAN = 32
PLANES = 96
MEMBERS = 64
CAP = 16
SLOTS = MEMBERS * CAP
ROWS = 16
COLS = 128
DROWS = 2
DCOLS = 384
FRINGE = 512
NEAR = 4
TIME_STEP = 0.05
SMAGORINSKY = 0.02
F32 = jnp.float32
BF16 = jnp.bfloat16
NT = (((1,), (1,)), ((), ()))
NN = (((1,), (0,)), ((), ()))
VMEM_LIMIT = 24 * 1024 * 1024
PACKED = CAP * PLANES
R_ROW, R_COL, R_FX, R_FY, R_GRID = range(5)


def position():
    column = lax.axis_index("gy")
    line = lax.axis_index("grid") * lax.axis_size("gx") + lax.axis_index("gx")
    tile = line * lax.axis_size("gy") + column
    return column, line, tile


def dot(a, b, dims):
    return lax.dot_general(a, b, dims, preferred_element_type=F32)


def iota(shape, dim):
    return lax.broadcasted_iota(jnp.int32, shape, dim)


def call(kernel, outs, ins, scratch=(), hbm_at=(), name=None):
    def spec(i):
        return pl.BlockSpec(memory_space=pltpu.HBM if i in hbm_at else pltpu.VMEM)

    return pl.pallas_call(
        kernel,
        out_shape=tuple(jax.ShapeDtypeStruct(s, d) for s, d in outs),
        in_specs=[spec(i) for i in range(len(ins))],
        out_specs=tuple(pl.BlockSpec(memory_space=pltpu.VMEM) for _ in outs),
        scratch_shapes=list(scratch),
        compiler_params=pltpu.CompilerParams(vmem_limit_bytes=VMEM_LIMIT),
        name=name,
    )(*ins)


def route_kernel(
    donors_hbm, stencil_hbm, cells_hbm, request_ref, fill_ref, rim_ref, near_ref, keep_ref,
    donors_ref, stencil_ref, cells_ref, local_ref, sems,
):
    pairs = [(donors_hbm, donors_ref), (stencil_hbm, stencil_ref), (cells_hbm, cells_ref)]
    copies = [pltpu.make_async_copy(a, b, sems.at[i]) for i, (a, b) in enumerate(pairs)]
    for c in copies:
        c.start()
    for c in copies:
        c.wait()
    donors = donors_ref[...]
    member = (iota((MEMBERS, FRINGE), 0) == donors).astype(F32)
    before = (iota((FRINGE, FRINGE), 0) < iota((FRINGE, FRINGE), 1)).astype(BF16)
    member_b = member.astype(BF16)
    earlier = dot(member_b, before, NN)
    rank = jnp.sum(member * earlier, axis=0, keepdims=True).astype(jnp.int32)
    at_rank = (iota((CAP, FRINGE), 0) == rank).astype(F32)

    def place(values):
        stacked = jnp.concatenate([at_rank * v.astype(F32) for v in values], axis=0)
        return dot(member_b, stacked.astype(BF16), NT)

    row = stencil_ref[0:1, :]
    col = stencil_ref[1:2, :]
    lane = iota((1, FRINGE), 1)
    grid = jnp.where(lane < NEAR, 1, 2)
    half = col >> 1
    sent = place([row, half, col - 2 * half, stencil_ref[2:3, :], stencil_ref[3:4, :], grid])
    request_ref[:, 0, :] = jnp.zeros((MEMBERS, 128), F32)
    request_ref[:, 0, 0:16] = sent[:, 0:16]
    request_ref[:, 0, 16:32] = 2.0 * sent[:, 16:32] + sent[:, 32:48]
    request_ref[:, 0, 32:80] = sent[:, 48:96]
    cells = jnp.concatenate([jnp.zeros((1, NEAR), jnp.int32), cells_ref[...]], axis=1)
    far = lane >= NEAR
    local_ref[...] = place(
        [
            jnp.where(far, (cells >> 7) + 1, 0),
            jnp.where(far, cells & 127, 0),
            jnp.where(far, 0, lane + 1),
        ]
    )
    landing(local_ref, fill_ref, rim_ref, near_ref, keep_ref)


def landing(local_ref, fill_ref, rim_ref, near_ref, keep_ref):
    lane = iota((MEMBERS, COLS), 1)
    places = local_ref[...].astype(jnp.int32)
    listed = [jnp.zeros((8, COLS), F32) for _ in range(ROWS + 1)]

    def over_eight(x):
        return jnp.sum(x.reshape(MEMBERS // 8, 8, COLS), axis=0)

    for s in range(CAP):
        at = slice(s * MEMBERS, (s + 1) * MEMBERS)
        row = jnp.broadcast_to(places[:, s : s + 1] - 1, (MEMBERS, COLS))
        col = jnp.broadcast_to(places[:, CAP + s : CAP + s + 1], (MEMBERS, COLS))
        hit = jnp.where(lane == col, 1.0, 0.0)
        for r in range(ROWS):
            here = jnp.where(row == r, hit, 0.0)
            fill_ref[at, r * COLS : (r + 1) * COLS] = here.astype(BF16)
            listed[r] = listed[r] + over_eight(here)
            if r == 0:
                rim_ref[at, 0:COLS] = here.astype(BF16)
            if r == ROWS - 1:
                rim_ref[at, COLS : 2 * COLS] = here.astype(BF16)
        side = jnp.where(col == 0, row, jnp.where(col == COLS - 1, row + ROWS, -1))
        here = jnp.where((lane == side) & (row >= 0), 1.0, 0.0)
        rim_ref[at, 2 * COLS : 3 * COLS] = here.astype(BF16)
        listed[ROWS] = listed[ROWS] + over_eight(here)
        if s < NEAR:
            near = places[:, 2 * CAP + s : 2 * CAP + s + 1] - 1
            place = jnp.where(near >= 0, (near >> 1) * COLS + COLS - 2 + (near & 1), -1)
            place = jnp.broadcast_to(place, (MEMBERS, COLS))
            for r in range(DROWS):
                near_ref[at, r * COLS : (r + 1) * COLS] = jnp.where(lane + r * COLS == place, 1.0, 0.0).astype(BF16)
    for r in range(ROWS + 1):
        keep_ref[r] = 1.0 - jnp.broadcast_to(jnp.sum(listed[r], axis=0, keepdims=True), (8, COLS))


def split(x):
    high = x.astype(BF16)
    return high, (x - high.astype(F32)).astype(BF16)


def weights(request_ref, rows_ref, far_ref, near_ref):
    rows_ref[...] = request_ref[:, 0, :]
    request = rows_ref[...]
    whole = request.astype(jnp.int32)
    lane = iota((MEMBERS, COLS), 1)

    def wide(x, f, s):
        at = f * CAP + s
        return jnp.broadcast_to(x[:, at : at + 1], (MEMBERS, COLS))

    for s in range(CAP):
        at = slice(s * MEMBERS, (s + 1) * MEMBERS)
        col = wide(whole, R_COL, s)
        fx = wide(request, R_FX, s) * (1.0 / 16.0)
        fy = wide(request, R_FY, s) * (1.0 / 16.0)
        grid = wide(request, R_GRID, s)
        on_deck = jnp.where(grid == 2.0, 1.0, 0.0)
        first, second = on_deck * (1.0 - fx), on_deck * fx
        share = [first * (1.0 - fy), first * fy, second * (1.0 - fy), second * fy]
        for t in range(DCOLS // COLS):
            low, high = lane + t * COLS == col, lane + t * COLS == col + 1
            for r in range(DROWS):
                here = jnp.where(low, share[2 * r], jnp.where(high, share[2 * r + 1], 0.0))
                start = r * DCOLS + t * COLS
                far_ref[at, start : start + COLS] = here.astype(BF16)
        if s < NEAR:
            row = wide(whole, R_ROW, s)
            on_back = jnp.where(grid == 1.0, 1.0, 0.0)
            across = jnp.where(lane == col, on_back * (1.0 - fy), jnp.where(lane == col + 1, on_back * fy, 0.0))
            first, second = (1.0 - fx) * across, fx * across
            for r in range(ROWS):
                here = jnp.where(row == r, first, jnp.where(row + 1 == r, second, 0.0))
                near_ref[at, r * COLS : (r + 1) * COLS] = here.astype(BF16)


def stack_deck(pieces, r, value):
    high, low = split(value)
    pieces[0:PLANES, r * DCOLS : (r + 1) * DCOLS] = high
    pieces[128 : 128 + PLANES, r * DCOLS : (r + 1) * DCOLS] = low


def stack_back(pieces, r, value):
    high, low = split(value)
    pieces[0:PLANES, r * COLS : (r + 1) * COLS] = high
    pieces[128 : 128 + PLANES, r * COLS : (r + 1) * COLS] = low


def clear_pieces(deck_pieces, back_pieces):
    for pieces in (deck_pieces, back_pieces):
        gap = jnp.zeros((128 - PLANES, pieces.shape[1]), BF16)
        pieces[PLANES:128, :] = gap
        pieces[128 + PLANES : 256, :] = gap


def answer(far_ref, near_ref, deck_pieces, back_pieces, out_ref):
    lane = iota((MEMBERS, 128), 1)
    for q in range(CAP // 4):
        got = dot(far_ref[q * 256 : (q + 1) * 256, :], deck_pieces[...], NT)
        if q == 0:
            got = got + dot(near_ref[...], back_pieces[...], NT)
        got = got[:, 0:128] + got[:, 128:256]
        a = [got[i * MEMBERS : (i + 1) * MEMBERS, :] for i in range(4)]
        base = q * 4 * PLANES
        out_ref[:, 0, base : base + 128] = jnp.where(lane < 96, a[0], pltpu.roll(a[1], 96, 1))
        out_ref[:, 0, base + 128 : base + 256] = jnp.where(
            lane < 64, pltpu.roll(a[1], 96, 1), pltpu.roll(a[2], 64, 1)
        )
        out_ref[:, 0, base + 256 : base + 384] = jnp.where(
            lane < 32, pltpu.roll(a[2], 64, 1), pltpu.roll(a[3], 32, 1)
        )


def first_answer_kernel(
    request_ref, deck_hbm, back_hbm, deck_out, back_out, far_ref, near_ref, out_ref,
    rows_ref, deck_pieces, back_pieces, deck_ref, back_ref, sems,
):
    copies = [
        pltpu.make_async_copy(deck_hbm, deck_ref, sems.at[0]),
        pltpu.make_async_copy(back_hbm, back_ref, sems.at[1]),
    ]
    for c in copies:
        c.start()
    clear_pieces(deck_pieces, back_pieces)
    weights(request_ref, rows_ref, far_ref, near_ref)
    for c in copies:
        c.wait()
    for r in range(DROWS):
        value = deck_ref[:, r, :]
        deck_out[r] = value
        stack_deck(deck_pieces, r, value)
    for r in range(ROWS):
        value = back_ref[:, r, :]
        back_out[r] = value
        stack_back(back_pieces, r, value)
    answer(far_ref, near_ref, deck_pieces, back_pieces, out_ref)


def rim_kernel(
    got_ref, rim_ref, near_ref, keep_ref, deck_ref, back_ref,
    got_pieces, deck_out, column_first, column_second, row_first, row_second,
):
    lane = iota((MEMBERS, 128), 1)
    for q in range(CAP // 4):
        base = q * 4 * PLANES
        c0 = got_ref[:, 0, base : base + 128]
        c1 = got_ref[:, 0, base + 128 : base + 256]
        c2 = got_ref[:, 0, base + 256 : base + 384]
        a0 = jnp.where(lane < 96, c0, 0.0)
        a1 = jnp.where(lane < 32, pltpu.roll(c0, 32, 1), jnp.where(lane < 96, pltpu.roll(c1, 32, 1), 0.0))
        a2 = jnp.where(lane < 64, pltpu.roll(c1, 64, 1), jnp.where(lane < 96, pltpu.roll(c2, 64, 1), 0.0))
        a3 = jnp.where(lane < 96, pltpu.roll(c2, 96, 1), 0.0)
        across = jnp.concatenate([a0, a1, a2, a3], axis=0).T
        high, low = split(across[0:PLANES, :])
        got_pieces[0:PLANES, q * 256 : (q + 1) * 256] = high
        got_pieces[PLANES : 2 * PLANES, q * 256 : (q + 1) * 256] = low
    near = dot(got_pieces[:, 0:256], near_ref[...], NN)
    near = near[0:PLANES] + near[PLANES : 2 * PLANES]
    lane = iota((PLANES, 128), 1)
    column, line, tile = position()
    odd = lax.rem(tile, 2) > 0
    odd_line = lax.rem(line, 2) > 0
    deck = []
    for r in range(DROWS):
        outer = jnp.where(lane >= 126, near[:, r * 128 : (r + 1) * 128], deck_ref[r, :, 256:384])
        deck.append(jnp.concatenate([deck_ref[r, :, 0:256], outer], axis=1))
        deck_out[r] = deck[r]
    row_first[:, 0:DCOLS] = jnp.where(odd, deck[0], deck[1])
    row_second[:, 0:DCOLS] = jnp.where(odd, deck[1], deck[0])
    rim = dot(got_pieces[...], rim_ref[...], NN)
    rim = rim[0:PLANES] + rim[PLANES : 2 * PLANES]
    north = back_ref[0] * keep_ref[0, 0:1, :] + rim[:, 0:COLS]
    south = back_ref[ROWS - 1] * keep_ref[ROWS - 1, 0:1, :] + rim[:, COLS : 2 * COLS]
    column_first[...] = jnp.where(odd_line, north, south)
    column_second[...] = jnp.where(odd_line, south, north)
    ends = jnp.zeros((PLANES, COLS), F32)
    for r in range(ROWS):
        ends = jnp.where(lane == r, back_ref[r, :, 0:1], ends)
        ends = jnp.where(lane == ROWS + r, back_ref[r, :, COLS - 1 : COLS], ends)
    ends = ends * keep_ref[ROWS, 0:1, :] + rim[:, 2 * COLS : 3 * COLS]
    row_first[:, DCOLS : DCOLS + COLS] = ends
    row_second[:, DCOLS : DCOLS + COLS] = ends


def fill_kernel(got_pieces, fill_ref, keep_ref, back_ref, back_out):
    for c in range(ROWS // 2):
        new = dot(got_pieces[...], fill_ref[:, c * 256 : (c + 1) * 256], NN)
        new = new[0:PLANES] + new[PLANES : 2 * PLANES]
        for half in range(2):
            r = 2 * c + half
            back_out[r] = back_ref[r] * keep_ref[r, 0:1, :] + new[:, half * 128 : (half + 1) * 128]


def update(here, minus_xi, plus_xi, minus_eta, plus_eta, metric, keep, base, section):
    d_xi, d_eta, d_span, lap = [], [], [], []
    strain = None
    for c in range(3):
        f = here[c]
        plus_span = jnp.concatenate([f[1:], f[:1]], axis=0)
        minus_span = jnp.concatenate([f[-1:], f[:-1]], axis=0)
        a = plus_xi[c] - minus_xi[c]
        b = plus_eta[c] - minus_eta[c]
        s = plus_span - minus_span
        square = a * a + b * b + s * s
        strain = square if strain is None else strain + square
        doubled = 2.0 * f
        l_xi = plus_xi[c] - doubled + minus_xi[c]
        l_eta = plus_eta[c] - doubled + minus_eta[c]
        if metric is not None:
            l_xi, l_eta = metric[4] * l_xi, metric[5] * l_eta
        lap.append(l_xi + l_eta + (plus_span - doubled + minus_span))
        d_xi.append(a)
        d_eta.append(b)
        d_span.append(s)
    viscosity = SMAGORINSKY * jnp.sqrt(1.0 + 0.25 * strain)
    if metric is None:
        speed_xi, speed_eta = here[0], here[1]
    else:
        speed_xi = metric[0] * here[0] + metric[1] * here[1]
        speed_eta = metric[2] * here[0] + metric[3] * here[1]
    out = []
    for c in range(3):
        advection = 0.5 * (speed_xi * d_xi[c] + speed_eta * d_eta[c] + here[2] * d_span[c])
        tendency = viscosity * lap[c] - advection
        if section == 0:
            out.append(here[c] + (TIME_STEP * keep) * tendency)
        elif section == 1:
            out.append(0.75 * base[c] + 0.25 * here[c] + (0.25 * TIME_STEP * keep) * tendency)
        else:
            out.append(base[c] * (1.0 / 3.0) + (2.0 / 3.0) * here[c] + (2.0 / 3.0 * TIME_STEP * keep) * tendency)
    return out


def fields(ref, at):
    return [ref[at + (slice(c * SPAN, (c + 1) * SPAN), slice(None))] for c in range(3)]


def section_kernel(section, *refs):
    refs = list(refs)
    deck_ref, back_ref, column_first, column_second, row_first, row_second, metric_ref, keep_ref = refs[:8]
    del refs[:8]
    base_deck = base_back = None
    if section > 0:
        base_deck, base_back = refs[:2]
        del refs[:2]
    last = section == 2
    if last:
        deck_out, back_out = refs
    else:
        far_ref, near_ref, deck_out, back_out, answer_out, deck_pieces, back_pieces = refs
        clear_pieces(deck_pieces, back_pieces)
    column, line, tile = position()
    odd = lax.rem(tile, 2) > 0
    odd_line = lax.rem(line, 2) > 0
    west_end = (column > 0).astype(F32)
    east_end = (column < lax.axis_size("gy") - 1).astype(F32)

    def ordered(flag, first, second, at):
        a, b = first[at], second[at]
        return jnp.where(flag, a, b), jnp.where(flag, b, a)

    spans = [slice(c * SPAN, (c + 1) * SPAN) for c in range(3)]
    across = [ordered(odd, row_first, row_second, (at, slice(0, DCOLS))) for at in spans]
    beside = [ordered(odd, row_first, row_second, (at, slice(DCOLS, DCOLS + COLS))) for at in spans]
    along = [ordered(odd_line, column_first, column_second, (at, slice(None))) for at in spans]
    lane = iota((SPAN, DCOLS), 1)
    keep_deck = jnp.where(iota((1, DCOLS), 1) < DCOLS - 2, 1.0, 0.0)
    for r in range(DROWS):
        here = fields(deck_ref, (r,))
        if r == 0:
            minus = [a[0] for a in across]
            plus = fields(deck_ref, (1,))
        else:
            minus = fields(deck_ref, (0,))
            plus = [a[1] for a in across]
        m = [metric_ref[i, r : r + 1, :] for i in range(4)]
        metric = m + [m[0] * m[0] + m[1] * m[1], m[2] * m[2] + m[3] * m[3]]
        plus_eta = [jnp.where(lane == DCOLS - 1, 0.0, pltpu.roll(f, DCOLS - 1, 1)) for f in here]
        minus_eta = [jnp.where(lane == 0, 0.0, pltpu.roll(f, 1, 1)) for f in here]
        base = fields(base_deck, (r,)) if section > 0 else None
        new = update(here, minus, plus, minus_eta, plus_eta, metric, keep_deck, base, section)
        for c in range(3):
            if last:
                deck_out[c * SPAN : (c + 1) * SPAN, r, :] = new[c]
            else:
                deck_out[r, c * SPAN : (c + 1) * SPAN, :] = new[c]
        if not last:
            stack_deck(deck_pieces, r, jnp.concatenate(new, axis=0))
    lane = iota((SPAN, COLS), 1)
    for r in range(ROWS):
        here = fields(back_ref, (r,))
        minus = fields(back_ref, (r - 1,)) if r > 0 else [a[0] for a in along]
        plus = fields(back_ref, (r + 1,)) if r < ROWS - 1 else [a[1] for a in along]
        plus_eta, minus_eta = [], []
        for c in range(3):
            from_west = beside[c][0][:, ROWS + r : ROWS + r + 1] * west_end
            from_east = beside[c][1][:, r : r + 1] * east_end
            plus_eta.append(jnp.where(lane == COLS - 1, from_east, pltpu.roll(here[c], COLS - 1, 1)))
            minus_eta.append(jnp.where(lane == 0, from_west, pltpu.roll(here[c], 1, 1)))
        base = fields(base_back, (r,)) if section > 0 else None
        new = update(here, minus, plus, minus_eta, plus_eta, None, keep_ref[r, 0:1, :], base, section)
        for c in range(3):
            if last:
                back_out[c * SPAN : (c + 1) * SPAN, r, :] = new[c]
            else:
                back_out[r, c * SPAN : (c + 1) * SPAN, :] = new[c]
        if not last:
            stack_back(back_pieces, r, jnp.concatenate(new, axis=0))
    if not last:
        answer(far_ref, near_ref, deck_pieces, back_pieces, answer_out)


def local(deck_fields, back_fields, metrics, donors, stencil, fringe_cells):
    group = ("gx", "gy")
    everyone = ("grid", "gx", "gy")

    def exchange(x):
        return lax.all_to_all(x, group, split_axis=0, concat_axis=0, tiled=True)

    count = lax.axis_size("grid") * lax.axis_size("gx") * lax.axis_size("gy")
    across_y = lax.axis_size("gy")

    def pairs(step, first):
        out = []
        for t in range(count):
            if (t // step) % 2 == first:
                other = t + step
                if other >= count and step > 1:
                    continue
                out += [(t, other % count), (other % count, t)]
        return out

    deck_in = deck_fields.reshape(PLANES, DROWS, DCOLS)
    back_in = back_fields.reshape(PLANES, ROWS, COLS)
    request, fill_map, rim_map, near_map, keep = call(
        route_kernel,
        [
            ((MEMBERS, 1, 128), F32),
            ((SLOTS, ROWS * COLS), BF16),
            ((SLOTS, 3 * COLS), BF16),
            ((NEAR * MEMBERS, 2 * COLS), BF16),
            ((ROWS + 1, 8, COLS), F32),
        ],
        [donors.reshape(1, FRINGE), stencil.reshape(FRINGE, 4).T, fringe_cells],
        scratch=[
            pltpu.VMEM((1, FRINGE), jnp.int32),
            pltpu.VMEM((4, FRINGE), jnp.int32),
            pltpu.VMEM((1, FRINGE - NEAR), jnp.int32),
            pltpu.VMEM((MEMBERS, 3 * CAP), F32),
            pltpu.SemaphoreType.DMA((3,)),
        ],
        hbm_at=(0, 1, 2),
        name="route",
    )
    request = exchange(request)
    pieces = [pltpu.VMEM((256, DROWS * DCOLS), BF16), pltpu.VMEM((256, ROWS * COLS), BF16)]
    deck, back_state, far, near, answers = call(
        first_answer_kernel,
        [
            ((DROWS, PLANES, DCOLS), F32),
            ((ROWS, PLANES, COLS), F32),
            ((SLOTS, DROWS * DCOLS), BF16),
            ((NEAR * MEMBERS, ROWS * COLS), BF16),
            ((MEMBERS, 1, PACKED), F32),
        ],
        [request, deck_in, back_in],
        scratch=[pltpu.VMEM((MEMBERS, 128), F32)]
        + pieces
        + [
            pltpu.VMEM((PLANES, DROWS, DCOLS), F32),
            pltpu.VMEM((PLANES, ROWS, COLS), F32),
            pltpu.SemaphoreType.DMA((2,)),
        ],
        hbm_at=(1, 2),
        name="first_answer",
    )
    base = None
    for section in range(3):
        got = exchange(answers)
        got_pieces, deck, column_first, column_second, row_first, row_second = call(
            rim_kernel,
            [
                ((2 * PLANES, SLOTS), BF16),
                ((DROWS, PLANES, DCOLS), F32),
                ((PLANES, COLS), F32),
                ((PLANES, COLS), F32),
                ((PLANES, DCOLS + COLS), F32),
                ((PLANES, DCOLS + COLS), F32),
            ],
            [got, rim_map, near_map, keep, deck, back_state],
            name="rim",
        )
        row_first = lax.ppermute(row_first, everyone, pairs(1, 0))
        row_second = lax.ppermute(row_second, everyone, pairs(1, 1))
        column_first = lax.ppermute(column_first, everyone, pairs(across_y, 0))
        column_second = lax.ppermute(column_second, everyone, pairs(across_y, 1))
        (back_state,) = call(
            fill_kernel,
            [((ROWS, PLANES, COLS), F32)],
            [got_pieces, fill_map, keep, back_state],
            name="fill",
        )
        if section == 0:
            base = [deck, back_state]
        ins = [deck, back_state, column_first, column_second, row_first, row_second, metrics, keep]
        if section > 0:
            ins += base
        kernel = functools.partial(section_kernel, section)
        if section < 2:
            deck, back_state, answers = call(
                kernel,
                [
                    ((DROWS, PLANES, DCOLS), F32),
                    ((ROWS, PLANES, COLS), F32),
                    ((MEMBERS, 1, PACKED), F32),
                ],
                ins + [far, near],
                scratch=pieces,
                name="section",
            )
        else:
            deck, back_state = call(
                kernel,
                [((PLANES, DROWS, DCOLS), F32), ((PLANES, ROWS, COLS), F32)],
                ins,
                name="section",
            )
    return deck.reshape(deck_fields.shape), back_state.reshape(back_fields.shape)


def solution(mesh):
    return jax.shard_map(
        local,
        mesh=mesh,
        in_specs=(
            P(None, None, ("grid", "gx", "gy"), None),
            P(None, None, ("grid", "gx"), "gy"),
            P(None, ("grid", "gx", "gy"), None),
            P(("grid", "gx", "gy"), None, None),
            P(("grid", "gx", "gy"), None, None),
            P(("grid", "gx", "gy"), None),
        ),
        out_specs=(P(None, None, ("grid", "gx", "gy"), None), P(None, None, ("grid", "gx"), "gy")),
        check_vma=False,
    )
```

```python
import functools

import jax
import jax.numpy as jnp
from jax import lax
from jax.experimental import pallas as pl
from jax.experimental.pallas import tpu as pltpu
from jax.sharding import PartitionSpec as P

SPAN = 32
PLANES = 96
MEMBERS = 64
CAP = 16
SLOTS = MEMBERS * CAP
ROWS = 16
COLS = 128
DROWS = 2
DCOLS = 384
FRINGE = 512
NEAR = 4
TIME_STEP = 0.05
SMAGORINSKY = 0.02
F32 = jnp.float32
BF16 = jnp.bfloat16
NT = (((1,), (1,)), ((), ()))
NN = (((1,), (0,)), ((), ()))
VMEM_LIMIT = 24 * 1024 * 1024
PACKED = CAP * PLANES
R_ROW, R_COL, R_FX, R_FY, R_GRID = range(5)


def position():
    column = lax.axis_index("gy")
    line = lax.axis_index("grid") * lax.axis_size("gx") + lax.axis_index("gx")
    tile = line * lax.axis_size("gy") + column
    return column, line, tile


def dot(a, b, dims):
    return lax.dot_general(a, b, dims, preferred_element_type=F32)


def iota(shape, dim):
    return lax.broadcasted_iota(jnp.int32, shape, dim)


def call(kernel, outs, ins, scratch=(), hbm_at=(), name=None):
    def spec(i):
        return pl.BlockSpec(memory_space=pltpu.HBM if i in hbm_at else pltpu.VMEM)

    ins = [pltpu.with_memory_space_constraint(x, pltpu.HBM) if i in hbm_at else x for i, x in enumerate(ins)]
    return pl.pallas_call(
        kernel,
        out_shape=tuple(jax.ShapeDtypeStruct(s, d) for s, d in outs),
        in_specs=[spec(i) for i in range(len(ins))],
        out_specs=tuple(pl.BlockSpec(memory_space=pltpu.VMEM) for _ in outs),
        scratch_shapes=list(scratch),
        compiler_params=pltpu.CompilerParams(vmem_limit_bytes=VMEM_LIMIT),
        name=name,
    )(*ins)


def route_kernel(
    donors_hbm, stencil_hbm, cells_hbm, request_ref, local_ref, rim_ref, near_ref, keep_ref,
    donors_ref, stencil_ref, cells_ref, sems,
):
    pairs = [(donors_hbm, donors_ref), (stencil_hbm, stencil_ref), (cells_hbm, cells_ref)]
    copies = [pltpu.make_async_copy(a, b, sems.at[i]) for i, (a, b) in enumerate(pairs)]
    for c in copies:
        c.start()
    for c in copies:
        c.wait()
    donors = donors_ref[...]
    member = (iota((MEMBERS, FRINGE), 0) == donors).astype(F32)
    before = (iota((FRINGE, FRINGE), 0) < iota((FRINGE, FRINGE), 1)).astype(BF16)
    member_b = member.astype(BF16)
    earlier = dot(member_b, before, NN)
    rank = jnp.sum(member * earlier, axis=0, keepdims=True).astype(jnp.int32)
    at_rank = (iota((CAP, FRINGE), 0) == rank).astype(F32)

    def place(values):
        stacked = jnp.concatenate([at_rank * v.astype(F32) for v in values], axis=0)
        return dot(member_b, stacked.astype(BF16), NT)

    row = stencil_ref[0:1, :]
    col = stencil_ref[1:2, :]
    lane = iota((1, FRINGE), 1)
    grid = jnp.where(lane < NEAR, 1, 2)
    half = col >> 1
    sent = place([row, half, col - 2 * half, stencil_ref[2:3, :], stencil_ref[3:4, :], grid])
    request_ref[:, 0, :] = jnp.zeros((MEMBERS, 128), F32)
    request_ref[:, 0, 0:16] = sent[:, 0:16]
    request_ref[:, 0, 16:32] = 2.0 * sent[:, 16:32] + sent[:, 32:48]
    request_ref[:, 0, 32:80] = sent[:, 48:96]
    cells = jnp.concatenate([jnp.zeros((1, NEAR), jnp.int32), cells_ref[...]], axis=1)
    far = lane >= NEAR
    local_ref[...] = place(
        [
            jnp.where(far, (cells >> 7) + 1, 0),
            jnp.where(far, cells & 127, 0),
            jnp.where(far, 0, lane + 1),
        ]
    )
    landing(local_ref, rim_ref, near_ref, keep_ref)


def over_eight(x):
    return jnp.sum(x.reshape(MEMBERS // 8, 8, COLS), axis=0)


def kept(listed):
    return 1.0 - jnp.broadcast_to(jnp.sum(listed, axis=0, keepdims=True), (8, COLS))


def landing(local_ref, rim_ref, near_ref, keep_ref):
    lane = iota((MEMBERS, COLS), 1)
    places = local_ref[...].astype(jnp.int32)
    listed = [jnp.zeros((8, COLS), F32) for _ in range(3)]

    for s in range(CAP):
        at = slice(s * MEMBERS, (s + 1) * MEMBERS)
        row = jnp.broadcast_to(places[:, s : s + 1] - 1, (MEMBERS, COLS))
        col = jnp.broadcast_to(places[:, CAP + s : CAP + s + 1], (MEMBERS, COLS))
        hit = jnp.where(lane == col, 1.0, 0.0)
        for i, r in enumerate((0, ROWS - 1)):
            here = jnp.where(row == r, hit, 0.0)
            rim_ref[at, i * COLS : (i + 1) * COLS] = here.astype(BF16)
            listed[i] = listed[i] + over_eight(here)
        side = jnp.where(col == 0, row, jnp.where(col == COLS - 1, row + ROWS, -1))
        here = jnp.where((lane == side) & (row >= 0), 1.0, 0.0)
        rim_ref[at, 2 * COLS : 3 * COLS] = here.astype(BF16)
        listed[2] = listed[2] + over_eight(here)
        if s < NEAR:
            near = places[:, 2 * CAP + s : 2 * CAP + s + 1] - 1
            place = jnp.where(near >= 0, (near >> 1) * COLS + COLS - 2 + (near & 1), -1)
            place = jnp.broadcast_to(place, (MEMBERS, COLS))
            for r in range(DROWS):
                near_ref[at, r * COLS : (r + 1) * COLS] = jnp.where(lane + r * COLS == place, 1.0, 0.0).astype(BF16)
    for i in range(3):
        keep_ref[i] = kept(listed[i])


def split(x):
    high = x.astype(BF16)
    return high, (x - high.astype(F32)).astype(BF16)


def weights(request_ref, rows_ref, far_ref, near_ref):
    rows_ref[...] = request_ref[:, 0, :]
    request = rows_ref[...]
    whole = request.astype(jnp.int32)
    lane = iota((MEMBERS, COLS), 1)

    def wide(x, f, s):
        at = f * CAP + s
        return jnp.broadcast_to(x[:, at : at + 1], (MEMBERS, COLS))

    for s in range(CAP):
        at = slice(s * MEMBERS, (s + 1) * MEMBERS)
        col = wide(whole, R_COL, s)
        fx = wide(request, R_FX, s) * (1.0 / 16.0)
        fy = wide(request, R_FY, s) * (1.0 / 16.0)
        grid = wide(request, R_GRID, s)
        on_deck = jnp.where(grid == 2.0, 1.0, 0.0)
        first, second = on_deck * (1.0 - fx), on_deck * fx
        share = [first * (1.0 - fy), first * fy, second * (1.0 - fy), second * fy]
        for t in range(DCOLS // COLS):
            low, high = lane + t * COLS == col, lane + t * COLS == col + 1
            for r in range(DROWS):
                here = jnp.where(low, share[2 * r], jnp.where(high, share[2 * r + 1], 0.0))
                start = r * DCOLS + t * COLS
                far_ref[at, start : start + COLS] = here.astype(BF16)
        if s < NEAR:
            row = wide(whole, R_ROW, s)
            on_back = jnp.where(grid == 1.0, 1.0, 0.0)
            across = jnp.where(lane == col, on_back * (1.0 - fy), jnp.where(lane == col + 1, on_back * fy, 0.0))
            first, second = (1.0 - fx) * across, fx * across
            for r in range(ROWS):
                here = jnp.where(row == r, first, jnp.where(row + 1 == r, second, 0.0))
                near_ref[at, r * COLS : (r + 1) * COLS] = here.astype(BF16)


def stack_deck(pieces, r, value):
    high, low = split(value)
    pieces[0:PLANES, r * DCOLS : (r + 1) * DCOLS] = high
    pieces[128 : 128 + PLANES, r * DCOLS : (r + 1) * DCOLS] = low


def stack_back(pieces, r, value):
    high, low = split(value)
    pieces[0:PLANES, r * COLS : (r + 1) * COLS] = high
    pieces[128 : 128 + PLANES, r * COLS : (r + 1) * COLS] = low


def clear_pieces(deck_pieces, back_pieces):
    for pieces in (deck_pieces, back_pieces):
        gap = jnp.zeros((128 - PLANES, pieces.shape[1]), BF16)
        pieces[PLANES:128, :] = gap
        pieces[128 + PLANES : 256, :] = gap


def answer(far_ref, near_ref, deck_pieces, back_pieces, out_ref):
    lane = iota((MEMBERS, 128), 1)
    for q in range(CAP // 4):
        got = dot(far_ref[q * 256 : (q + 1) * 256, :], deck_pieces[...], NT)
        if q == 0:
            got = got + dot(near_ref[...], back_pieces[...], NT)
        got = got[:, 0:128] + got[:, 128:256]
        a = [got[i * MEMBERS : (i + 1) * MEMBERS, :] for i in range(4)]
        base = q * 4 * PLANES
        out_ref[:, 0, base : base + 128] = jnp.where(lane < 96, a[0], pltpu.roll(a[1], 96, 1))
        out_ref[:, 0, base + 128 : base + 256] = jnp.where(
            lane < 64, pltpu.roll(a[1], 96, 1), pltpu.roll(a[2], 64, 1)
        )
        out_ref[:, 0, base + 256 : base + 384] = jnp.where(
            lane < 32, pltpu.roll(a[2], 64, 1), pltpu.roll(a[3], 32, 1)
        )


def first_answer_kernel(
    request_ref, deck_hbm, back_hbm, deck_out, back_out, far_ref, near_ref, out_ref,
    rows_ref, deck_pieces, back_pieces, deck_ref, back_ref, sems,
):
    copies = [
        pltpu.make_async_copy(deck_hbm, deck_ref, sems.at[0]),
        pltpu.make_async_copy(back_hbm, back_ref, sems.at[1]),
    ]
    for c in copies:
        c.start()
    clear_pieces(deck_pieces, back_pieces)
    weights(request_ref, rows_ref, far_ref, near_ref)
    for c in copies:
        c.wait()
    for r in range(DROWS):
        value = deck_ref[:, r, :]
        deck_out[r] = value
        stack_deck(deck_pieces, r, value)
    for r in range(ROWS):
        value = back_ref[:, r, :]
        back_out[r] = value
        stack_back(back_pieces, r, value)
    answer(far_ref, near_ref, deck_pieces, back_pieces, out_ref)


def rim_kernel(
    got_ref, rim_ref, near_ref, keep_ref, deck_ref, back_ref,
    got_pieces, deck_out, column_first, column_second, row_first, row_second,
):
    lane = iota((MEMBERS, 128), 1)
    for q in range(CAP // 4):
        base = q * 4 * PLANES
        c0 = got_ref[:, 0, base : base + 128]
        c1 = got_ref[:, 0, base + 128 : base + 256]
        c2 = got_ref[:, 0, base + 256 : base + 384]
        a0 = jnp.where(lane < 96, c0, 0.0)
        a1 = jnp.where(lane < 32, pltpu.roll(c0, 32, 1), jnp.where(lane < 96, pltpu.roll(c1, 32, 1), 0.0))
        a2 = jnp.where(lane < 64, pltpu.roll(c1, 64, 1), jnp.where(lane < 96, pltpu.roll(c2, 64, 1), 0.0))
        a3 = jnp.where(lane < 96, pltpu.roll(c2, 96, 1), 0.0)
        across = jnp.concatenate([a0, a1, a2, a3], axis=0).T
        high, low = split(across[0:PLANES, :])
        got_pieces[0:PLANES, q * 256 : (q + 1) * 256] = high
        got_pieces[PLANES : 2 * PLANES, q * 256 : (q + 1) * 256] = low
    near = dot(got_pieces[:, 0:256], near_ref[...], NN)
    near = near[0:PLANES] + near[PLANES : 2 * PLANES]
    lane = iota((PLANES, 128), 1)
    column, line, tile = position()
    odd = lax.rem(tile, 2) > 0
    odd_line = lax.rem(line, 2) > 0
    deck = []
    for r in range(DROWS):
        outer = jnp.where(lane >= 126, near[:, r * 128 : (r + 1) * 128], deck_ref[r, :, 256:384])
        deck.append(jnp.concatenate([deck_ref[r, :, 0:256], outer], axis=1))
        deck_out[r] = deck[r]
    row_first[0:PLANES, :] = jnp.where(odd, deck[0], deck[1])
    row_second[0:PLANES, :] = jnp.where(odd, deck[1], deck[0])
    rim = dot(got_pieces[...], rim_ref[...], NN)
    rim = rim[0:PLANES] + rim[PLANES : 2 * PLANES]
    north = back_ref[0] * keep_ref[0, 0:1, :] + rim[:, 0:COLS]
    south = back_ref[ROWS - 1] * keep_ref[1, 0:1, :] + rim[:, COLS : 2 * COLS]
    column_first[...] = jnp.where(odd_line, north, south)
    column_second[...] = jnp.where(odd_line, south, north)
    ends = jnp.zeros((PLANES, COLS), F32)
    for r in range(ROWS):
        ends = jnp.where(lane == r, back_ref[r, :, 0:1], ends)
        ends = jnp.where(lane == ROWS + r, back_ref[r, :, COLS - 1 : COLS], ends)
    ends = ends * keep_ref[2, 0:1, :] + rim[:, 2 * COLS : 3 * COLS]
    ends = jnp.concatenate([ends, jnp.zeros((COLS - PLANES, COLS), F32)], axis=0).T
    parts = [ends[i * 8 : (i + 1) * 8, :] for i in range(4)]
    for side, flag in ((row_first, odd), (row_second, jnp.logical_not(odd))):
        for i in range(2):
            side[PLANES : PLANES + 8, i * COLS : (i + 1) * COLS] = jnp.where(flag, parts[i], parts[2 + i])
        side[PLANES : PLANES + 8, 2 * COLS : 3 * COLS] = jnp.zeros((8, COLS), F32)


def fill_kernel(got_pieces, fill_ref, keep_ref, back_ref, back_out):
    for c in range(ROWS // 2):
        new = dot(got_pieces[...], fill_ref[:, c * 256 : (c + 1) * 256], NN)
        new = new[0:PLANES] + new[PLANES : 2 * PLANES]
        for half in range(2):
            r = 2 * c + half
            back_out[r] = back_ref[r] * keep_ref[r, 0:1, :] + new[:, half * 128 : (half + 1) * 128]


def first_fill_kernel(got_pieces, local_ref, back_ref, back_out, fill_ref, keep_ref):
    lane = iota((MEMBERS, COLS), 1)
    places = local_ref[...].astype(jnp.int32)
    listed = [jnp.zeros((8, COLS), F32) for _ in range(ROWS)]
    for s in range(CAP):
        at = slice(s * MEMBERS, (s + 1) * MEMBERS)
        row = jnp.broadcast_to(places[:, s : s + 1] - 1, (MEMBERS, COLS))
        col = jnp.broadcast_to(places[:, CAP + s : CAP + s + 1], (MEMBERS, COLS))
        hit = jnp.where(lane == col, 1.0, 0.0)
        for r in range(ROWS):
            here = jnp.where(row == r, hit, 0.0)
            fill_ref[at, r * COLS : (r + 1) * COLS] = here.astype(BF16)
            listed[r] = listed[r] + over_eight(here)
    for r in range(ROWS):
        keep_ref[r] = kept(listed[r])
    fill_kernel(got_pieces, fill_ref, keep_ref, back_ref, back_out)


def update(here, minus_xi, plus_xi, minus_eta, plus_eta, metric, keep, base, section):
    weight = (1.0, 0.25, 2.0 / 3.0)[section]
    step = (weight * TIME_STEP) * keep
    d_xi, d_eta, d_span, lap = [], [], [], []
    strain = None
    for c in range(3):
        f = here[c]
        plus_span = pltpu.roll(f, SPAN - 1, 0)
        minus_span = pltpu.roll(f, 1, 0)
        a = plus_xi[c] - minus_xi[c]
        b = plus_eta[c] - minus_eta[c]
        s = plus_span - minus_span
        square = a * a + b * b + s * s
        strain = square if strain is None else strain + square
        if metric is None:
            around = (plus_xi[c] + minus_xi[c]) + (plus_eta[c] + minus_eta[c]) + (plus_span + minus_span)
            lap.append(around - 6.0 * f)
        else:
            doubled = 2.0 * f
            l_xi = plus_xi[c] - doubled + minus_xi[c]
            l_eta = plus_eta[c] - doubled + minus_eta[c]
            lap.append(metric[4] * l_xi + metric[5] * l_eta + (plus_span - doubled + minus_span))
        d_xi.append(a)
        d_eta.append(b)
        d_span.append(s)
    viscosity = (SMAGORINSKY * step) * jnp.sqrt(1.0 + 0.25 * strain)
    half = 0.5 * step
    if metric is None:
        speed_xi, speed_eta = half * here[0], half * here[1]
    else:
        speed_xi = half * (metric[0] * here[0] + metric[1] * here[1])
        speed_eta = half * (metric[2] * here[0] + metric[3] * here[1])
    speed_span = half * here[2]
    out = []
    for c in range(3):
        change = viscosity * lap[c] - (speed_xi * d_xi[c] + speed_eta * d_eta[c] + speed_span * d_span[c])
        if section == 0:
            out.append(here[c] + change)
        elif section == 1:
            out.append(0.75 * base[c] + (0.25 * here[c] + change))
        else:
            out.append(base[c] * (1.0 / 3.0) + ((2.0 / 3.0) * here[c] + change))
    return out


def fields(ref, at):
    return [ref[at + (slice(c * SPAN, (c + 1) * SPAN), slice(None))] for c in range(3)]


def section_kernel(section, *refs):
    refs = list(refs)
    deck_ref, back_ref, column_first, column_second, row_first, row_second, metric_ref, keep_ref = refs[:8]
    del refs[:8]
    base_deck = base_back = None
    if section > 0:
        base_deck, base_back = refs[:2]
        del refs[:2]
    last = section == 2
    if last:
        deck_out, back_out = refs
    else:
        far_ref, near_ref, deck_out, back_out, answer_out, deck_pieces, back_pieces = refs
        clear_pieces(deck_pieces, back_pieces)
    column, line, tile = position()
    odd = lax.rem(tile, 2) > 0
    odd_line = lax.rem(line, 2) > 0
    west_end = (column > 0).astype(F32)
    east_end = (column < lax.axis_size("gy") - 1).astype(F32)

    def ordered(flag, first, second, at):
        a, b = first[at], second[at]
        return jnp.where(flag, a, b), jnp.where(flag, b, a)

    spans = [slice(c * SPAN, (c + 1) * SPAN) for c in range(3)]
    across = [ordered(odd, row_first, row_second, (at, slice(None))) for at in spans]
    beside = []
    halves = [
        ordered(odd, row_first, row_second, (slice(PLANES, PLANES + 8), slice(i * COLS, (i + 1) * COLS)))
        for i in range(2)
    ]
    for side in range(2):
        cells = jnp.concatenate([halves[0][side], halves[1][side], jnp.zeros((COLS - 16, COLS), F32)], axis=0)
        beside.append(cells.T)
    north_end = (line > 0).astype(F32)
    south_end = (line < lax.axis_size("grid") * lax.axis_size("gx") - 1).astype(F32)
    along = [ordered(odd_line, column_first, column_second, (at, slice(None))) for at in spans]
    along = [(before * north_end, after * south_end) for before, after in along]
    lane = iota((SPAN, DCOLS), 1)
    keep_deck = jnp.where(iota((1, DCOLS), 1) < DCOLS - 2, 1.0, 0.0)
    for r in range(DROWS):
        here = fields(deck_ref, (r,))
        if r == 0:
            minus = [a[0] for a in across]
            plus = fields(deck_ref, (1,))
        else:
            minus = fields(deck_ref, (0,))
            plus = [a[1] for a in across]
        m = [metric_ref[i, r : r + 1, :] for i in range(4)]
        metric = m + [m[0] * m[0] + m[1] * m[1], m[2] * m[2] + m[3] * m[3]]
        plus_eta = [jnp.where(lane == DCOLS - 1, 0.0, pltpu.roll(f, DCOLS - 1, 1)) for f in here]
        minus_eta = [jnp.where(lane == 0, 0.0, pltpu.roll(f, 1, 1)) for f in here]
        base = fields(base_deck, (r,)) if section > 0 else None
        new = update(here, minus, plus, minus_eta, plus_eta, metric, keep_deck, base, section)
        for c in range(3):
            if last:
                deck_out[c * SPAN : (c + 1) * SPAN, r, :] = new[c]
            else:
                deck_out[r, c * SPAN : (c + 1) * SPAN, :] = new[c]
        if not last:
            stack_deck(deck_pieces, r, jnp.concatenate(new, axis=0))
    lane = iota((SPAN, COLS), 1)
    for r in range(ROWS):
        here = fields(back_ref, (r,))
        minus = fields(back_ref, (r - 1,)) if r > 0 else [a[0] for a in along]
        plus = fields(back_ref, (r + 1,)) if r < ROWS - 1 else [a[1] for a in along]
        plus_eta, minus_eta = [], []
        for c in range(3):
            from_west = beside[0][spans[c], r : r + 1] * west_end
            from_east = beside[1][spans[c], r : r + 1] * east_end
            plus_eta.append(jnp.where(lane == COLS - 1, from_east, pltpu.roll(here[c], COLS - 1, 1)))
            minus_eta.append(jnp.where(lane == 0, from_west, pltpu.roll(here[c], 1, 1)))
        base = fields(base_back, (r,)) if section > 0 else None
        new = update(here, minus, plus, minus_eta, plus_eta, None, keep_ref[r, 0:1, :], base, section)
        for c in range(3):
            if last:
                back_out[c * SPAN : (c + 1) * SPAN, r, :] = new[c]
            else:
                back_out[r, c * SPAN : (c + 1) * SPAN, :] = new[c]
        if not last:
            stack_back(back_pieces, r, jnp.concatenate(new, axis=0))
    if not last:
        answer(far_ref, near_ref, deck_pieces, back_pieces, answer_out)


def local(deck_fields, back_fields, metrics, donors, stencil, fringe_cells):
    group = ("gx", "gy")
    everyone = ("grid", "gx", "gy")

    def exchange(x):
        return lax.all_to_all(x, group, split_axis=0, concat_axis=0, tiled=True)

    count = lax.axis_size("grid") * lax.axis_size("gx") * lax.axis_size("gy")
    across_y = lax.axis_size("gy")

    def pairs(step, first, periodic=False):
        out = []
        for t in range(count):
            if (t // step) % 2 == first:
                other = (t + step) % count
                if periodic or t + step < count:
                    out += [(t, other), (other, t)]
                else:
                    out += [(t, t ^ 1), (other, other ^ 1)]
        return out

    deck_in = deck_fields.reshape(PLANES, DROWS, DCOLS)
    back_in = back_fields.reshape(PLANES, ROWS, COLS)
    request, placing, rim_map, near_map, rim_keep = call(
        route_kernel,
        [
            ((MEMBERS, 1, 128), F32),
            ((MEMBERS, 3 * CAP), F32),
            ((SLOTS, 3 * COLS), BF16),
            ((NEAR * MEMBERS, 2 * COLS), BF16),
            ((3, 8, COLS), F32),
        ],
        [donors.reshape(1, FRINGE), stencil.reshape(FRINGE, 4).T, fringe_cells],
        scratch=[
            pltpu.VMEM((1, FRINGE), jnp.int32),
            pltpu.VMEM((4, FRINGE), jnp.int32),
            pltpu.VMEM((1, FRINGE - NEAR), jnp.int32),
            pltpu.SemaphoreType.DMA((3,)),
        ],
        hbm_at=(0, 1, 2),
        name="route",
    )
    request = exchange(request)
    pieces = [pltpu.VMEM((256, DROWS * DCOLS), BF16), pltpu.VMEM((256, ROWS * COLS), BF16)]
    deck, back_state, far, near, answers = call(
        first_answer_kernel,
        [
            ((DROWS, PLANES, DCOLS), F32),
            ((ROWS, PLANES, COLS), F32),
            ((SLOTS, DROWS * DCOLS), BF16),
            ((NEAR * MEMBERS, ROWS * COLS), BF16),
            ((MEMBERS, 1, PACKED), F32),
        ],
        [request, deck_in, back_in],
        scratch=[pltpu.VMEM((MEMBERS, 128), F32)]
        + pieces
        + [
            pltpu.VMEM((PLANES, DROWS, DCOLS), F32),
            pltpu.VMEM((PLANES, ROWS, COLS), F32),
            pltpu.SemaphoreType.DMA((2,)),
        ],
        hbm_at=(1, 2),
        name="first_answer",
    )
    base = None
    for section in range(3):
        got = exchange(answers)
        got_pieces, deck, column_first, column_second, row_first, row_second = call(
            rim_kernel,
            [
                ((2 * PLANES, SLOTS), BF16),
                ((DROWS, PLANES, DCOLS), F32),
                ((PLANES, COLS), F32),
                ((PLANES, COLS), F32),
                ((PLANES + 8, DCOLS), F32),
                ((PLANES + 8, DCOLS), F32),
            ],
            [got, rim_map, near_map, rim_keep, deck, back_state],
            name="rim",
        )
        row_first = lax.ppermute(row_first, everyone, pairs(1, 0, True))
        row_second = lax.ppermute(row_second, everyone, pairs(1, 1, True))
        column_first = lax.ppermute(column_first, everyone, pairs(across_y, 0))
        column_second = lax.ppermute(column_second, everyone, pairs(across_y, 1))
        if section == 0:
            back_state, fill_map, keep = call(
                first_fill_kernel,
                [((ROWS, PLANES, COLS), F32), ((SLOTS, ROWS * COLS), BF16), ((ROWS, 8, COLS), F32)],
                [got_pieces, placing, back_state],
                name="fill",
            )
            base = [deck, back_state]
        else:
            (back_state,) = call(
                fill_kernel,
                [((ROWS, PLANES, COLS), F32)],
                [got_pieces, fill_map, keep, back_state],
                name="fill",
            )
        ins = [deck, back_state, column_first, column_second, row_first, row_second, metrics, keep]
        if section > 0:
            ins += base
        kernel = functools.partial(section_kernel, section)
        if section < 2:
            deck, back_state, answers = call(
                kernel,
                [
                    ((DROWS, PLANES, DCOLS), F32),
                    ((ROWS, PLANES, COLS), F32),
                    ((MEMBERS, 1, PACKED), F32),
                ],
                ins + [far, near],
                scratch=pieces,
                name="section",
            )
        else:
            deck, back_state = call(
                kernel,
                [((PLANES, DROWS, DCOLS), F32), ((PLANES, ROWS, COLS), F32)],
                ins,
                name="section",
            )
    return deck.reshape(deck_fields.shape), back_state.reshape(back_fields.shape)


def solution(mesh):
    return jax.shard_map(
        local,
        mesh=mesh,
        in_specs=(
            P(None, None, ("grid", "gx", "gy"), None),
            P(None, None, ("grid", "gx"), "gy"),
            P(None, ("grid", "gx", "gy"), None),
            P(("grid", "gx", "gy"), None, None),
            P(("grid", "gx", "gy"), None, None),
            P(("grid", "gx", "gy"), None),
        ),
        out_specs=(P(None, None, ("grid", "gx", "gy"), None), P(None, None, ("grid", "gx"), "gy")),
        check_vma=False,
    )
```

```python
import functools

import jax
import jax.numpy as jnp
from jax import lax
from jax.experimental import pallas as pl
from jax.experimental.pallas import tpu as pltpu
from jax.sharding import PartitionSpec as P

SPAN = 32
PLANES = 96
MEMBERS = 64
CAP = 16
SLOTS = MEMBERS * CAP
ROWS = 16
COLS = 128
DROWS = 2
DCOLS = 384
FRINGE = 512
NEAR = 4
TIME_STEP = 0.05
SMAGORINSKY = 0.02
F32 = jnp.float32
BF16 = jnp.bfloat16
NT = (((1,), (1,)), ((), ()))
NN = (((1,), (0,)), ((), ()))
VMEM_LIMIT = 24 * 1024 * 1024
PACKED = CAP * PLANES
R_ROW, R_COL, R_FX, R_FY, R_GRID = range(5)


def position():
    column = lax.axis_index("gy")
    line = lax.axis_index("grid") * lax.axis_size("gx") + lax.axis_index("gx")
    tile = line * lax.axis_size("gy") + column
    return column, line, tile


def dot(a, b, dims):
    return lax.dot_general(a, b, dims, preferred_element_type=F32)


def iota(shape, dim):
    return lax.broadcasted_iota(jnp.int32, shape, dim)


def call(kernel, outs, ins, scratch=(), hbm_at=(), outs_in=pltpu.VMEM, name=None):
    def spec(i):
        return pl.BlockSpec(memory_space=pltpu.HBM if i in hbm_at else pltpu.VMEM)

    ins = [pltpu.with_memory_space_constraint(x, pltpu.HBM) if i in hbm_at else x for i, x in enumerate(ins)]
    return pl.pallas_call(
        kernel,
        out_shape=tuple(jax.ShapeDtypeStruct(s, d) for s, d in outs),
        in_specs=[spec(i) for i in range(len(ins))],
        out_specs=tuple(pl.BlockSpec(memory_space=outs_in) for _ in outs),
        scratch_shapes=list(scratch),
        compiler_params=pltpu.CompilerParams(vmem_limit_bytes=VMEM_LIMIT),
        name=name,
    )(*ins)


def route_kernel(
    donors_hbm, stencil_hbm, cells_hbm, request_ref, local_ref, rim_ref, near_ref, keep_ref,
    donors_ref, stencil_ref, cells_ref, sems,
):
    pairs = [(donors_hbm, donors_ref), (stencil_hbm, stencil_ref), (cells_hbm, cells_ref)]
    copies = [pltpu.make_async_copy(a, b, sems.at[i]) for i, (a, b) in enumerate(pairs)]
    for c in copies:
        c.start()
    for c in copies:
        c.wait()
    donors = donors_ref[...]
    member = (iota((MEMBERS, FRINGE), 0) == donors).astype(F32)
    before = (iota((FRINGE, FRINGE), 0) < iota((FRINGE, FRINGE), 1)).astype(BF16)
    member_b = member.astype(BF16)
    earlier = dot(member_b, before, NN)
    rank = jnp.sum(member * earlier, axis=0, keepdims=True).astype(jnp.int32)
    at_rank = (iota((CAP, FRINGE), 0) == rank).astype(F32)

    def place(values):
        stacked = jnp.concatenate([at_rank * v.astype(F32) for v in values], axis=0)
        return dot(member_b, stacked.astype(BF16), NT)

    row = stencil_ref[0:1, :]
    col = stencil_ref[1:2, :]
    lane = iota((1, FRINGE), 1)
    grid = jnp.where(lane < NEAR, 1, 2)
    half = col >> 1
    sent = place([row, half, col - 2 * half, stencil_ref[2:3, :], stencil_ref[3:4, :], grid])
    request_ref[:, 0, :] = jnp.zeros((MEMBERS, 128), F32)
    request_ref[:, 0, 0:16] = sent[:, 0:16]
    request_ref[:, 0, 16:32] = 2.0 * sent[:, 16:32] + sent[:, 32:48]
    request_ref[:, 0, 32:80] = sent[:, 48:96]
    cells = jnp.concatenate([jnp.zeros((1, NEAR), jnp.int32), cells_ref[...]], axis=1)
    far = lane >= NEAR
    local_ref[...] = place(
        [
            jnp.where(far, (cells >> 7) + 1, 0),
            jnp.where(far, cells & 127, 0),
            jnp.where(far, 0, lane + 1),
        ]
    )
    landing(local_ref, rim_ref, near_ref, keep_ref)


def over_eight(x):
    return jnp.sum(x.reshape(MEMBERS // 8, 8, COLS), axis=0)


def kept(listed):
    return 1.0 - jnp.broadcast_to(jnp.sum(listed, axis=0, keepdims=True), (8, COLS))


def landing(local_ref, rim_ref, near_ref, keep_ref):
    lane = iota((MEMBERS, COLS), 1)
    places = local_ref[...].astype(jnp.int32)
    listed = [jnp.zeros((8, COLS), F32) for _ in range(3)]

    for s in range(CAP):
        at = slice(s * MEMBERS, (s + 1) * MEMBERS)
        row = jnp.broadcast_to(places[:, s : s + 1] - 1, (MEMBERS, COLS))
        col = jnp.broadcast_to(places[:, CAP + s : CAP + s + 1], (MEMBERS, COLS))
        hit = jnp.where(lane == col, 1.0, 0.0)
        for i, r in enumerate((0, ROWS - 1)):
            here = jnp.where(row == r, hit, 0.0)
            rim_ref[at, i * COLS : (i + 1) * COLS] = here.astype(BF16)
            listed[i] = listed[i] + over_eight(here)
        side = jnp.where(col == 0, row, jnp.where(col == COLS - 1, row + ROWS, -1))
        here = jnp.where((lane == side) & (row >= 0), 1.0, 0.0)
        rim_ref[at, 2 * COLS : 3 * COLS] = here.astype(BF16)
        listed[2] = listed[2] + over_eight(here)
        if s < NEAR:
            near = places[:, 2 * CAP + s : 2 * CAP + s + 1] - 1
            place = jnp.where(near >= 0, (near >> 1) * COLS + COLS - 2 + (near & 1), -1)
            place = jnp.broadcast_to(place, (MEMBERS, COLS))
            for r in range(DROWS):
                near_ref[at, r * COLS : (r + 1) * COLS] = jnp.where(lane + r * COLS == place, 1.0, 0.0).astype(BF16)
    for i in range(3):
        keep_ref[i] = kept(listed[i])


def split(x):
    high = x.astype(BF16)
    return high, (x - high.astype(F32)).astype(BF16)


def weights(request_ref, rows_ref, far_ref, near_ref):
    rows_ref[...] = request_ref[:, 0, :]
    request = rows_ref[...]
    whole = request.astype(jnp.int32)
    lane = iota((MEMBERS, COLS), 1)

    def wide(x, f, s):
        at = f * CAP + s
        return jnp.broadcast_to(x[:, at : at + 1], (MEMBERS, COLS))

    for s in range(CAP):
        at = slice(s * MEMBERS, (s + 1) * MEMBERS)
        col = wide(whole, R_COL, s)
        fx = wide(request, R_FX, s) * (1.0 / 16.0)
        fy = wide(request, R_FY, s) * (1.0 / 16.0)
        grid = wide(request, R_GRID, s)
        on_deck = jnp.where(grid == 2.0, 1.0, 0.0)
        first, second = on_deck * (1.0 - fx), on_deck * fx
        share = [first * (1.0 - fy), first * fy, second * (1.0 - fy), second * fy]
        for t in range(DCOLS // COLS):
            low, high = lane + t * COLS == col, lane + t * COLS == col + 1
            for r in range(DROWS):
                here = jnp.where(low, share[2 * r], jnp.where(high, share[2 * r + 1], 0.0))
                start = r * DCOLS + t * COLS
                far_ref[at, start : start + COLS] = here.astype(BF16)
        if s < NEAR:
            row = wide(whole, R_ROW, s)
            on_back = jnp.where(grid == 1.0, 1.0, 0.0)
            across = jnp.where(lane == col, on_back * (1.0 - fy), jnp.where(lane == col + 1, on_back * fy, 0.0))
            first, second = (1.0 - fx) * across, fx * across
            for r in range(ROWS):
                here = jnp.where(row == r, first, jnp.where(row + 1 == r, second, 0.0))
                near_ref[at, r * COLS : (r + 1) * COLS] = here.astype(BF16)


def stack_deck(pieces, r, value):
    high, low = split(value)
    pieces[0:PLANES, r * DCOLS : (r + 1) * DCOLS] = high
    pieces[128 : 128 + PLANES, r * DCOLS : (r + 1) * DCOLS] = low


def stack_back(pieces, r, value):
    high, low = split(value)
    pieces[0:PLANES, r * COLS : (r + 1) * COLS] = high
    pieces[128 : 128 + PLANES, r * COLS : (r + 1) * COLS] = low


def clear_pieces(deck_pieces, back_pieces):
    for pieces in (deck_pieces, back_pieces):
        gap = jnp.zeros((128 - PLANES, pieces.shape[1]), BF16)
        pieces[PLANES:128, :] = gap
        pieces[128 + PLANES : 256, :] = gap


def answer(far_ref, near_ref, deck_pieces, back_pieces, out_ref):
    lane = iota((MEMBERS, 128), 1)
    for q in range(CAP // 4):
        got = dot(far_ref[q * 256 : (q + 1) * 256, :], deck_pieces[...], NT)
        if q == 0:
            got = got + dot(near_ref[...], back_pieces[...], NT)
        got = got[:, 0:128] + got[:, 128:256]
        a = [got[i * MEMBERS : (i + 1) * MEMBERS, :] for i in range(4)]
        base = q * 4 * PLANES
        out_ref[:, 0, base : base + 128] = jnp.where(lane < 96, a[0], pltpu.roll(a[1], 96, 1))
        out_ref[:, 0, base + 128 : base + 256] = jnp.where(
            lane < 64, pltpu.roll(a[1], 96, 1), pltpu.roll(a[2], 64, 1)
        )
        out_ref[:, 0, base + 256 : base + 384] = jnp.where(
            lane < 32, pltpu.roll(a[2], 64, 1), pltpu.roll(a[3], 32, 1)
        )


def first_answer_kernel(
    request_ref, deck_hbm, back_hbm, deck_out, back_out, far_ref, near_ref, out_ref,
    rows_ref, deck_pieces, back_pieces, deck_sems, back_sems,
):
    copies = [
        pltpu.make_async_copy(deck_hbm.at[:, r, :], deck_out.at[r], deck_sems.at[r]) for r in range(DROWS)
    ] + [pltpu.make_async_copy(back_hbm.at[:, r, :], back_out.at[r], back_sems.at[r]) for r in range(ROWS)]
    for c in copies:
        c.start()
    clear_pieces(deck_pieces, back_pieces)
    weights(request_ref, rows_ref, far_ref, near_ref)
    for c in copies:
        c.wait()
    for r in range(DROWS):
        stack_deck(deck_pieces, r, deck_out[r])
    for r in range(ROWS):
        stack_back(back_pieces, r, back_out[r])
    answer(far_ref, near_ref, deck_pieces, back_pieces, out_ref)


def rim_kernel(
    got_ref, rim_ref, near_ref, keep_ref, deck_ref, back_ref,
    got_pieces, deck_out, column_first, column_second, row_first, row_second, plain_ref,
):
    plain_ref[...] = got_ref[:, 0, :]
    lane = iota((MEMBERS, 128), 1)
    for q in range(CAP // 4):
        base = q * 4 * PLANES
        c0 = plain_ref[:, base : base + 128]
        c1 = plain_ref[:, base + 128 : base + 256]
        c2 = plain_ref[:, base + 256 : base + 384]
        a0 = jnp.where(lane < 96, c0, 0.0)
        a1 = jnp.where(lane < 32, pltpu.roll(c0, 32, 1), jnp.where(lane < 96, pltpu.roll(c1, 32, 1), 0.0))
        a2 = jnp.where(lane < 64, pltpu.roll(c1, 64, 1), jnp.where(lane < 96, pltpu.roll(c2, 64, 1), 0.0))
        a3 = jnp.where(lane < 96, pltpu.roll(c2, 96, 1), 0.0)
        across = jnp.concatenate([a0, a1, a2, a3], axis=0).T
        high, low = split(across[0:PLANES, :])
        got_pieces[0:PLANES, q * 256 : (q + 1) * 256] = high
        got_pieces[PLANES : 2 * PLANES, q * 256 : (q + 1) * 256] = low
    near = dot(got_pieces[:, 0:256], near_ref[...], NN)
    near = near[0:PLANES] + near[PLANES : 2 * PLANES]
    lane = iota((PLANES, 128), 1)
    column, line, tile = position()
    odd = lax.rem(tile, 2) == 0
    odd_line = lax.rem(line, 2) == 0
    deck = []
    for r in range(DROWS):
        outer = jnp.where(lane >= 126, near[:, r * 128 : (r + 1) * 128], deck_ref[r, :, 256:384])
        deck.append(jnp.concatenate([deck_ref[r, :, 0:256], outer], axis=1))
        deck_out[r] = deck[r]
    row_first[0:PLANES, :] = jnp.where(odd, deck[0], deck[1])
    row_second[0:PLANES, :] = jnp.where(odd, deck[1], deck[0])
    rim = dot(got_pieces[...], rim_ref[...], NN)
    rim = rim[0:PLANES] + rim[PLANES : 2 * PLANES]
    north = back_ref[0] * keep_ref[0, 0:1, :] + rim[:, 0:COLS]
    south = back_ref[ROWS - 1] * keep_ref[1, 0:1, :] + rim[:, COLS : 2 * COLS]
    column_first[...] = jnp.where(odd_line, north, south)
    column_second[...] = jnp.where(odd_line, south, north)
    ends = jnp.zeros((PLANES, COLS), F32)
    for r in range(ROWS):
        ends = jnp.where(lane == r, back_ref[r, :, 0:1], ends)
        ends = jnp.where(lane == ROWS + r, back_ref[r, :, COLS - 1 : COLS], ends)
    ends = ends * keep_ref[2, 0:1, :] + rim[:, 2 * COLS : 3 * COLS]
    ends = jnp.concatenate([ends, jnp.zeros((COLS - PLANES, COLS), F32)], axis=0).T
    parts = [ends[i * 8 : (i + 1) * 8, :] for i in range(4)]
    for side, flag in ((row_first, odd), (row_second, jnp.logical_not(odd))):
        for i in range(2):
            side[PLANES : PLANES + 8, i * COLS : (i + 1) * COLS] = jnp.where(flag, parts[i], parts[2 + i])
        side[PLANES : PLANES + 8, 2 * COLS : 3 * COLS] = jnp.zeros((8, COLS), F32)


def fill_kernel(got_pieces, fill_ref, keep_ref, back_ref, back_out):
    for c in range(ROWS // 2):
        new = dot(got_pieces[...], fill_ref[:, c * 256 : (c + 1) * 256], NN)
        new = new[0:PLANES] + new[PLANES : 2 * PLANES]
        for half in range(2):
            r = 2 * c + half
            back_out[r] = back_ref[r] * keep_ref[r, 0:1, :] + new[:, half * 128 : (half + 1) * 128]


def first_fill_kernel(got_pieces, local_ref, back_ref, back_out, fill_ref, keep_ref):
    lane = iota((MEMBERS, COLS), 1)
    places = local_ref[...].astype(jnp.int32)
    listed = [jnp.zeros((8, COLS), F32) for _ in range(ROWS)]
    for s in range(CAP):
        at = slice(s * MEMBERS, (s + 1) * MEMBERS)
        row = jnp.broadcast_to(places[:, s : s + 1] - 1, (MEMBERS, COLS))
        col = jnp.broadcast_to(places[:, CAP + s : CAP + s + 1], (MEMBERS, COLS))
        hit = jnp.where(lane == col, 1.0, 0.0)
        for r in range(ROWS):
            here = jnp.where(row == r, hit, 0.0)
            fill_ref[at, r * COLS : (r + 1) * COLS] = here.astype(BF16)
            listed[r] = listed[r] + over_eight(here)
    for r in range(ROWS):
        keep_ref[r] = kept(listed[r])
    fill_kernel(got_pieces, fill_ref, keep_ref, back_ref, back_out)


def update(here, minus_xi, plus_xi, minus_eta, plus_eta, metric, keep, base, section):
    weight = (1.0, 0.25, 2.0 / 3.0)[section]
    step = (weight * TIME_STEP) * keep
    d_xi, d_eta, d_span, lap = [], [], [], []
    strain = None
    for c in range(3):
        f = here[c]
        plus_span = pltpu.roll(f, SPAN - 1, 0)
        minus_span = pltpu.roll(f, 1, 0)
        a = plus_xi[c] - minus_xi[c]
        b = plus_eta[c] - minus_eta[c]
        s = plus_span - minus_span
        square = a * a + b * b + s * s
        strain = square if strain is None else strain + square
        if metric is None:
            around = (plus_xi[c] + minus_xi[c]) + (plus_eta[c] + minus_eta[c]) + (plus_span + minus_span)
            lap.append(around - 6.0 * f)
        else:
            doubled = 2.0 * f
            l_xi = plus_xi[c] - doubled + minus_xi[c]
            l_eta = plus_eta[c] - doubled + minus_eta[c]
            lap.append(metric[4] * l_xi + metric[5] * l_eta + (plus_span - doubled + minus_span))
        d_xi.append(a)
        d_eta.append(b)
        d_span.append(s)
    viscosity = (SMAGORINSKY * step) * jnp.sqrt(1.0 + 0.25 * strain)
    half = 0.5 * step
    if metric is None:
        speed_xi, speed_eta = half * here[0], half * here[1]
    else:
        speed_xi = half * (metric[0] * here[0] + metric[1] * here[1])
        speed_eta = half * (metric[2] * here[0] + metric[3] * here[1])
    speed_span = half * here[2]
    out = []
    for c in range(3):
        change = viscosity * lap[c] - (speed_xi * d_xi[c] + speed_eta * d_eta[c] + speed_span * d_span[c])
        if section == 0:
            out.append(here[c] + change)
        elif section == 1:
            out.append(0.75 * base[c] + (0.25 * here[c] + change))
        else:
            out.append(base[c] * (1.0 / 3.0) + ((2.0 / 3.0) * here[c] + change))
    return out


def fields(ref, at):
    return [ref[at + (slice(c * SPAN, (c + 1) * SPAN), slice(None))] for c in range(3)]


def section_kernel(section, *refs):
    refs = list(refs)
    deck_ref, back_ref, column_first, column_second, row_first, row_second, metric_ref, keep_ref = refs[:8]
    del refs[:8]
    base_deck = base_back = None
    if section > 0:
        base_deck, base_back = refs[:2]
        del refs[:2]
    last = section == 2
    if last:
        deck_hbm, back_hbm, deck_out, back_out, deck_sems, back_sems = refs
        copies = []

        def send(rows, r, whole, sems):
            copies.append(pltpu.make_async_copy(rows.at[r], whole.at[:, r, :], sems.at[r]))
            copies[-1].start()

    else:
        far_ref, near_ref, deck_out, back_out, answer_out, deck_pieces, back_pieces = refs
        clear_pieces(deck_pieces, back_pieces)
    column, line, tile = position()
    odd = lax.rem(tile, 2) == 0
    odd_line = lax.rem(line, 2) == 0
    west_end = (column > 0).astype(F32)
    east_end = (column < lax.axis_size("gy") - 1).astype(F32)

    def ordered(flag, first, second, at):
        a, b = first[at], second[at]
        return jnp.where(flag, a, b), jnp.where(flag, b, a)

    spans = [slice(c * SPAN, (c + 1) * SPAN) for c in range(3)]
    across = [ordered(odd, row_first, row_second, (at, slice(None))) for at in spans]
    beside = []
    halves = [
        ordered(odd, row_first, row_second, (slice(PLANES, PLANES + 8), slice(i * COLS, (i + 1) * COLS)))
        for i in range(2)
    ]
    for side in range(2):
        cells = jnp.concatenate([halves[0][side], halves[1][side], jnp.zeros((COLS - 16, COLS), F32)], axis=0)
        beside.append(cells.T)
    north_end = (line > 0).astype(F32)
    south_end = (line < lax.axis_size("grid") * lax.axis_size("gx") - 1).astype(F32)
    along = [ordered(odd_line, column_first, column_second, (at, slice(None))) for at in spans]
    along = [(before * north_end, after * south_end) for before, after in along]
    lane = iota((SPAN, DCOLS), 1)
    keep_deck = jnp.where(iota((1, DCOLS), 1) < DCOLS - 2, 1.0, 0.0)
    for r in range(DROWS):
        here = fields(deck_ref, (r,))
        if r == 0:
            minus = [a[0] for a in across]
            plus = fields(deck_ref, (1,))
        else:
            minus = fields(deck_ref, (0,))
            plus = [a[1] for a in across]
        m = [metric_ref[i, r : r + 1, :] for i in range(4)]
        metric = m + [m[0] * m[0] + m[1] * m[1], m[2] * m[2] + m[3] * m[3]]
        plus_eta = [jnp.where(lane == DCOLS - 1, 0.0, pltpu.roll(f, DCOLS - 1, 1)) for f in here]
        minus_eta = [jnp.where(lane == 0, 0.0, pltpu.roll(f, 1, 1)) for f in here]
        base = fields(base_deck, (r,)) if section > 0 else None
        new = update(here, minus, plus, minus_eta, plus_eta, metric, keep_deck, base, section)
        for c in range(3):
            deck_out[r, c * SPAN : (c + 1) * SPAN, :] = new[c]
        if last:
            send(deck_out, r, deck_hbm, deck_sems)
        else:
            stack_deck(deck_pieces, r, jnp.concatenate(new, axis=0))
    lane = iota((SPAN, COLS), 1)
    for r in range(ROWS):
        here = fields(back_ref, (r,))
        minus = fields(back_ref, (r - 1,)) if r > 0 else [a[0] for a in along]
        plus = fields(back_ref, (r + 1,)) if r < ROWS - 1 else [a[1] for a in along]
        plus_eta, minus_eta = [], []
        for c in range(3):
            from_west = beside[0][spans[c], r : r + 1] * west_end
            from_east = beside[1][spans[c], r : r + 1] * east_end
            plus_eta.append(jnp.where(lane == COLS - 1, from_east, pltpu.roll(here[c], COLS - 1, 1)))
            minus_eta.append(jnp.where(lane == 0, from_west, pltpu.roll(here[c], 1, 1)))
        base = fields(base_back, (r,)) if section > 0 else None
        new = update(here, minus, plus, minus_eta, plus_eta, None, keep_ref[r, 0:1, :], base, section)
        for c in range(3):
            back_out[r, c * SPAN : (c + 1) * SPAN, :] = new[c]
        if last:
            send(back_out, r, back_hbm, back_sems)
        else:
            stack_back(back_pieces, r, jnp.concatenate(new, axis=0))
    if last:
        for c in copies:
            c.wait()
    else:
        answer(far_ref, near_ref, deck_pieces, back_pieces, answer_out)


def local(deck_fields, back_fields, metrics, donors, stencil, fringe_cells):
    group = ("gx", "gy")
    everyone = ("grid", "gx", "gy")

    def exchange(x):
        return lax.all_to_all(x, group, split_axis=0, concat_axis=0, tiled=True)

    count = lax.axis_size("grid") * lax.axis_size("gx") * lax.axis_size("gy")
    across_y = lax.axis_size("gy")

    def pairs(step, first, periodic=False):
        out = []
        for t in range(count):
            if (t // step) % 2 == first:
                other = (t + step) % count
                if periodic or t + step < count:
                    out += [(t, other), (other, t)]
                else:
                    out += [(t, t ^ 1), (other, other ^ 1)]
        return out

    deck_in = deck_fields.reshape(PLANES, DROWS, DCOLS)
    back_in = back_fields.reshape(PLANES, ROWS, COLS)
    request, placing, rim_map, near_map, rim_keep = call(
        route_kernel,
        [
            ((MEMBERS, 1, 128), F32),
            ((MEMBERS, 3 * CAP), F32),
            ((SLOTS, 3 * COLS), BF16),
            ((NEAR * MEMBERS, 2 * COLS), BF16),
            ((3, 8, COLS), F32),
        ],
        [donors.reshape(1, FRINGE), stencil.reshape(FRINGE, 4).T, fringe_cells],
        scratch=[
            pltpu.VMEM((1, FRINGE), jnp.int32),
            pltpu.VMEM((4, FRINGE), jnp.int32),
            pltpu.VMEM((1, FRINGE - NEAR), jnp.int32),
            pltpu.SemaphoreType.DMA((3,)),
        ],
        hbm_at=(0, 1, 2),
        name="route",
    )
    request = exchange(request)
    pieces = [pltpu.VMEM((256, DROWS * DCOLS), BF16), pltpu.VMEM((256, ROWS * COLS), BF16)]
    deck, back_state, far, near, answers = call(
        first_answer_kernel,
        [
            ((DROWS, PLANES, DCOLS), F32),
            ((ROWS, PLANES, COLS), F32),
            ((SLOTS, DROWS * DCOLS), BF16),
            ((NEAR * MEMBERS, ROWS * COLS), BF16),
            ((MEMBERS, 1, PACKED), F32),
        ],
        [request, deck_in, back_in],
        scratch=[pltpu.VMEM((MEMBERS, 128), F32)]
        + pieces
        + [
            pltpu.SemaphoreType.DMA((DROWS,)),
            pltpu.SemaphoreType.DMA((ROWS,)),
        ],
        hbm_at=(1, 2),
        name="first_answer",
    )
    base = None
    for section in range(3):
        got = exchange(answers)
        got_pieces, deck, column_first, column_second, row_first, row_second = call(
            rim_kernel,
            [
                ((2 * PLANES, SLOTS), BF16),
                ((DROWS, PLANES, DCOLS), F32),
                ((PLANES, COLS), F32),
                ((PLANES, COLS), F32),
                ((PLANES + 8, DCOLS), F32),
                ((PLANES + 8, DCOLS), F32),
            ],
            [got, rim_map, near_map, rim_keep, deck, back_state],
            scratch=[pltpu.VMEM((MEMBERS, PACKED), F32)],
            name="rim",
        )
        row_first = lax.ppermute(row_first, everyone, pairs(1, 1, True))
        row_second = lax.ppermute(row_second, everyone, pairs(1, 0, True))
        column_first = lax.ppermute(column_first, everyone, pairs(across_y, 1))
        column_second = lax.ppermute(column_second, everyone, pairs(across_y, 0))
        if section == 0:
            back_state, fill_map, keep = call(
                first_fill_kernel,
                [((ROWS, PLANES, COLS), F32), ((SLOTS, ROWS * COLS), BF16), ((ROWS, 8, COLS), F32)],
                [got_pieces, placing, back_state],
                name="fill",
            )
            base = [deck, back_state]
        else:
            (back_state,) = call(
                fill_kernel,
                [((ROWS, PLANES, COLS), F32)],
                [got_pieces, fill_map, keep, back_state],
                name="fill",
            )
        ins = [deck, back_state, column_first, column_second, row_first, row_second, metrics, keep]
        if section > 0:
            ins += base
        kernel = functools.partial(section_kernel, section)
        if section < 2:
            deck, back_state, answers = call(
                kernel,
                [
                    ((DROWS, PLANES, DCOLS), F32),
                    ((ROWS, PLANES, COLS), F32),
                    ((MEMBERS, 1, PACKED), F32),
                ],
                ins + [far, near],
                scratch=pieces,
                name="section",
            )
        else:
            deck, back_state = call(
                kernel,
                [((PLANES, DROWS, DCOLS), F32), ((PLANES, ROWS, COLS), F32)],
                ins,
                scratch=[
                    pltpu.VMEM((DROWS, PLANES, DCOLS), F32),
                    pltpu.VMEM((ROWS, PLANES, COLS), F32),
                    pltpu.SemaphoreType.DMA((DROWS,)),
                    pltpu.SemaphoreType.DMA((ROWS,)),
                ],
                outs_in=pl.ANY,
                name="section",
            )
    return deck.reshape(deck_fields.shape), back_state.reshape(back_fields.shape)


def solution(mesh):
    return jax.shard_map(
        local,
        mesh=mesh,
        in_specs=(
            P(None, None, ("grid", "gx", "gy"), None),
            P(None, None, ("grid", "gx"), "gy"),
            P(None, ("grid", "gx", "gy"), None),
            P(("grid", "gx", "gy"), None, None),
            P(("grid", "gx", "gy"), None, None),
            P(("grid", "gx", "gy"), None),
        ),
        out_specs=(P(None, None, ("grid", "gx", "gy"), None), P(None, None, ("grid", "gx"), "gy")),
        check_vma=False,
    )
```

```python
import functools

import jax
import jax.numpy as jnp
from jax import lax
from jax.experimental import pallas as pl
from jax.experimental.pallas import tpu as pltpu
from jax.sharding import PartitionSpec as P

SPAN = 32
PLANES = 96
MEMBERS = 64
CAP = 16
SLOTS = MEMBERS * CAP
ROWS = 16
COLS = 128
DROWS = 2
DCOLS = 384
FRINGE = 512
NEAR = 4
TIME_STEP = 0.05
SMAGORINSKY = 0.02
F32 = jnp.float32
BF16 = jnp.bfloat16
NT = (((1,), (1,)), ((), ()))
NN = (((1,), (0,)), ((), ()))
VMEM_LIMIT = 24 * 1024 * 1024
PACKED = CAP * PLANES
R_ROW, R_COL, R_FX, R_FY, R_GRID = range(5)


def position():
    column = lax.axis_index("gy")
    line = lax.axis_index("grid") * lax.axis_size("gx") + lax.axis_index("gx")
    tile = line * lax.axis_size("gy") + column
    return column, line, tile


def dot(a, b, dims):
    return lax.dot_general(a, b, dims, preferred_element_type=F32)


def iota(shape, dim):
    return lax.broadcasted_iota(jnp.int32, shape, dim)


def call(kernel, outs, ins, scratch=(), hbm_at=(), outs_in=pltpu.VMEM, name=None):
    def spec(i):
        return pl.BlockSpec(memory_space=pltpu.HBM if i in hbm_at else pltpu.VMEM)

    ins = [pltpu.with_memory_space_constraint(x, pltpu.HBM) if i in hbm_at else x for i, x in enumerate(ins)]
    return pl.pallas_call(
        kernel,
        out_shape=tuple(jax.ShapeDtypeStruct(s, d) for s, d in outs),
        in_specs=[spec(i) for i in range(len(ins))],
        out_specs=tuple(pl.BlockSpec(memory_space=outs_in) for _ in outs),
        scratch_shapes=list(scratch),
        compiler_params=pltpu.CompilerParams(vmem_limit_bytes=VMEM_LIMIT),
        name=name,
    )(*ins)


def route_kernel(
    donors_hbm, stencil_hbm, cells_hbm, request_ref, local_ref, rim_ref, near_ref, keep_ref,
    donors_ref, stencil_ref, cells_ref, sems,
):
    pairs = [(donors_hbm, donors_ref), (stencil_hbm, stencil_ref), (cells_hbm, cells_ref)]
    copies = [pltpu.make_async_copy(a, b, sems.at[i]) for i, (a, b) in enumerate(pairs)]
    for c in copies:
        c.start()
    for c in copies:
        c.wait()
    donors = donors_ref[...]
    donors = (donors & 7) * 8 + (donors >> 3)
    member = (iota((MEMBERS, FRINGE), 0) == donors).astype(F32)
    before = (iota((FRINGE, FRINGE), 0) < iota((FRINGE, FRINGE), 1)).astype(BF16)
    member_b = member.astype(BF16)
    earlier = dot(member_b, before, NN)
    rank = jnp.sum(member * earlier, axis=0, keepdims=True).astype(jnp.int32)
    at_rank = (iota((CAP, FRINGE), 0) == rank).astype(F32)

    def place(values):
        stacked = jnp.concatenate([at_rank * v.astype(F32) for v in values], axis=0)
        return dot(member_b, stacked.astype(BF16), NT)

    row = stencil_ref[0:1, :]
    col = stencil_ref[1:2, :]
    lane = iota((1, FRINGE), 1)
    grid = jnp.where(lane < NEAR, 1, 2)
    half = col >> 1
    sent = place([row, half, col - 2 * half, stencil_ref[2:3, :], stencil_ref[3:4, :], grid])
    request_ref[:, 0, :] = jnp.zeros((MEMBERS, 128), F32)
    request_ref[:, 0, 0:16] = sent[:, 0:16]
    request_ref[:, 0, 16:32] = 2.0 * sent[:, 16:32] + sent[:, 32:48]
    request_ref[:, 0, 32:80] = sent[:, 48:96]
    cells = jnp.concatenate([jnp.zeros((1, NEAR), jnp.int32), cells_ref[...]], axis=1)
    far = lane >= NEAR
    local_ref[...] = place(
        [
            jnp.where(far, (cells >> 7) + 1, 0),
            jnp.where(far, cells & 127, 0),
            jnp.where(far, 0, lane + 1),
        ]
    )
    landing(local_ref, rim_ref, near_ref, keep_ref)


def over_eight(x):
    return jnp.sum(x.reshape(MEMBERS // 8, 8, COLS), axis=0)


def kept(listed):
    return 1.0 - jnp.broadcast_to(jnp.sum(listed, axis=0, keepdims=True), (8, COLS))


def landing(local_ref, rim_ref, near_ref, keep_ref):
    lane = iota((MEMBERS, COLS), 1)
    places = local_ref[...].astype(jnp.int32)
    listed = [jnp.zeros((8, COLS), F32) for _ in range(3)]

    for s in range(CAP):
        at = slice(s * MEMBERS, (s + 1) * MEMBERS)
        row = jnp.broadcast_to(places[:, s : s + 1] - 1, (MEMBERS, COLS))
        col = jnp.broadcast_to(places[:, CAP + s : CAP + s + 1], (MEMBERS, COLS))
        hit = jnp.where(lane == col, 1.0, 0.0)
        for i, r in enumerate((0, ROWS - 1)):
            here = jnp.where(row == r, hit, 0.0)
            rim_ref[at, i * COLS : (i + 1) * COLS] = here.astype(BF16)
            listed[i] = listed[i] + over_eight(here)
        side = jnp.where(col == 0, row, jnp.where(col == COLS - 1, row + ROWS, -1))
        here = jnp.where((lane == side) & (row >= 0), 1.0, 0.0)
        rim_ref[at, 2 * COLS : 3 * COLS] = here.astype(BF16)
        listed[2] = listed[2] + over_eight(here)
        if s < NEAR:
            near = places[:, 2 * CAP + s : 2 * CAP + s + 1] - 1
            place = jnp.where(near >= 0, (near >> 1) * COLS + COLS - 2 + (near & 1), -1)
            place = jnp.broadcast_to(place, (MEMBERS, COLS))
            for r in range(DROWS):
                near_ref[at, r * COLS : (r + 1) * COLS] = jnp.where(lane + r * COLS == place, 1.0, 0.0).astype(BF16)
    for i in range(3):
        keep_ref[i] = kept(listed[i])


def split(x):
    high = x.astype(BF16)
    return high, (x - high.astype(F32)).astype(BF16)


def weights(request_ref, rows_ref, far_ref, near_ref):
    rows_ref[...] = request_ref[:, 0, :]
    request = rows_ref[...]
    whole = request.astype(jnp.int32)
    lane = iota((MEMBERS, COLS), 1)

    def wide(x, f, s):
        at = f * CAP + s
        return jnp.broadcast_to(x[:, at : at + 1], (MEMBERS, COLS))

    for s in range(CAP):
        at = slice(s * MEMBERS, (s + 1) * MEMBERS)
        col = wide(whole, R_COL, s)
        fx = wide(request, R_FX, s) * (1.0 / 16.0)
        fy = wide(request, R_FY, s) * (1.0 / 16.0)
        grid = wide(request, R_GRID, s)
        on_deck = jnp.where(grid == 2.0, 1.0, 0.0)
        first, second = on_deck * (1.0 - fx), on_deck * fx
        share = [first * (1.0 - fy), first * fy, second * (1.0 - fy), second * fy]
        for t in range(DCOLS // COLS):
            low, high = lane + t * COLS == col, lane + t * COLS == col + 1
            for r in range(DROWS):
                here = jnp.where(low, share[2 * r], jnp.where(high, share[2 * r + 1], 0.0))
                start = r * DCOLS + t * COLS
                far_ref[at, start : start + COLS] = here.astype(BF16)
        if s < NEAR:
            row = wide(whole, R_ROW, s)
            on_back = jnp.where(grid == 1.0, 1.0, 0.0)
            across = jnp.where(lane == col, on_back * (1.0 - fy), jnp.where(lane == col + 1, on_back * fy, 0.0))
            first, second = (1.0 - fx) * across, fx * across
            for r in range(ROWS):
                here = jnp.where(row == r, first, jnp.where(row + 1 == r, second, 0.0))
                near_ref[at, r * COLS : (r + 1) * COLS] = here.astype(BF16)


def stack_deck(pieces, r, value):
    high, low = split(value)
    pieces[0:PLANES, r * DCOLS : (r + 1) * DCOLS] = high
    pieces[128 : 128 + PLANES, r * DCOLS : (r + 1) * DCOLS] = low


def stack_back(pieces, r, value):
    high, low = split(value)
    pieces[0:PLANES, r * COLS : (r + 1) * COLS] = high
    pieces[128 : 128 + PLANES, r * COLS : (r + 1) * COLS] = low


def clear_pieces(deck_pieces, back_pieces):
    for pieces in (deck_pieces, back_pieces):
        gap = jnp.zeros((128 - PLANES, pieces.shape[1]), BF16)
        pieces[PLANES:128, :] = gap
        pieces[128 + PLANES : 256, :] = gap


def answer(far_ref, near_ref, deck_pieces, back_pieces, out_ref):
    lane = iota((MEMBERS, 128), 1)
    for q in range(CAP // 4):
        got = dot(far_ref[q * 256 : (q + 1) * 256, :], deck_pieces[...], NT)
        if q == 0:
            got = got + dot(near_ref[...], back_pieces[...], NT)
        got = got[:, 0:128] + got[:, 128:256]
        a = [got[i * MEMBERS : (i + 1) * MEMBERS, :] for i in range(4)]
        base = q * 4 * PLANES
        out_ref[:, 0, base : base + 128] = jnp.where(lane < 96, a[0], pltpu.roll(a[1], 96, 1))
        out_ref[:, 0, base + 128 : base + 256] = jnp.where(
            lane < 64, pltpu.roll(a[1], 96, 1), pltpu.roll(a[2], 64, 1)
        )
        out_ref[:, 0, base + 256 : base + 384] = jnp.where(
            lane < 32, pltpu.roll(a[2], 64, 1), pltpu.roll(a[3], 32, 1)
        )


def first_answer_kernel(
    request_ref, deck_hbm, back_hbm, deck_out, back_out, far_ref, near_ref, out_ref,
    rows_ref, deck_pieces, back_pieces, deck_sems, back_sems,
):
    copies = [
        pltpu.make_async_copy(deck_hbm.at[:, r, :], deck_out.at[r], deck_sems.at[r]) for r in range(DROWS)
    ] + [pltpu.make_async_copy(back_hbm.at[:, r, :], back_out.at[r], back_sems.at[r]) for r in range(ROWS)]
    for c in copies:
        c.start()
    clear_pieces(deck_pieces, back_pieces)
    weights(request_ref, rows_ref, far_ref, near_ref)
    for c in copies:
        c.wait()
    for r in range(DROWS):
        stack_deck(deck_pieces, r, deck_out[r])
    for r in range(ROWS):
        stack_back(back_pieces, r, back_out[r])
    answer(far_ref, near_ref, deck_pieces, back_pieces, out_ref)


def rim_kernel(
    got_ref, rim_ref, near_ref, keep_ref, deck_ref, back_ref,
    got_pieces, deck_out, column_first, column_second, row_first, row_second, plain_ref,
):
    plain_ref[...] = got_ref[:, 0, :]
    lane = iota((MEMBERS, 128), 1)
    for q in range(CAP // 4):
        base = q * 4 * PLANES
        c0 = plain_ref[:, base : base + 128]
        c1 = plain_ref[:, base + 128 : base + 256]
        c2 = plain_ref[:, base + 256 : base + 384]
        a0 = jnp.where(lane < 96, c0, 0.0)
        a1 = jnp.where(lane < 32, pltpu.roll(c0, 32, 1), jnp.where(lane < 96, pltpu.roll(c1, 32, 1), 0.0))
        a2 = jnp.where(lane < 64, pltpu.roll(c1, 64, 1), jnp.where(lane < 96, pltpu.roll(c2, 64, 1), 0.0))
        a3 = jnp.where(lane < 96, pltpu.roll(c2, 96, 1), 0.0)
        across = jnp.concatenate([a0, a1, a2, a3], axis=0).T
        high, low = split(across[0:PLANES, :])
        got_pieces[0:PLANES, q * 256 : (q + 1) * 256] = high
        got_pieces[PLANES : 2 * PLANES, q * 256 : (q + 1) * 256] = low
    near = dot(got_pieces[:, 0:256], near_ref[...], NN)
    near = near[0:PLANES] + near[PLANES : 2 * PLANES]
    lane = iota((PLANES, 128), 1)
    column, line, tile = position()
    odd = lax.rem(tile, 2) == 0
    odd_line = lax.rem(line, 2) == 0
    deck = []
    for r in range(DROWS):
        outer = jnp.where(lane >= 126, near[:, r * 128 : (r + 1) * 128], deck_ref[r, :, 256:384])
        deck.append(jnp.concatenate([deck_ref[r, :, 0:256], outer], axis=1))
        deck_out[r] = deck[r]
    row_first[0:PLANES, :] = jnp.where(odd, deck[0], deck[1])
    row_second[0:PLANES, :] = jnp.where(odd, deck[1], deck[0])
    rim = dot(got_pieces[...], rim_ref[...], NN)
    rim = rim[0:PLANES] + rim[PLANES : 2 * PLANES]
    north = back_ref[0] * keep_ref[0, 0:1, :] + rim[:, 0:COLS]
    south = back_ref[ROWS - 1] * keep_ref[1, 0:1, :] + rim[:, COLS : 2 * COLS]
    column_first[...] = jnp.where(odd_line, north, south)
    column_second[...] = jnp.where(odd_line, south, north)
    ends = jnp.zeros((PLANES, COLS), F32)
    for r in range(ROWS):
        ends = jnp.where(lane == r, back_ref[r, :, 0:1], ends)
        ends = jnp.where(lane == ROWS + r, back_ref[r, :, COLS - 1 : COLS], ends)
    ends = ends * keep_ref[2, 0:1, :] + rim[:, 2 * COLS : 3 * COLS]
    ends = jnp.concatenate([ends, jnp.zeros((COLS - PLANES, COLS), F32)], axis=0).T
    parts = [ends[i * 8 : (i + 1) * 8, :] for i in range(4)]
    for side, flag in ((row_first, odd), (row_second, jnp.logical_not(odd))):
        for i in range(2):
            side[PLANES : PLANES + 8, i * COLS : (i + 1) * COLS] = jnp.where(flag, parts[i], parts[2 + i])
        side[PLANES : PLANES + 8, 2 * COLS : 3 * COLS] = jnp.zeros((8, COLS), F32)


def fill_kernel(got_pieces, fill_ref, keep_ref, back_ref, back_out):
    for c in range(ROWS // 2):
        new = dot(got_pieces[...], fill_ref[:, c * 256 : (c + 1) * 256], NN)
        new = new[0:PLANES] + new[PLANES : 2 * PLANES]
        for half in range(2):
            r = 2 * c + half
            back_out[r] = back_ref[r] * keep_ref[r, 0:1, :] + new[:, half * 128 : (half + 1) * 128]


def first_fill_kernel(got_pieces, local_ref, back_ref, back_out, fill_ref, keep_ref):
    lane = iota((MEMBERS, COLS), 1)
    places = local_ref[...].astype(jnp.int32)
    listed = [jnp.zeros((8, COLS), F32) for _ in range(ROWS)]
    for s in range(CAP):
        at = slice(s * MEMBERS, (s + 1) * MEMBERS)
        row = jnp.broadcast_to(places[:, s : s + 1] - 1, (MEMBERS, COLS))
        col = jnp.broadcast_to(places[:, CAP + s : CAP + s + 1], (MEMBERS, COLS))
        hit = jnp.where(lane == col, 1.0, 0.0)
        for r in range(ROWS):
            here = jnp.where(row == r, hit, 0.0)
            fill_ref[at, r * COLS : (r + 1) * COLS] = here.astype(BF16)
            listed[r] = listed[r] + over_eight(here)
    for r in range(ROWS):
        keep_ref[r] = kept(listed[r])
    fill_kernel(got_pieces, fill_ref, keep_ref, back_ref, back_out)


def update(here, minus_xi, plus_xi, minus_eta, plus_eta, metric, keep, base, section):
    weight = (1.0, 0.25, 2.0 / 3.0)[section]
    step = (weight * TIME_STEP) * keep
    d_xi, d_eta, d_span, lap = [], [], [], []
    strain = None
    for c in range(3):
        f = here[c]
        plus_span = pltpu.roll(f, SPAN - 1, 0)
        minus_span = pltpu.roll(f, 1, 0)
        a = plus_xi[c] - minus_xi[c]
        b = plus_eta[c] - minus_eta[c]
        s = plus_span - minus_span
        square = a * a + b * b + s * s
        strain = square if strain is None else strain + square
        if metric is None:
            around = (plus_xi[c] + minus_xi[c]) + (plus_eta[c] + minus_eta[c]) + (plus_span + minus_span)
            lap.append(around - 6.0 * f)
        else:
            doubled = 2.0 * f
            l_xi = plus_xi[c] - doubled + minus_xi[c]
            l_eta = plus_eta[c] - doubled + minus_eta[c]
            lap.append(metric[4] * l_xi + metric[5] * l_eta + (plus_span - doubled + minus_span))
        d_xi.append(a)
        d_eta.append(b)
        d_span.append(s)
    stretched = 1.0 + 0.25 * strain
    viscosity = (SMAGORINSKY * step) * (stretched * lax.rsqrt(stretched))
    half = 0.5 * step
    if metric is None:
        speed_xi, speed_eta = half * here[0], half * here[1]
    else:
        speed_xi = half * (metric[0] * here[0] + metric[1] * here[1])
        speed_eta = half * (metric[2] * here[0] + metric[3] * here[1])
    speed_span = half * here[2]
    out = []
    for c in range(3):
        change = viscosity * lap[c] - (speed_xi * d_xi[c] + speed_eta * d_eta[c] + speed_span * d_span[c])
        if section == 0:
            out.append(here[c] + change)
        elif section == 1:
            out.append(0.75 * base[c] + (0.25 * here[c] + change))
        else:
            out.append(base[c] * (1.0 / 3.0) + ((2.0 / 3.0) * here[c] + change))
    return out


def fields(ref, at):
    return [ref[at + (slice(c * SPAN, (c + 1) * SPAN), slice(None))] for c in range(3)]


def section_kernel(section, *refs):
    refs = list(refs)
    deck_ref, back_ref, column_first, column_second, row_first, row_second, metric_ref, keep_ref = refs[:8]
    del refs[:8]
    base_deck = base_back = None
    if section > 0:
        base_deck, base_back = refs[:2]
        del refs[:2]
    last = section == 2
    if last:
        deck_hbm, back_hbm, deck_out, back_out, deck_sems, back_sems = refs
        copies = []

        def send(rows, r, whole, sems):
            copies.append(pltpu.make_async_copy(rows.at[r], whole.at[:, r, :], sems.at[r]))
            copies[-1].start()

    else:
        far_ref, near_ref, deck_out, back_out, answer_out, deck_pieces, back_pieces = refs
        clear_pieces(deck_pieces, back_pieces)
    column, line, tile = position()
    odd = lax.rem(tile, 2) == 0
    odd_line = lax.rem(line, 2) == 0
    west_end = (column > 0).astype(F32)
    east_end = (column < lax.axis_size("gy") - 1).astype(F32)

    def ordered(flag, first, second, at):
        a, b = first[at], second[at]
        return jnp.where(flag, a, b), jnp.where(flag, b, a)

    spans = [slice(c * SPAN, (c + 1) * SPAN) for c in range(3)]
    across = [ordered(odd, row_first, row_second, (at, slice(None))) for at in spans]
    beside = []
    halves = [
        ordered(odd, row_first, row_second, (slice(PLANES, PLANES + 8), slice(i * COLS, (i + 1) * COLS)))
        for i in range(2)
    ]
    for side in range(2):
        cells = jnp.concatenate([halves[0][side], halves[1][side], jnp.zeros((COLS - 16, COLS), F32)], axis=0)
        beside.append(cells.T)
    north_end = (line > 0).astype(F32)
    south_end = (line < lax.axis_size("grid") * lax.axis_size("gx") - 1).astype(F32)
    along = [ordered(odd_line, column_first, column_second, (at, slice(None))) for at in spans]
    along = [(before * north_end, after * south_end) for before, after in along]
    lane = iota((SPAN, DCOLS), 1)
    keep_deck = jnp.where(iota((1, DCOLS), 1) < DCOLS - 2, 1.0, 0.0)
    for r in range(DROWS):
        here = fields(deck_ref, (r,))
        if r == 0:
            minus = [a[0] for a in across]
            plus = fields(deck_ref, (1,))
        else:
            minus = fields(deck_ref, (0,))
            plus = [a[1] for a in across]
        m = [metric_ref[i, r : r + 1, :] for i in range(4)]
        metric = m + [m[0] * m[0] + m[1] * m[1], m[2] * m[2] + m[3] * m[3]]
        plus_eta = [jnp.where(lane == DCOLS - 1, 0.0, pltpu.roll(f, DCOLS - 1, 1)) for f in here]
        minus_eta = [jnp.where(lane == 0, 0.0, pltpu.roll(f, 1, 1)) for f in here]
        base = fields(base_deck, (r,)) if section > 0 else None
        new = update(here, minus, plus, minus_eta, plus_eta, metric, keep_deck, base, section)
        for c in range(3):
            deck_out[r, c * SPAN : (c + 1) * SPAN, :] = new[c]
        if last:
            send(deck_out, r, deck_hbm, deck_sems)
        else:
            stack_deck(deck_pieces, r, jnp.concatenate(new, axis=0))
    lane = iota((SPAN, COLS), 1)
    for r in range(ROWS):
        here = fields(back_ref, (r,))
        minus = fields(back_ref, (r - 1,)) if r > 0 else [a[0] for a in along]
        plus = fields(back_ref, (r + 1,)) if r < ROWS - 1 else [a[1] for a in along]
        plus_eta, minus_eta = [], []
        for c in range(3):
            from_west = beside[0][spans[c], r : r + 1] * west_end
            from_east = beside[1][spans[c], r : r + 1] * east_end
            plus_eta.append(jnp.where(lane == COLS - 1, from_east, pltpu.roll(here[c], COLS - 1, 1)))
            minus_eta.append(jnp.where(lane == 0, from_west, pltpu.roll(here[c], 1, 1)))
        base = fields(base_back, (r,)) if section > 0 else None
        new = update(here, minus, plus, minus_eta, plus_eta, None, keep_ref[r, 0:1, :], base, section)
        for c in range(3):
            back_out[r, c * SPAN : (c + 1) * SPAN, :] = new[c]
        if last:
            send(back_out, r, back_hbm, back_sems)
        else:
            stack_back(back_pieces, r, jnp.concatenate(new, axis=0))
    if last:
        for c in copies:
            c.wait()
    else:
        answer(far_ref, near_ref, deck_pieces, back_pieces, answer_out)


def local(deck_fields, back_fields, metrics, donors, stencil, fringe_cells):
    group = ("gy", "gx")
    everyone = ("grid", "gx", "gy")

    def exchange(x):
        return lax.all_to_all(x, group, split_axis=0, concat_axis=0, tiled=True)

    count = lax.axis_size("grid") * lax.axis_size("gx") * lax.axis_size("gy")
    across_y = lax.axis_size("gy")

    def pairs(step, first, periodic=False):
        out = []
        for t in range(count):
            if (t // step) % 2 == first:
                other = (t + step) % count
                if periodic or t + step < count:
                    out += [(t, other), (other, t)]
                else:
                    out += [(t, t ^ 1), (other, other ^ 1)]
        return out

    deck_in = deck_fields.reshape(PLANES, DROWS, DCOLS)
    back_in = back_fields.reshape(PLANES, ROWS, COLS)
    request, placing, rim_map, near_map, rim_keep = call(
        route_kernel,
        [
            ((MEMBERS, 1, 128), F32),
            ((MEMBERS, 3 * CAP), F32),
            ((SLOTS, 3 * COLS), BF16),
            ((NEAR * MEMBERS, 2 * COLS), BF16),
            ((3, 8, COLS), F32),
        ],
        [donors.reshape(1, FRINGE), stencil.reshape(FRINGE, 4).T, fringe_cells],
        scratch=[
            pltpu.VMEM((1, FRINGE), jnp.int32),
            pltpu.VMEM((4, FRINGE), jnp.int32),
            pltpu.VMEM((1, FRINGE - NEAR), jnp.int32),
            pltpu.SemaphoreType.DMA((3,)),
        ],
        hbm_at=(0, 1, 2),
        name="route",
    )
    request = exchange(request)
    pieces = [pltpu.VMEM((256, DROWS * DCOLS), BF16), pltpu.VMEM((256, ROWS * COLS), BF16)]
    deck, back_state, far, near, answers = call(
        first_answer_kernel,
        [
            ((DROWS, PLANES, DCOLS), F32),
            ((ROWS, PLANES, COLS), F32),
            ((SLOTS, DROWS * DCOLS), BF16),
            ((NEAR * MEMBERS, ROWS * COLS), BF16),
            ((MEMBERS, 1, PACKED), F32),
        ],
        [request, deck_in, back_in],
        scratch=[pltpu.VMEM((MEMBERS, 128), F32)]
        + pieces
        + [
            pltpu.SemaphoreType.DMA((DROWS,)),
            pltpu.SemaphoreType.DMA((ROWS,)),
        ],
        hbm_at=(1, 2),
        name="first_answer",
    )
    base = None
    for section in range(3):
        got = exchange(answers)
        got_pieces, deck, column_first, column_second, row_first, row_second = call(
            rim_kernel,
            [
                ((2 * PLANES, SLOTS), BF16),
                ((DROWS, PLANES, DCOLS), F32),
                ((PLANES, COLS), F32),
                ((PLANES, COLS), F32),
                ((PLANES + 8, DCOLS), F32),
                ((PLANES + 8, DCOLS), F32),
            ],
            [got, rim_map, near_map, rim_keep, deck, back_state],
            scratch=[pltpu.VMEM((MEMBERS, PACKED), F32)],
            name="rim",
        )
        row_first = lax.ppermute(row_first, everyone, pairs(1, 1, True))
        row_second = lax.ppermute(row_second, everyone, pairs(1, 0, True))
        column_first = lax.ppermute(column_first, everyone, pairs(across_y, 1))
        column_second = lax.ppermute(column_second, everyone, pairs(across_y, 0))
        if section == 0:
            back_state, fill_map, keep = call(
                first_fill_kernel,
                [((ROWS, PLANES, COLS), F32), ((SLOTS, ROWS * COLS), BF16), ((ROWS, 8, COLS), F32)],
                [got_pieces, placing, back_state],
                name="fill",
            )
            base = [deck, back_state]
        else:
            (back_state,) = call(
                fill_kernel,
                [((ROWS, PLANES, COLS), F32)],
                [got_pieces, fill_map, keep, back_state],
                name="fill",
            )
        ins = [deck, back_state, column_first, column_second, row_first, row_second, metrics, keep]
        if section > 0:
            ins += base
        kernel = functools.partial(section_kernel, section)
        if section < 2:
            deck, back_state, answers = call(
                kernel,
                [
                    ((DROWS, PLANES, DCOLS), F32),
                    ((ROWS, PLANES, COLS), F32),
                    ((MEMBERS, 1, PACKED), F32),
                ],
                ins + [far, near],
                scratch=pieces,
                name="section",
            )
        else:
            deck, back_state = call(
                kernel,
                [((PLANES, DROWS, DCOLS), F32), ((PLANES, ROWS, COLS), F32)],
                ins,
                scratch=[
                    pltpu.VMEM((DROWS, PLANES, DCOLS), F32),
                    pltpu.VMEM((ROWS, PLANES, COLS), F32),
                    pltpu.SemaphoreType.DMA((DROWS,)),
                    pltpu.SemaphoreType.DMA((ROWS,)),
                ],
                outs_in=pl.ANY,
                name="section",
            )
    return deck.reshape(deck_fields.shape), back_state.reshape(back_fields.shape)


def solution(mesh):
    return jax.shard_map(
        local,
        mesh=mesh,
        in_specs=(
            P(None, None, ("grid", "gx", "gy"), None),
            P(None, None, ("grid", "gx"), "gy"),
            P(None, ("grid", "gx", "gy"), None),
            P(("grid", "gx", "gy"), None, None),
            P(("grid", "gx", "gy"), None, None),
            P(("grid", "gx", "gy"), None),
        ),
        out_specs=(P(None, None, ("grid", "gx", "gy"), None), P(None, None, ("grid", "gx"), "gy")),
        check_vma=False,
    )
```

```python
import functools

import jax
import jax.numpy as jnp
from jax import lax
from jax.experimental import pallas as pl
from jax.experimental.pallas import tpu as pltpu
from jax.sharding import PartitionSpec as P

SPAN = 32
PLANES = 96
MEMBERS = 64
CAP = 16
SLOTS = MEMBERS * CAP
ROWS = 16
COLS = 128
DROWS = 2
DCOLS = 384
FRINGE = 512
NEAR = 4
TIME_STEP = 0.05
SMAGORINSKY = 0.02
F32 = jnp.float32
BF16 = jnp.bfloat16
NT = (((1,), (1,)), ((), ()))
NN = (((1,), (0,)), ((), ()))
VMEM_LIMIT = 24 * 1024 * 1024
PACKED = CAP * PLANES
R_ROW, R_COL, R_FX, R_FY, R_GRID = range(5)


def position():
    column = lax.axis_index("gy")
    line = lax.axis_index("grid") * lax.axis_size("gx") + lax.axis_index("gx")
    tile = line * lax.axis_size("gy") + column
    return column, line, tile


def dot(a, b, dims):
    return lax.dot_general(a, b, dims, preferred_element_type=F32)


def iota(shape, dim):
    return lax.broadcasted_iota(jnp.int32, shape, dim)


def call(kernel, outs, ins, scratch=(), hbm_at=(), outs_in=pltpu.VMEM, name=None):
    def spec(i):
        return pl.BlockSpec(memory_space=pltpu.HBM if i in hbm_at else pltpu.VMEM)

    ins = [pltpu.with_memory_space_constraint(x, pltpu.HBM) if i in hbm_at else x for i, x in enumerate(ins)]
    return pl.pallas_call(
        kernel,
        out_shape=tuple(jax.ShapeDtypeStruct(s, d) for s, d in outs),
        in_specs=[spec(i) for i in range(len(ins))],
        out_specs=tuple(pl.BlockSpec(memory_space=outs_in) for _ in outs),
        scratch_shapes=list(scratch),
        compiler_params=pltpu.CompilerParams(vmem_limit_bytes=VMEM_LIMIT),
        name=name,
    )(*ins)


def route_kernel(
    donors_hbm, stencil_hbm, cells_hbm, request_ref, local_ref, rim_ref, near_ref, keep_ref,
    donors_ref, stencil_ref, cells_ref, sems,
):
    pairs = [(donors_hbm, donors_ref), (stencil_hbm, stencil_ref), (cells_hbm, cells_ref)]
    copies = [pltpu.make_async_copy(a, b, sems.at[i]) for i, (a, b) in enumerate(pairs)]
    for c in copies:
        c.start()
    for c in copies:
        c.wait()
    donors = donors_ref[...]
    donors = (donors & 7) * 8 + (donors >> 3)
    member = (iota((MEMBERS, FRINGE), 0) == donors).astype(F32)
    before = (iota((FRINGE, FRINGE), 0) < iota((FRINGE, FRINGE), 1)).astype(BF16)
    member_b = member.astype(BF16)
    earlier = dot(member_b, before, NN)
    rank = jnp.sum(member * earlier, axis=0, keepdims=True).astype(jnp.int32)
    at_rank = (iota((CAP, FRINGE), 0) == rank).astype(F32)

    def place(values):
        stacked = jnp.concatenate([at_rank * v.astype(F32) for v in values], axis=0)
        return dot(member_b, stacked.astype(BF16), NT)

    row = stencil_ref[0:1, :]
    col = stencil_ref[1:2, :]
    lane = iota((1, FRINGE), 1)
    grid = jnp.where(lane < NEAR, 1, 2)
    half = col >> 1
    sent = place([row, half, col - 2 * half, stencil_ref[2:3, :], stencil_ref[3:4, :], grid])
    request_ref[:, 0, :] = jnp.zeros((MEMBERS, 128), F32)
    request_ref[:, 0, 0:16] = sent[:, 0:16]
    request_ref[:, 0, 16:32] = 2.0 * sent[:, 16:32] + sent[:, 32:48]
    request_ref[:, 0, 32:80] = sent[:, 48:96]
    cells = jnp.concatenate([jnp.zeros((1, NEAR), jnp.int32), cells_ref[...]], axis=1)
    far = lane >= NEAR
    local_ref[...] = place(
        [
            jnp.where(far, (cells >> 7) + 1, 0),
            jnp.where(far, cells & 127, 0),
            jnp.where(far, 0, lane + 1),
        ]
    )
    landing(local_ref, rim_ref, near_ref, keep_ref)


def over_eight(x):
    return jnp.sum(x.reshape(MEMBERS // 8, 8, COLS), axis=0)


def kept(listed):
    return 1.0 - jnp.broadcast_to(jnp.sum(listed, axis=0, keepdims=True), (8, COLS))


def landing(local_ref, rim_ref, near_ref, keep_ref):
    lane = iota((MEMBERS, COLS), 1)
    places = local_ref[...].astype(jnp.int32)
    listed = [jnp.zeros((8, COLS), F32) for _ in range(3)]

    for s in range(CAP):
        at = slice(s * MEMBERS, (s + 1) * MEMBERS)
        row = jnp.broadcast_to(places[:, s : s + 1] - 1, (MEMBERS, COLS))
        col = jnp.broadcast_to(places[:, CAP + s : CAP + s + 1], (MEMBERS, COLS))
        hit = jnp.where(lane == col, 1.0, 0.0)
        for i, r in enumerate((0, ROWS - 1)):
            here = jnp.where(row == r, hit, 0.0)
            rim_ref[at, i * COLS : (i + 1) * COLS] = here.astype(BF16)
            listed[i] = listed[i] + over_eight(here)
        side = jnp.where(col == 0, row, jnp.where(col == COLS - 1, row + ROWS, -1))
        here = jnp.where((lane == side) & (row >= 0), 1.0, 0.0)
        rim_ref[at, 2 * COLS : 3 * COLS] = here.astype(BF16)
        listed[2] = listed[2] + over_eight(here)
        if s < NEAR:
            near = places[:, 2 * CAP + s : 2 * CAP + s + 1] - 1
            place = jnp.where(near >= 0, (near >> 1) * COLS + COLS - 2 + (near & 1), -1)
            place = jnp.broadcast_to(place, (MEMBERS, COLS))
            for r in range(DROWS):
                near_ref[at, r * COLS : (r + 1) * COLS] = jnp.where(lane + r * COLS == place, 1.0, 0.0).astype(BF16)
    for i in range(3):
        keep_ref[i] = kept(listed[i])


def split(x):
    high = x.astype(BF16)
    return high, (x - high.astype(F32)).astype(BF16)


def weights(request_ref, rows_ref, far_ref, near_ref):
    rows_ref[...] = request_ref[:, 0, :]
    request = rows_ref[...]
    whole = request.astype(jnp.int32)
    lane = iota((MEMBERS, COLS), 1)

    def wide(x, f, s):
        at = f * CAP + s
        return jnp.broadcast_to(x[:, at : at + 1], (MEMBERS, COLS))

    for s in range(CAP):
        at = slice(s * MEMBERS, (s + 1) * MEMBERS)
        col = wide(whole, R_COL, s)
        fx = wide(request, R_FX, s) * (1.0 / 16.0)
        fy = wide(request, R_FY, s) * (1.0 / 16.0)
        grid = wide(request, R_GRID, s)
        on_deck = jnp.where(grid == 2.0, 1.0, 0.0)
        first, second = on_deck * (1.0 - fx), on_deck * fx
        share = [first * (1.0 - fy), first * fy, second * (1.0 - fy), second * fy]
        for t in range(DCOLS // COLS):
            low, high = lane + t * COLS == col, lane + t * COLS == col + 1
            for r in range(DROWS):
                here = jnp.where(low, share[2 * r], jnp.where(high, share[2 * r + 1], 0.0))
                start = r * DCOLS + t * COLS
                far_ref[at, start : start + COLS] = here.astype(BF16)
        if s < NEAR:
            row = wide(whole, R_ROW, s)
            on_back = jnp.where(grid == 1.0, 1.0, 0.0)
            across = jnp.where(lane == col, on_back * (1.0 - fy), jnp.where(lane == col + 1, on_back * fy, 0.0))
            first, second = (1.0 - fx) * across, fx * across
            for r in range(ROWS):
                here = jnp.where(row == r, first, jnp.where(row + 1 == r, second, 0.0))
                near_ref[at, r * COLS : (r + 1) * COLS] = here.astype(BF16)


def stack_deck(pieces, r, value):
    high, low = split(value)
    pieces[0:PLANES, r * DCOLS : (r + 1) * DCOLS] = high
    pieces[128 : 128 + PLANES, r * DCOLS : (r + 1) * DCOLS] = low


def stack_back(pieces, r, value):
    high, low = split(value)
    pieces[0:PLANES, r * COLS : (r + 1) * COLS] = high
    pieces[128 : 128 + PLANES, r * COLS : (r + 1) * COLS] = low


def clear_pieces(deck_pieces, back_pieces):
    for pieces in (deck_pieces, back_pieces):
        gap = jnp.zeros((128 - PLANES, pieces.shape[1]), BF16)
        pieces[PLANES:128, :] = gap
        pieces[128 + PLANES : 256, :] = gap


def answer(far_ref, near_ref, deck_pieces, back_pieces, out_ref):
    lane = iota((MEMBERS, 128), 1)
    for q in range(CAP // 4):
        got = dot(far_ref[q * 256 : (q + 1) * 256, :], deck_pieces[...], NT)
        if q == 0:
            got = got + dot(near_ref[...], back_pieces[...], NT)
        got = got[:, 0:128] + got[:, 128:256]
        a = [got[i * MEMBERS : (i + 1) * MEMBERS, :] for i in range(4)]
        base = q * 4 * PLANES
        out_ref[:, 0, base : base + 128] = jnp.where(lane < 96, a[0], pltpu.roll(a[1], 96, 1))
        out_ref[:, 0, base + 128 : base + 256] = jnp.where(
            lane < 64, pltpu.roll(a[1], 96, 1), pltpu.roll(a[2], 64, 1)
        )
        out_ref[:, 0, base + 256 : base + 384] = jnp.where(
            lane < 32, pltpu.roll(a[2], 64, 1), pltpu.roll(a[3], 32, 1)
        )


def first_answer_kernel(
    request_ref, deck_hbm, back_hbm, deck_out, back_out, far_ref, near_ref, out_ref,
    rows_ref, deck_pieces, back_pieces, deck_sems, back_sems,
):
    copies = [
        pltpu.make_async_copy(deck_hbm.at[:, r, :], deck_out.at[r], deck_sems.at[r]) for r in range(DROWS)
    ] + [pltpu.make_async_copy(back_hbm.at[:, r, :], back_out.at[r], back_sems.at[r]) for r in range(ROWS)]
    for c in copies:
        c.start()
    clear_pieces(deck_pieces, back_pieces)
    weights(request_ref, rows_ref, far_ref, near_ref)
    for c in copies:
        c.wait()
    for r in range(DROWS):
        stack_deck(deck_pieces, r, deck_out[r])
    for r in range(ROWS):
        stack_back(back_pieces, r, back_out[r])
    answer(far_ref, near_ref, deck_pieces, back_pieces, out_ref)


def rim_kernel(
    got_ref, rim_ref, near_ref, keep_ref, deck_ref, back_ref,
    got_pieces, deck_out, column_first, column_second, row_first, row_second, plain_ref,
):
    plain_ref[...] = got_ref[:, 0, :]
    lane = iota((MEMBERS, 128), 1)
    for q in range(CAP // 4):
        base = q * 4 * PLANES
        c0 = plain_ref[:, base : base + 128]
        c1 = plain_ref[:, base + 128 : base + 256]
        c2 = plain_ref[:, base + 256 : base + 384]
        a0 = jnp.where(lane < 96, c0, 0.0)
        a1 = jnp.where(lane < 32, pltpu.roll(c0, 32, 1), jnp.where(lane < 96, pltpu.roll(c1, 32, 1), 0.0))
        a2 = jnp.where(lane < 64, pltpu.roll(c1, 64, 1), jnp.where(lane < 96, pltpu.roll(c2, 64, 1), 0.0))
        a3 = jnp.where(lane < 96, pltpu.roll(c2, 96, 1), 0.0)
        across = jnp.concatenate([a0, a1, a2, a3], axis=0).T
        high, low = split(across[0:PLANES, :])
        got_pieces[0:PLANES, q * 256 : (q + 1) * 256] = high
        got_pieces[PLANES : 2 * PLANES, q * 256 : (q + 1) * 256] = low
    near = dot(got_pieces[:, 0:256], near_ref[...], NN)
    near = near[0:PLANES] + near[PLANES : 2 * PLANES]
    lane = iota((PLANES, 128), 1)
    column, line, tile = position()
    odd = lax.rem(tile, 2) == 0
    odd_line = lax.rem(line, 2) == 0
    deck = []
    for r in range(DROWS):
        outer = jnp.where(lane >= 126, near[:, r * 128 : (r + 1) * 128], deck_ref[r, :, 256:384])
        deck.append(jnp.concatenate([deck_ref[r, :, 0:256], outer], axis=1))
        deck_out[r] = deck[r]
    row_first[0:PLANES, :] = jnp.where(odd, deck[0], deck[1])
    row_second[0:PLANES, :] = jnp.where(odd, deck[1], deck[0])
    rim = dot(got_pieces[...], rim_ref[...], NN)
    rim = rim[0:PLANES] + rim[PLANES : 2 * PLANES]
    north = back_ref[0] * keep_ref[0, 0:1, :] + rim[:, 0:COLS]
    south = back_ref[ROWS - 1] * keep_ref[1, 0:1, :] + rim[:, COLS : 2 * COLS]
    column_first[...] = jnp.where(odd_line, north, south)
    column_second[...] = jnp.where(odd_line, south, north)
    ends = jnp.zeros((PLANES, COLS), F32)
    for r in range(ROWS):
        ends = jnp.where(lane == r, back_ref[r, :, 0:1], ends)
        ends = jnp.where(lane == ROWS + r, back_ref[r, :, COLS - 1 : COLS], ends)
    ends = ends * keep_ref[2, 0:1, :] + rim[:, 2 * COLS : 3 * COLS]
    ends = jnp.concatenate([ends, jnp.zeros((COLS - PLANES, COLS), F32)], axis=0).T
    parts = [ends[i * 8 : (i + 1) * 8, :] for i in range(4)]
    for side, flag in ((row_first, odd), (row_second, jnp.logical_not(odd))):
        for i in range(2):
            side[PLANES : PLANES + 8, i * COLS : (i + 1) * COLS] = jnp.where(flag, parts[i], parts[2 + i])
        side[PLANES : PLANES + 8, 2 * COLS : 3 * COLS] = jnp.zeros((8, COLS), F32)


def fill_rows(got_pieces, fill_ref, keep_ref, back_ref, back_out):
    for c in range(ROWS // 2):
        new = dot(got_pieces[...], fill_ref[:, c * 256 : (c + 1) * 256], NN)
        new = new[0:PLANES] + new[PLANES : 2 * PLANES]
        for half in range(2):
            r = 2 * c + half
            back_out[r] = back_ref[r] * keep_ref[r, 0:1, :] + new[:, half * 128 : (half + 1) * 128]


def fill_kernel(section, got_pieces, fill_ref, keep_ref, back_ref, base_ref, back_out, *inner):
    fill_rows(got_pieces, fill_ref, keep_ref, back_ref, back_out)
    inner_rows(section, back_out, keep_ref, base_ref, *inner)


def first_fill_kernel(got_pieces, local_ref, back_ref, back_out, fill_ref, keep_ref, *inner):
    lane = iota((MEMBERS, COLS), 1)
    places = local_ref[...].astype(jnp.int32)
    listed = [jnp.zeros((8, COLS), F32) for _ in range(ROWS)]
    for s in range(CAP):
        at = slice(s * MEMBERS, (s + 1) * MEMBERS)
        row = jnp.broadcast_to(places[:, s : s + 1] - 1, (MEMBERS, COLS))
        col = jnp.broadcast_to(places[:, CAP + s : CAP + s + 1], (MEMBERS, COLS))
        hit = jnp.where(lane == col, 1.0, 0.0)
        for r in range(ROWS):
            here = jnp.where(row == r, hit, 0.0)
            fill_ref[at, r * COLS : (r + 1) * COLS] = here.astype(BF16)
            listed[r] = listed[r] + over_eight(here)
    for r in range(ROWS):
        keep_ref[r] = kept(listed[r])
    fill_rows(got_pieces, fill_ref, keep_ref, back_ref, back_out)
    inner_rows(0, back_out, keep_ref, None, *inner)


def deck_update(here, minus_xi, plus_xi, minus_eta, plus_eta, metric, keep, base, section):
    weight = (1.0, 0.25, 2.0 / 3.0)[section]
    step = (weight * TIME_STEP) * keep
    d_xi, d_eta, d_span, lap = [], [], [], []
    strain = None
    for c in range(3):
        f = here[c]
        plus_span = pltpu.roll(f, SPAN - 1, 0)
        minus_span = pltpu.roll(f, 1, 0)
        a = plus_xi[c] - minus_xi[c]
        b = plus_eta[c] - minus_eta[c]
        s = plus_span - minus_span
        square = a * a + b * b + s * s
        strain = square if strain is None else strain + square
        doubled = 2.0 * f
        l_xi = plus_xi[c] - doubled + minus_xi[c]
        l_eta = plus_eta[c] - doubled + minus_eta[c]
        lap.append(metric[4] * l_xi + metric[5] * l_eta + (plus_span - doubled + minus_span))
        d_xi.append(a)
        d_eta.append(b)
        d_span.append(s)
    stretched = 1.0 + 0.25 * strain
    viscosity = (SMAGORINSKY * step) * (stretched * lax.rsqrt(stretched))
    half = 0.5 * step
    speed_xi = half * (metric[0] * here[0] + metric[1] * here[1])
    speed_eta = half * (metric[2] * here[0] + metric[3] * here[1])
    speed_span = half * here[2]
    out = []
    for c in range(3):
        change = viscosity * lap[c] - (speed_xi * d_xi[c] + speed_eta * d_eta[c] + speed_span * d_span[c])
        if section == 0:
            out.append(here[c] + change)
        elif section == 1:
            out.append(0.75 * base[c] + (0.25 * here[c] + change))
        else:
            out.append(base[c] * (1.0 / 3.0) + ((2.0 / 3.0) * here[c] + change))
    return out


def inner_part(here, minus_xi, plus_xi, keep, base, section):
    weight = (1.0, 0.25, 2.0 / 3.0)[section]
    half = (0.5 * weight * TIME_STEP) * keep
    speed_xi, speed_span = half * here[0], half * here[2]
    strain, lap, rest = None, [], []
    for c in range(3):
        f = here[c]
        plus_span = pltpu.roll(f, SPAN - 1, 0)
        minus_span = pltpu.roll(f, 1, 0)
        a = plus_xi[c] - minus_xi[c]
        s = plus_span - minus_span
        square = a * a + s * s
        strain = square if strain is None else strain + square
        lap.append((plus_xi[c] + minus_xi[c]) + (plus_span + minus_span) - 6.0 * f)
        advection = speed_xi * a + speed_span * s
        if section == 0:
            rest.append(f - advection)
        elif section == 1:
            rest.append(0.75 * base[c] + (0.25 * f - advection))
        else:
            rest.append(base[c] * (1.0 / 3.0) + ((2.0 / 3.0) * f - advection))
    return strain, lap, rest


def outer_part(here, minus_eta, plus_eta, part, keep, section):
    strain, lap, rest = part
    step = ((1.0, 0.25, 2.0 / 3.0)[section] * TIME_STEP) * keep
    b = [plus_eta[c] - minus_eta[c] for c in range(3)]
    strain = strain + (b[0] * b[0] + b[1] * b[1] + b[2] * b[2])
    stretched = 1.0 + 0.25 * strain
    viscosity = (SMAGORINSKY * step) * (stretched * lax.rsqrt(stretched))
    speed_eta = (0.5 * step) * here[1]
    return [
        rest[c] + (viscosity * (lap[c] + (plus_eta[c] + minus_eta[c])) - speed_eta * b[c])
        for c in range(3)
    ]


def inner_rows(section, back_ref, keep_ref, base_ref, strain_out, lap_out, rest_out):
    for r in range(1, ROWS - 1):
        strain, lap, rest = inner_part(
            fields(back_ref, (r,)),
            fields(back_ref, (r - 1,)),
            fields(back_ref, (r + 1,)),
            keep_ref[r, 0:1, :],
            None if base_ref is None else fields(base_ref, (r,)),
            section,
        )
        strain_out[r - 1] = strain
        for c in range(3):
            lap_out[r - 1, c * SPAN : (c + 1) * SPAN, :] = lap[c]
            rest_out[r - 1, c * SPAN : (c + 1) * SPAN, :] = rest[c]


def fields(ref, at):
    return [ref[at + (slice(c * SPAN, (c + 1) * SPAN), slice(None))] for c in range(3)]


def section_kernel(section, *refs):
    refs = list(refs)
    deck_ref, back_ref, column_first, column_second, row_first, row_second, metric_ref, keep_ref = refs[:8]
    strain_ref, lap_ref, rest_ref = refs[8:11]
    del refs[:11]
    base_deck = base_back = None
    if section > 0:
        base_deck, base_back = refs[:2]
        del refs[:2]
    last = section == 2
    if last:
        deck_hbm, back_hbm, deck_out, back_out, deck_sems, back_sems = refs
        copies = []

        def send(rows, r, whole, sems):
            copies.append(pltpu.make_async_copy(rows.at[r], whole.at[:, r, :], sems.at[r]))
            copies[-1].start()

    else:
        far_ref, near_ref, deck_out, back_out, answer_out, deck_pieces, back_pieces = refs
        clear_pieces(deck_pieces, back_pieces)
    column, line, tile = position()
    odd = lax.rem(tile, 2) == 0
    odd_line = lax.rem(line, 2) == 0
    west_end = (column > 0).astype(F32)
    east_end = (column < lax.axis_size("gy") - 1).astype(F32)

    def ordered(flag, first, second, at):
        a, b = first[at], second[at]
        return jnp.where(flag, a, b), jnp.where(flag, b, a)

    spans = [slice(c * SPAN, (c + 1) * SPAN) for c in range(3)]
    across = [ordered(odd, row_first, row_second, (at, slice(None))) for at in spans]
    beside = []
    halves = [
        ordered(odd, row_first, row_second, (slice(PLANES, PLANES + 8), slice(i * COLS, (i + 1) * COLS)))
        for i in range(2)
    ]
    for side in range(2):
        cells = jnp.concatenate([halves[0][side], halves[1][side], jnp.zeros((COLS - 16, COLS), F32)], axis=0)
        beside.append(cells.T)
    north_end = (line > 0).astype(F32)
    south_end = (line < lax.axis_size("grid") * lax.axis_size("gx") - 1).astype(F32)
    along = [ordered(odd_line, column_first, column_second, (at, slice(None))) for at in spans]
    along = [(before * north_end, after * south_end) for before, after in along]
    lane = iota((SPAN, DCOLS), 1)
    keep_deck = jnp.where(iota((1, DCOLS), 1) < DCOLS - 2, 1.0, 0.0)
    for r in range(DROWS):
        here = fields(deck_ref, (r,))
        if r == 0:
            minus = [a[0] for a in across]
            plus = fields(deck_ref, (1,))
        else:
            minus = fields(deck_ref, (0,))
            plus = [a[1] for a in across]
        m = [metric_ref[i, r : r + 1, :] for i in range(4)]
        metric = m + [m[0] * m[0] + m[1] * m[1], m[2] * m[2] + m[3] * m[3]]
        plus_eta = [jnp.where(lane == DCOLS - 1, 0.0, pltpu.roll(f, DCOLS - 1, 1)) for f in here]
        minus_eta = [jnp.where(lane == 0, 0.0, pltpu.roll(f, 1, 1)) for f in here]
        base = fields(base_deck, (r,)) if section > 0 else None
        new = deck_update(here, minus, plus, minus_eta, plus_eta, metric, keep_deck, base, section)
        for c in range(3):
            deck_out[r, c * SPAN : (c + 1) * SPAN, :] = new[c]
        if last:
            send(deck_out, r, deck_hbm, deck_sems)
        else:
            stack_deck(deck_pieces, r, jnp.concatenate(new, axis=0))
    lane = iota((SPAN, COLS), 1)
    for r in range(ROWS):
        here = fields(back_ref, (r,))
        plus_eta, minus_eta = [], []
        for c in range(3):
            from_west = beside[0][spans[c], r : r + 1] * west_end
            from_east = beside[1][spans[c], r : r + 1] * east_end
            plus_eta.append(jnp.where(lane == COLS - 1, from_east, pltpu.roll(here[c], COLS - 1, 1)))
            minus_eta.append(jnp.where(lane == 0, from_west, pltpu.roll(here[c], 1, 1)))
        keep = keep_ref[r, 0:1, :]
        if 0 < r < ROWS - 1:
            part = strain_ref[r - 1], fields(lap_ref, (r - 1,)), fields(rest_ref, (r - 1,))
        else:
            minus = fields(back_ref, (r - 1,)) if r > 0 else [a[0] for a in along]
            plus = fields(back_ref, (r + 1,)) if r < ROWS - 1 else [a[1] for a in along]
            base = fields(base_back, (r,)) if section > 0 else None
            part = inner_part(here, minus, plus, keep, base, section)
        new = outer_part(here, minus_eta, plus_eta, part, keep, section)
        for c in range(3):
            back_out[r, c * SPAN : (c + 1) * SPAN, :] = new[c]
        if last:
            send(back_out, r, back_hbm, back_sems)
        else:
            stack_back(back_pieces, r, jnp.concatenate(new, axis=0))
    if last:
        for c in copies:
            c.wait()
    else:
        answer(far_ref, near_ref, deck_pieces, back_pieces, answer_out)


def local(deck_fields, back_fields, metrics, donors, stencil, fringe_cells):
    group = ("gy", "gx")
    everyone = ("grid", "gx", "gy")

    def exchange(x):
        return lax.all_to_all(x, group, split_axis=0, concat_axis=0, tiled=True)

    count = lax.axis_size("grid") * lax.axis_size("gx") * lax.axis_size("gy")
    across_y = lax.axis_size("gy")

    def pairs(step, first, periodic=False):
        out = []
        for t in range(count):
            if (t // step) % 2 == first:
                other = (t + step) % count
                if periodic or t + step < count:
                    out += [(t, other), (other, t)]
                else:
                    out += [(t, t ^ 2), (other, other ^ 2)]
        return out

    deck_in = deck_fields.reshape(PLANES, DROWS, DCOLS)
    back_in = back_fields.reshape(PLANES, ROWS, COLS)
    request, placing, rim_map, near_map, rim_keep = call(
        route_kernel,
        [
            ((MEMBERS, 1, 128), F32),
            ((MEMBERS, 3 * CAP), F32),
            ((SLOTS, 3 * COLS), BF16),
            ((NEAR * MEMBERS, 2 * COLS), BF16),
            ((3, 8, COLS), F32),
        ],
        [donors.reshape(1, FRINGE), stencil.reshape(FRINGE, 4).T, fringe_cells],
        scratch=[
            pltpu.VMEM((1, FRINGE), jnp.int32),
            pltpu.VMEM((4, FRINGE), jnp.int32),
            pltpu.VMEM((1, FRINGE - NEAR), jnp.int32),
            pltpu.SemaphoreType.DMA((3,)),
        ],
        hbm_at=(0, 1, 2),
        name="route",
    )
    request = exchange(request)
    pieces = [pltpu.VMEM((256, DROWS * DCOLS), BF16), pltpu.VMEM((256, ROWS * COLS), BF16)]
    deck, back_state, far, near, answers = call(
        first_answer_kernel,
        [
            ((DROWS, PLANES, DCOLS), F32),
            ((ROWS, PLANES, COLS), F32),
            ((SLOTS, DROWS * DCOLS), BF16),
            ((NEAR * MEMBERS, ROWS * COLS), BF16),
            ((MEMBERS, 1, PACKED), F32),
        ],
        [request, deck_in, back_in],
        scratch=[pltpu.VMEM((MEMBERS, 128), F32)]
        + pieces
        + [
            pltpu.SemaphoreType.DMA((DROWS,)),
            pltpu.SemaphoreType.DMA((ROWS,)),
        ],
        hbm_at=(1, 2),
        name="first_answer",
    )
    base = None
    for section in range(3):
        got = exchange(answers)
        got_pieces, deck, column_first, column_second, row_first, row_second = call(
            rim_kernel,
            [
                ((2 * PLANES, SLOTS), BF16),
                ((DROWS, PLANES, DCOLS), F32),
                ((PLANES, COLS), F32),
                ((PLANES, COLS), F32),
                ((PLANES + 8, DCOLS), F32),
                ((PLANES + 8, DCOLS), F32),
            ],
            [got, rim_map, near_map, rim_keep, deck, back_state],
            scratch=[pltpu.VMEM((MEMBERS, PACKED), F32)],
            name="rim",
        )
        row_first = lax.ppermute(row_first, everyone, pairs(1, 1, True))
        row_second = lax.ppermute(row_second, everyone, pairs(1, 0, True))
        column_first = lax.ppermute(column_first, everyone, pairs(across_y, 1))
        column_second = lax.ppermute(column_second, everyone, pairs(across_y, 0))
        inner = [
            ((ROWS - 2, SPAN, COLS), F32),
            ((ROWS - 2, PLANES, COLS), F32),
            ((ROWS - 2, PLANES, COLS), F32),
        ]
        if section == 0:
            back_state, fill_map, keep, *inner = call(
                first_fill_kernel,
                [((ROWS, PLANES, COLS), F32), ((SLOTS, ROWS * COLS), BF16), ((ROWS, 8, COLS), F32)] + inner,
                [got_pieces, placing, back_state],
                name="fill",
            )
            base = [deck, back_state]
        else:
            back_state, *inner = call(
                functools.partial(fill_kernel, section),
                [((ROWS, PLANES, COLS), F32)] + inner,
                [got_pieces, fill_map, keep, back_state, base[1]],
                name="fill",
            )
        ins = [deck, back_state, column_first, column_second, row_first, row_second, metrics, keep] + inner
        if section > 0:
            ins += base
        kernel = functools.partial(section_kernel, section)
        if section < 2:
            deck, back_state, answers = call(
                kernel,
                [
                    ((DROWS, PLANES, DCOLS), F32),
                    ((ROWS, PLANES, COLS), F32),
                    ((MEMBERS, 1, PACKED), F32),
                ],
                ins + [far, near],
                scratch=pieces,
                name="section",
            )
        else:
            deck, back_state = call(
                kernel,
                [((PLANES, DROWS, DCOLS), F32), ((PLANES, ROWS, COLS), F32)],
                ins,
                scratch=[
                    pltpu.VMEM((DROWS, PLANES, DCOLS), F32),
                    pltpu.VMEM((ROWS, PLANES, COLS), F32),
                    pltpu.SemaphoreType.DMA((DROWS,)),
                    pltpu.SemaphoreType.DMA((ROWS,)),
                ],
                outs_in=pl.ANY,
                name="section",
            )
    return deck.reshape(deck_fields.shape), back_state.reshape(back_fields.shape)


def solution(mesh):
    return jax.shard_map(
        local,
        mesh=mesh,
        in_specs=(
            P(None, None, ("grid", "gx", "gy"), None),
            P(None, None, ("grid", "gx"), "gy"),
            P(None, ("grid", "gx", "gy"), None),
            P(("grid", "gx", "gy"), None, None),
            P(("grid", "gx", "gy"), None, None),
            P(("grid", "gx", "gy"), None),
        ),
        out_specs=(P(None, None, ("grid", "gx", "gy"), None), P(None, None, ("grid", "gx"), "gy")),
        check_vma=False,
    )
```

```python
import functools

import jax
import jax.numpy as jnp
from jax import lax
from jax.experimental import pallas as pl
from jax.experimental.pallas import tpu as pltpu
from jax.sharding import PartitionSpec as P

SPAN = 32
PLANES = 96
MEMBERS = 64
CAP = 16
SLOTS = MEMBERS * CAP
ROWS = 16
COLS = 128
DROWS = 2
DCOLS = 384
FRINGE = 512
NEAR = 4
TIME_STEP = 0.05
SMAGORINSKY = 0.02
WEIGHTS = (1.0, 0.25, 2.0 / 3.0)
F32 = jnp.float32
BF16 = jnp.bfloat16
NT = (((1,), (1,)), ((), ()))
NN = (((1,), (0,)), ((), ()))
VMEM_LIMIT = 24 * 1024 * 1024
PACKED = CAP * PLANES
R_ROW, R_COL, R_FX, R_FY, R_GRID = range(5)


def position():
    column = lax.axis_index("gy")
    line = lax.axis_index("grid") * lax.axis_size("gx") + lax.axis_index("gx")
    tile = line * lax.axis_size("gy") + column
    return column, line, tile


def dot(a, b, dims):
    return lax.dot_general(a, b, dims, preferred_element_type=F32)


def iota(shape, dim):
    return lax.broadcasted_iota(jnp.int32, shape, dim)


def call(kernel, outs, ins, scratch=(), hbm_at=(), outs_in=pltpu.VMEM, name=None):
    def spec(i):
        return pl.BlockSpec(memory_space=pltpu.HBM if i in hbm_at else pltpu.VMEM)

    ins = [pltpu.with_memory_space_constraint(x, pltpu.HBM) if i in hbm_at else x for i, x in enumerate(ins)]
    return pl.pallas_call(
        kernel,
        out_shape=tuple(jax.ShapeDtypeStruct(s, d) for s, d in outs),
        in_specs=[spec(i) for i in range(len(ins))],
        out_specs=tuple(pl.BlockSpec(memory_space=outs_in) for _ in outs),
        scratch_shapes=list(scratch),
        compiler_params=pltpu.CompilerParams(vmem_limit_bytes=VMEM_LIMIT),
        name=name,
    )(*ins)


def route_kernel(
    donors_hbm, stencil_hbm, cells_hbm, request_ref, local_ref, rim_ref, near_ref, keep_ref,
    donors_ref, stencil_ref, cells_ref, sems,
):
    pairs = [(donors_hbm, donors_ref), (stencil_hbm, stencil_ref), (cells_hbm, cells_ref)]
    copies = [pltpu.make_async_copy(a, b, sems.at[i]) for i, (a, b) in enumerate(pairs)]
    for c in copies:
        c.start()
    for c in copies:
        c.wait()
    donors = donors_ref[...]
    donors = (donors & 7) * 8 + (donors >> 3)
    member = (iota((MEMBERS, FRINGE), 0) == donors).astype(F32)
    before = (iota((FRINGE, FRINGE), 0) < iota((FRINGE, FRINGE), 1)).astype(BF16)
    member_b = member.astype(BF16)
    earlier = dot(member_b, before, NN)
    rank = jnp.sum(member * earlier, axis=0, keepdims=True).astype(jnp.int32)
    at_rank = (iota((CAP, FRINGE), 0) == rank).astype(F32)

    def place(values):
        stacked = jnp.concatenate([at_rank * v.astype(F32) for v in values], axis=0)
        return dot(member_b, stacked.astype(BF16), NT)

    row = stencil_ref[0:1, :]
    col = stencil_ref[1:2, :]
    lane = iota((1, FRINGE), 1)
    grid = jnp.where(lane < NEAR, 1, 2)
    half = col >> 1
    sent = place([row, half, col - 2 * half, stencil_ref[2:3, :], stencil_ref[3:4, :], grid])
    request_ref[:, 0, :] = jnp.zeros((MEMBERS, 128), F32)
    request_ref[:, 0, 0:16] = sent[:, 0:16]
    request_ref[:, 0, 16:32] = 2.0 * sent[:, 16:32] + sent[:, 32:48]
    request_ref[:, 0, 32:80] = sent[:, 48:96]
    cells = jnp.concatenate([jnp.zeros((1, NEAR), jnp.int32), cells_ref[...]], axis=1)
    far = lane >= NEAR
    local_ref[...] = place(
        [
            jnp.where(far, (cells >> 7) + 1, 0),
            jnp.where(far, cells & 127, 0),
            jnp.where(far, 0, lane + 1),
        ]
    )
    landing(local_ref, rim_ref, near_ref, keep_ref)


def over_eight(x):
    return jnp.sum(x.reshape(MEMBERS // 8, 8, COLS), axis=0)


def kept(listed):
    return 1.0 - jnp.broadcast_to(jnp.sum(listed, axis=0, keepdims=True), (8, COLS))


def landing(local_ref, rim_ref, near_ref, keep_ref):
    lane = iota((MEMBERS, COLS), 1)
    places = local_ref[...].astype(jnp.int32)
    listed = [jnp.zeros((8, COLS), F32) for _ in range(3)]

    for s in range(CAP):
        at = slice(s * MEMBERS, (s + 1) * MEMBERS)
        row = jnp.broadcast_to(places[:, s : s + 1] - 1, (MEMBERS, COLS))
        col = jnp.broadcast_to(places[:, CAP + s : CAP + s + 1], (MEMBERS, COLS))
        hit = jnp.where(lane == col, 1.0, 0.0)
        for i, r in enumerate((0, ROWS - 1)):
            here = jnp.where(row == r, hit, 0.0)
            rim_ref[at, i * COLS : (i + 1) * COLS] = here.astype(BF16)
            listed[i] = listed[i] + over_eight(here)
        side = jnp.where(col == 0, row, jnp.where(col == COLS - 1, row + ROWS, -1))
        here = jnp.where((lane == side) & (row >= 0), 1.0, 0.0)
        rim_ref[at, 2 * COLS : 3 * COLS] = here.astype(BF16)
        listed[2] = listed[2] + over_eight(here)
        if s < NEAR:
            near = places[:, 2 * CAP + s : 2 * CAP + s + 1] - 1
            place = jnp.where(near >= 0, (near >> 1) * COLS + COLS - 2 + (near & 1), -1)
            place = jnp.broadcast_to(place, (MEMBERS, COLS))
            for r in range(DROWS):
                near_ref[at, r * COLS : (r + 1) * COLS] = jnp.where(lane + r * COLS == place, 1.0, 0.0).astype(BF16)
    for i in range(3):
        keep_ref[i] = kept(listed[i])


def split(x):
    high = x.astype(BF16)
    return high, (x - high.astype(F32)).astype(BF16)


def weights(request_ref, rows_ref, far_ref, near_ref):
    rows_ref[...] = request_ref[:, 0, :]
    request = rows_ref[...]
    whole = request.astype(jnp.int32)
    lane = iota((MEMBERS, COLS), 1)

    def wide(x, f, s):
        at = f * CAP + s
        return jnp.broadcast_to(x[:, at : at + 1], (MEMBERS, COLS))

    for s in range(CAP):
        at = slice(s * MEMBERS, (s + 1) * MEMBERS)
        col = wide(whole, R_COL, s)
        fx = wide(request, R_FX, s) * (1.0 / 16.0)
        fy = wide(request, R_FY, s) * (1.0 / 16.0)
        grid = wide(request, R_GRID, s)
        on_deck = jnp.where(grid == 2.0, 1.0, 0.0)
        first, second = on_deck * (1.0 - fx), on_deck * fx
        share = [first * (1.0 - fy), first * fy, second * (1.0 - fy), second * fy]
        for t in range(DCOLS // COLS):
            low, high = lane + t * COLS == col, lane + t * COLS == col + 1
            for r in range(DROWS):
                here = jnp.where(low, share[2 * r], jnp.where(high, share[2 * r + 1], 0.0))
                start = r * DCOLS + t * COLS
                far_ref[at, start : start + COLS] = here.astype(BF16)
        if s < NEAR:
            row = wide(whole, R_ROW, s)
            on_back = jnp.where(grid == 1.0, 1.0, 0.0)
            across = jnp.where(lane == col, on_back * (1.0 - fy), jnp.where(lane == col + 1, on_back * fy, 0.0))
            first, second = (1.0 - fx) * across, fx * across
            for r in range(ROWS):
                here = jnp.where(row == r, first, jnp.where(row + 1 == r, second, 0.0))
                near_ref[at, r * COLS : (r + 1) * COLS] = here.astype(BF16)


def stack_deck(pieces, r, value):
    high, low = split(value)
    pieces[0:PLANES, r * DCOLS : (r + 1) * DCOLS] = high
    pieces[128 : 128 + PLANES, r * DCOLS : (r + 1) * DCOLS] = low


def stack_back(pieces, r, value):
    high, low = split(value)
    pieces[0:PLANES, r * COLS : (r + 1) * COLS] = high
    pieces[128 : 128 + PLANES, r * COLS : (r + 1) * COLS] = low


def clear_pieces(deck_pieces, back_pieces):
    for pieces in (deck_pieces, back_pieces):
        gap = jnp.zeros((128 - PLANES, pieces.shape[1]), BF16)
        pieces[PLANES:128, :] = gap
        pieces[128 + PLANES : 256, :] = gap


def answer(far_ref, near_ref, deck_pieces, back_pieces, out_ref):
    lane = iota((MEMBERS, 128), 1)
    for q in range(CAP // 4):
        got = dot(far_ref[q * 256 : (q + 1) * 256, :], deck_pieces[...], NT)
        if q == 0:
            got = got + dot(near_ref[...], back_pieces[...], NT)
        got = got[:, 0:128] + got[:, 128:256]
        a = [got[i * MEMBERS : (i + 1) * MEMBERS, :] for i in range(4)]
        base = q * 4 * PLANES
        out_ref[:, 0, base : base + 128] = jnp.where(lane < 96, a[0], pltpu.roll(a[1], 96, 1))
        out_ref[:, 0, base + 128 : base + 256] = jnp.where(
            lane < 64, pltpu.roll(a[1], 96, 1), pltpu.roll(a[2], 64, 1)
        )
        out_ref[:, 0, base + 256 : base + 384] = jnp.where(
            lane < 32, pltpu.roll(a[2], 64, 1), pltpu.roll(a[3], 32, 1)
        )


def first_answer_kernel(
    request_ref, deck_hbm, back_hbm, deck_out, back_out, far_ref, near_ref, out_ref,
    rows_ref, deck_pieces, back_pieces, deck_sems, back_sems,
):
    copies = [
        pltpu.make_async_copy(deck_hbm.at[:, r, :], deck_out.at[r], deck_sems.at[r]) for r in range(DROWS)
    ] + [pltpu.make_async_copy(back_hbm.at[:, r, :], back_out.at[r], back_sems.at[r]) for r in range(ROWS)]
    for c in copies:
        c.start()
    clear_pieces(deck_pieces, back_pieces)
    weights(request_ref, rows_ref, far_ref, near_ref)
    for c in copies:
        c.wait()
    for r in range(DROWS):
        stack_deck(deck_pieces, r, deck_out[r])
    for r in range(ROWS):
        stack_back(back_pieces, r, back_out[r])
    answer(far_ref, near_ref, deck_pieces, back_pieces, out_ref)


def rim_kernel(
    got_ref, rim_ref, near_ref, keep_ref, deck_ref, back_ref,
    got_pieces, deck_out, column_first, column_second, row_first, row_second, plain_ref,
):
    plain_ref[...] = got_ref[:, 0, :]
    lane = iota((MEMBERS, 128), 1)
    for q in range(CAP // 4):
        base = q * 4 * PLANES
        c0 = plain_ref[:, base : base + 128]
        c1 = plain_ref[:, base + 128 : base + 256]
        c2 = plain_ref[:, base + 256 : base + 384]
        a0 = jnp.where(lane < 96, c0, 0.0)
        a1 = jnp.where(lane < 32, pltpu.roll(c0, 32, 1), jnp.where(lane < 96, pltpu.roll(c1, 32, 1), 0.0))
        a2 = jnp.where(lane < 64, pltpu.roll(c1, 64, 1), jnp.where(lane < 96, pltpu.roll(c2, 64, 1), 0.0))
        a3 = jnp.where(lane < 96, pltpu.roll(c2, 96, 1), 0.0)
        across = jnp.concatenate([a0, a1, a2, a3], axis=0).T
        high, low = split(across[0:PLANES, :])
        got_pieces[0:PLANES, q * 256 : (q + 1) * 256] = high
        got_pieces[PLANES : 2 * PLANES, q * 256 : (q + 1) * 256] = low
    near = dot(got_pieces[:, 0:256], near_ref[...], NN)
    near = near[0:PLANES] + near[PLANES : 2 * PLANES]
    lane = iota((PLANES, 128), 1)
    column, line, tile = position()
    odd = lax.rem(tile, 2) == 0
    odd_line = lax.rem(line, 2) == 0
    deck = []
    for r in range(DROWS):
        outer = jnp.where(lane >= 126, near[:, r * 128 : (r + 1) * 128], deck_ref[r, :, 256:384])
        deck.append(jnp.concatenate([deck_ref[r, :, 0:256], outer], axis=1))
        deck_out[r] = deck[r]
    row_first[0:PLANES, :] = jnp.where(odd, deck[0], deck[1])
    row_second[0:PLANES, :] = jnp.where(odd, deck[1], deck[0])
    rim = dot(got_pieces[...], rim_ref[...], NN)
    rim = rim[0:PLANES] + rim[PLANES : 2 * PLANES]
    north = back_ref[0] * keep_ref[0, 0:1, :] + rim[:, 0:COLS]
    south = back_ref[ROWS - 1] * keep_ref[1, 0:1, :] + rim[:, COLS : 2 * COLS]
    column_first[...] = jnp.where(odd_line, north, south)
    column_second[...] = jnp.where(odd_line, south, north)
    ends = jnp.zeros((PLANES, COLS), F32)
    for r in range(ROWS):
        ends = jnp.where(lane == r, back_ref[r, :, 0:1], ends)
        ends = jnp.where(lane == ROWS + r, back_ref[r, :, COLS - 1 : COLS], ends)
    ends = ends * keep_ref[2, 0:1, :] + rim[:, 2 * COLS : 3 * COLS]
    ends = jnp.concatenate([ends, jnp.zeros((COLS - PLANES, COLS), F32)], axis=0).T
    parts = [ends[i * 8 : (i + 1) * 8, :] for i in range(4)]
    for side, flag in ((row_first, odd), (row_second, jnp.logical_not(odd))):
        for i in range(2):
            side[PLANES : PLANES + 8, i * COLS : (i + 1) * COLS] = jnp.where(flag, parts[i], parts[2 + i])
        side[PLANES : PLANES + 8, 2 * COLS : 3 * COLS] = jnp.zeros((8, COLS), F32)


def fill_rows(got_pieces, fill_ref, keep_ref, back_ref, back_out):
    for c in range(ROWS // 2):
        new = dot(got_pieces[...], fill_ref[:, c * 256 : (c + 1) * 256], NN)
        new = new[0:PLANES] + new[PLANES : 2 * PLANES]
        for half in range(2):
            r = 2 * c + half
            back_out[r] = back_ref[r] * keep_ref[r, 0:1, :] + new[:, half * 128 : (half + 1) * 128]


def fill_kernel(
    section, got_pieces, fill_ref, keep_ref, back_ref, deck_ref, metric_ref, base_deck, base_back, back_out, *inner
):
    fill_rows(got_pieces, fill_ref, keep_ref, back_ref, back_out)
    inner_rows(section, back_out, keep_ref, base_back, *inner[:3])
    deck_inner(section, deck_ref, metric_ref, base_deck, *inner[3:])


def first_fill_kernel(
    got_pieces, local_ref, back_ref, deck_ref, metric_ref, back_out, fill_ref, keep_ref, *inner
):
    lane = iota((MEMBERS, COLS), 1)
    places = local_ref[...].astype(jnp.int32)
    listed = [jnp.zeros((8, COLS), F32) for _ in range(ROWS)]
    for s in range(CAP):
        at = slice(s * MEMBERS, (s + 1) * MEMBERS)
        row = jnp.broadcast_to(places[:, s : s + 1] - 1, (MEMBERS, COLS))
        col = jnp.broadcast_to(places[:, CAP + s : CAP + s + 1], (MEMBERS, COLS))
        hit = jnp.where(lane == col, 1.0, 0.0)
        for r in range(ROWS):
            here = jnp.where(row == r, hit, 0.0)
            fill_ref[at, r * COLS : (r + 1) * COLS] = here.astype(BF16)
            listed[r] = listed[r] + over_eight(here)
    for r in range(ROWS):
        keep_ref[r] = kept(listed[r])
    fill_rows(got_pieces, fill_ref, keep_ref, back_ref, back_out)
    inner_rows(0, back_out, keep_ref, None, *inner[:3])
    deck_inner(0, deck_ref, metric_ref, None, *inner[3:])


def deck_metric(metric_ref, r):
    return [metric_ref[i, r : r + 1, :] for i in range(4)]


def deck_keep():
    return jnp.where(iota((1, DCOLS), 1) < DCOLS - 2, 1.0, 0.0)


def deck_inner(section, deck_ref, metric_ref, base_ref, strain_out, lap_out, rest_out):
    lane = iota((SPAN, DCOLS), 1)
    half = (0.5 * WEIGHTS[section] * TIME_STEP) * deck_keep()
    for r in range(DROWS):
        here = fields(deck_ref, (r,))
        base = None if base_ref is None else fields(base_ref, (r,))
        m = deck_metric(metric_ref, r)
        g1, g2 = m[0] * m[0] + m[1] * m[1], m[2] * m[2] + m[3] * m[3]
        speed_eta, speed_span = half * (m[2] * here[0] + m[3] * here[1]), half * here[2]
        strain = None
        for c in range(3):
            f = here[c]
            plus_eta = jnp.where(lane == DCOLS - 1, 0.0, pltpu.roll(f, DCOLS - 1, 1))
            minus_eta = jnp.where(lane == 0, 0.0, pltpu.roll(f, 1, 1))
            plus_span = pltpu.roll(f, SPAN - 1, 0)
            minus_span = pltpu.roll(f, 1, 0)
            b, s = plus_eta - minus_eta, plus_span - minus_span
            square = b * b + s * s
            strain = square if strain is None else strain + square
            doubled = 2.0 * f
            at = slice(c * SPAN, (c + 1) * SPAN)
            lap_out[r, at, :] = g2 * (plus_eta - doubled + minus_eta) + (plus_span - doubled + minus_span) - g1 * doubled
            rest_out[r, at, :] = carried(section, f, base, c) - (speed_eta * b + speed_span * s)
        strain_out[r] = strain


def deck_outer(section, here, minus_xi, plus_xi, m, part):
    strain, lap, rest = part
    step = (WEIGHTS[section] * TIME_STEP) * deck_keep()
    a = [plus_xi[c] - minus_xi[c] for c in range(3)]
    strain = strain + (a[0] * a[0] + a[1] * a[1] + a[2] * a[2])
    stretched = 1.0 + 0.25 * strain
    viscosity = (SMAGORINSKY * step) * (stretched * lax.rsqrt(stretched))
    speed_xi = (0.5 * step) * (m[0] * here[0] + m[1] * here[1])
    g1 = m[0] * m[0] + m[1] * m[1]
    return [
        rest[c] + (viscosity * (lap[c] + g1 * (plus_xi[c] + minus_xi[c])) - speed_xi * a[c])
        for c in range(3)
    ]


def carried(section, f, base, c):
    if section == 0:
        return f
    if section == 1:
        return 0.75 * base[c] + 0.25 * f
    return base[c] * (1.0 / 3.0) + (2.0 / 3.0) * f


def inner_part(here, minus_xi, plus_xi, keep, base, section):
    half = (0.5 * WEIGHTS[section] * TIME_STEP) * keep
    speed_xi, speed_span = half * here[0], half * here[2]
    strain, lap, rest = None, [], []
    for c in range(3):
        f = here[c]
        plus_span = pltpu.roll(f, SPAN - 1, 0)
        minus_span = pltpu.roll(f, 1, 0)
        a = plus_xi[c] - minus_xi[c]
        s = plus_span - minus_span
        square = a * a + s * s
        strain = square if strain is None else strain + square
        lap.append((plus_xi[c] + minus_xi[c]) + (plus_span + minus_span) - 6.0 * f)
        advection = speed_xi * a + speed_span * s
        rest.append(carried(section, f, base, c) - advection)
    return strain, lap, rest


def outer_part(here, minus_eta, plus_eta, part, keep, section):
    strain, lap, rest = part
    step = (WEIGHTS[section] * TIME_STEP) * keep
    b = [plus_eta[c] - minus_eta[c] for c in range(3)]
    strain = strain + (b[0] * b[0] + b[1] * b[1] + b[2] * b[2])
    stretched = 1.0 + 0.25 * strain
    viscosity = (SMAGORINSKY * step) * (stretched * lax.rsqrt(stretched))
    speed_eta = (0.5 * step) * here[1]
    return [
        rest[c] + (viscosity * (lap[c] + (plus_eta[c] + minus_eta[c])) - speed_eta * b[c])
        for c in range(3)
    ]


def inner_rows(section, back_ref, keep_ref, base_ref, strain_out, lap_out, rest_out):
    for r in range(1, ROWS - 1):
        strain, lap, rest = inner_part(
            fields(back_ref, (r,)),
            fields(back_ref, (r - 1,)),
            fields(back_ref, (r + 1,)),
            keep_ref[r, 0:1, :],
            None if base_ref is None else fields(base_ref, (r,)),
            section,
        )
        strain_out[r - 1] = strain
        for c in range(3):
            lap_out[r - 1, c * SPAN : (c + 1) * SPAN, :] = lap[c]
            rest_out[r - 1, c * SPAN : (c + 1) * SPAN, :] = rest[c]


def fields(ref, at):
    return [ref[at + (slice(c * SPAN, (c + 1) * SPAN), slice(None))] for c in range(3)]


def section_kernel(section, *refs):
    refs = list(refs)
    deck_ref, back_ref, column_first, column_second, row_first, row_second, metric_ref, keep_ref = refs[:8]
    strain_ref, lap_ref, rest_ref, deck_strain, deck_lap, deck_rest = refs[8:14]
    del refs[:14]
    base_back = None
    if section > 0:
        base_back = refs[0]
        del refs[0]
    last = section == 2
    if last:
        deck_hbm, back_hbm, deck_out, back_out, deck_sems, back_sems = refs
        copies = []

        def send(rows, r, whole, sems):
            copies.append(pltpu.make_async_copy(rows.at[r], whole.at[:, r, :], sems.at[r]))
            copies[-1].start()

    else:
        far_ref, near_ref, deck_out, back_out, answer_out, deck_pieces, back_pieces = refs
        clear_pieces(deck_pieces, back_pieces)
    column, line, tile = position()
    odd = lax.rem(tile, 2) == 0
    odd_line = lax.rem(line, 2) == 0
    west_end = (column > 0).astype(F32)
    east_end = (column < lax.axis_size("gy") - 1).astype(F32)

    def ordered(flag, first, second, at):
        a, b = first[at], second[at]
        return jnp.where(flag, a, b), jnp.where(flag, b, a)

    spans = [slice(c * SPAN, (c + 1) * SPAN) for c in range(3)]
    across = [ordered(odd, row_first, row_second, (at, slice(None))) for at in spans]
    beside = []
    halves = [
        ordered(odd, row_first, row_second, (slice(PLANES, PLANES + 8), slice(i * COLS, (i + 1) * COLS)))
        for i in range(2)
    ]
    for side in range(2):
        cells = jnp.concatenate([halves[0][side], halves[1][side], jnp.zeros((COLS - 16, COLS), F32)], axis=0)
        beside.append(cells.T)
    north_end = (line > 0).astype(F32)
    south_end = (line < lax.axis_size("grid") * lax.axis_size("gx") - 1).astype(F32)
    along = [ordered(odd_line, column_first, column_second, (at, slice(None))) for at in spans]
    along = [(before * north_end, after * south_end) for before, after in along]
    for r in range(DROWS):
        if r == 0:
            minus = [a[0] for a in across]
            plus = fields(deck_ref, (1,))
        else:
            minus = fields(deck_ref, (0,))
            plus = [a[1] for a in across]
        part = deck_strain[r], fields(deck_lap, (r,)), fields(deck_rest, (r,))
        new = deck_outer(section, fields(deck_ref, (r,)), minus, plus, deck_metric(metric_ref, r), part)
        for c in range(3):
            deck_out[r, c * SPAN : (c + 1) * SPAN, :] = new[c]
        if last:
            send(deck_out, r, deck_hbm, deck_sems)
        else:
            stack_deck(deck_pieces, r, jnp.concatenate(new, axis=0))
    lane = iota((SPAN, COLS), 1)
    for r in range(ROWS):
        here = fields(back_ref, (r,))
        plus_eta, minus_eta = [], []
        for c in range(3):
            from_west = beside[0][spans[c], r : r + 1] * west_end
            from_east = beside[1][spans[c], r : r + 1] * east_end
            plus_eta.append(jnp.where(lane == COLS - 1, from_east, pltpu.roll(here[c], COLS - 1, 1)))
            minus_eta.append(jnp.where(lane == 0, from_west, pltpu.roll(here[c], 1, 1)))
        keep = keep_ref[r, 0:1, :]
        if 0 < r < ROWS - 1:
            part = strain_ref[r - 1], fields(lap_ref, (r - 1,)), fields(rest_ref, (r - 1,))
        else:
            minus = fields(back_ref, (r - 1,)) if r > 0 else [a[0] for a in along]
            plus = fields(back_ref, (r + 1,)) if r < ROWS - 1 else [a[1] for a in along]
            base = fields(base_back, (r,)) if section > 0 else None
            part = inner_part(here, minus, plus, keep, base, section)
        new = outer_part(here, minus_eta, plus_eta, part, keep, section)
        for c in range(3):
            back_out[r, c * SPAN : (c + 1) * SPAN, :] = new[c]
        if last:
            send(back_out, r, back_hbm, back_sems)
        else:
            stack_back(back_pieces, r, jnp.concatenate(new, axis=0))
    if last:
        for c in copies:
            c.wait()
    else:
        answer(far_ref, near_ref, deck_pieces, back_pieces, answer_out)


def local(deck_fields, back_fields, metrics, donors, stencil, fringe_cells):
    group = ("gy", "gx")
    everyone = ("grid", "gx", "gy")

    def exchange(x):
        return lax.all_to_all(x, group, split_axis=0, concat_axis=0, tiled=True)

    count = lax.axis_size("grid") * lax.axis_size("gx") * lax.axis_size("gy")
    across_y = lax.axis_size("gy")

    def pairs(step, first, periodic=False):
        out = []
        for t in range(count):
            if (t // step) % 2 == first:
                other = (t + step) % count
                if periodic or t + step < count:
                    out += [(t, other), (other, t)]
                else:
                    out += [(t, t ^ 2), (other, other ^ 2)]
        return out

    deck_in = deck_fields.reshape(PLANES, DROWS, DCOLS)
    back_in = back_fields.reshape(PLANES, ROWS, COLS)
    request, placing, rim_map, near_map, rim_keep = call(
        route_kernel,
        [
            ((MEMBERS, 1, 128), F32),
            ((MEMBERS, 3 * CAP), F32),
            ((SLOTS, 3 * COLS), BF16),
            ((NEAR * MEMBERS, 2 * COLS), BF16),
            ((3, 8, COLS), F32),
        ],
        [donors.reshape(1, FRINGE), stencil.reshape(FRINGE, 4).T, fringe_cells],
        scratch=[
            pltpu.VMEM((1, FRINGE), jnp.int32),
            pltpu.VMEM((4, FRINGE), jnp.int32),
            pltpu.VMEM((1, FRINGE - NEAR), jnp.int32),
            pltpu.SemaphoreType.DMA((3,)),
        ],
        hbm_at=(0, 1, 2),
        name="route",
    )
    request = exchange(request)
    pieces = [pltpu.VMEM((256, DROWS * DCOLS), BF16), pltpu.VMEM((256, ROWS * COLS), BF16)]
    deck, back_state, far, near, answers = call(
        first_answer_kernel,
        [
            ((DROWS, PLANES, DCOLS), F32),
            ((ROWS, PLANES, COLS), F32),
            ((SLOTS, DROWS * DCOLS), BF16),
            ((NEAR * MEMBERS, ROWS * COLS), BF16),
            ((MEMBERS, 1, PACKED), F32),
        ],
        [request, deck_in, back_in],
        scratch=[pltpu.VMEM((MEMBERS, 128), F32)]
        + pieces
        + [
            pltpu.SemaphoreType.DMA((DROWS,)),
            pltpu.SemaphoreType.DMA((ROWS,)),
        ],
        hbm_at=(1, 2),
        name="first_answer",
    )
    base = None
    for section in range(3):
        got = exchange(answers)
        got_pieces, deck, column_first, column_second, row_first, row_second = call(
            rim_kernel,
            [
                ((2 * PLANES, SLOTS), BF16),
                ((DROWS, PLANES, DCOLS), F32),
                ((PLANES, COLS), F32),
                ((PLANES, COLS), F32),
                ((PLANES + 8, DCOLS), F32),
                ((PLANES + 8, DCOLS), F32),
            ],
            [got, rim_map, near_map, rim_keep, deck, back_state],
            scratch=[pltpu.VMEM((MEMBERS, PACKED), F32)],
            name="rim",
        )
        row_first = lax.ppermute(row_first, everyone, pairs(1, 1, True))
        row_second = lax.ppermute(row_second, everyone, pairs(1, 0, True))
        column_first = lax.ppermute(column_first, everyone, pairs(across_y, 1))
        column_second = lax.ppermute(column_second, everyone, pairs(across_y, 0))
        inner = [
            ((ROWS - 2, SPAN, COLS), F32),
            ((ROWS - 2, PLANES, COLS), F32),
            ((ROWS - 2, PLANES, COLS), F32),
            ((DROWS, SPAN, DCOLS), F32),
            ((DROWS, PLANES, DCOLS), F32),
            ((DROWS, PLANES, DCOLS), F32),
        ]
        if section == 0:
            back_state, fill_map, keep, *inner = call(
                first_fill_kernel,
                [((ROWS, PLANES, COLS), F32), ((SLOTS, ROWS * COLS), BF16), ((ROWS, 8, COLS), F32)] + inner,
                [got_pieces, placing, back_state, deck, metrics],
                name="fill",
            )
            base = [deck, back_state]
        else:
            back_state, *inner = call(
                functools.partial(fill_kernel, section),
                [((ROWS, PLANES, COLS), F32)] + inner,
                [got_pieces, fill_map, keep, back_state, deck, metrics] + base,
                name="fill",
            )
        ins = [deck, back_state, column_first, column_second, row_first, row_second, metrics, keep] + inner
        if section > 0:
            ins.append(base[1])
        kernel = functools.partial(section_kernel, section)
        if section < 2:
            deck, back_state, answers = call(
                kernel,
                [
                    ((DROWS, PLANES, DCOLS), F32),
                    ((ROWS, PLANES, COLS), F32),
                    ((MEMBERS, 1, PACKED), F32),
                ],
                ins + [far, near],
                scratch=pieces,
                name="section",
            )
        else:
            deck, back_state = call(
                kernel,
                [((PLANES, DROWS, DCOLS), F32), ((PLANES, ROWS, COLS), F32)],
                ins,
                scratch=[
                    pltpu.VMEM((DROWS, PLANES, DCOLS), F32),
                    pltpu.VMEM((ROWS, PLANES, COLS), F32),
                    pltpu.SemaphoreType.DMA((DROWS,)),
                    pltpu.SemaphoreType.DMA((ROWS,)),
                ],
                outs_in=pl.ANY,
                name="section",
            )
    return deck.reshape(deck_fields.shape), back_state.reshape(back_fields.shape)


def solution(mesh):
    return jax.shard_map(
        local,
        mesh=mesh,
        in_specs=(
            P(None, None, ("grid", "gx", "gy"), None),
            P(None, None, ("grid", "gx"), "gy"),
            P(None, ("grid", "gx", "gy"), None),
            P(("grid", "gx", "gy"), None, None),
            P(("grid", "gx", "gy"), None, None),
            P(("grid", "gx", "gy"), None),
        ),
        out_specs=(P(None, None, ("grid", "gx", "gy"), None), P(None, None, ("grid", "gx"), "gy")),
        check_vma=False,
    )
```

```python
import functools

import jax
import jax.numpy as jnp
from jax import lax
from jax.experimental import pallas as pl
from jax.experimental.pallas import tpu as pltpu
from jax.sharding import PartitionSpec as P

SPAN = 32
PLANES = 96
MEMBERS = 64
CAP = 16
SLOTS = MEMBERS * CAP
ROWS = 16
COLS = 128
DROWS = 2
DCOLS = 384
FRINGE = 512
NEAR = 4
TIME_STEP = 0.05
SMAGORINSKY = 0.02
WEIGHTS = (1.0, 0.25, 2.0 / 3.0)
F32 = jnp.float32
BF16 = jnp.bfloat16
NT = (((1,), (1,)), ((), ()))
NN = (((1,), (0,)), ((), ()))
VMEM_LIMIT = 24 * 1024 * 1024
PACKED = CAP * PLANES
R_ROW, R_COL, R_FX, R_FY, R_GRID = range(5)


def position():
    column = lax.axis_index("gy")
    line = lax.axis_index("grid") * lax.axis_size("gx") + lax.axis_index("gx")
    tile = line * lax.axis_size("gy") + column
    return column, line, tile


def dot(a, b, dims):
    return lax.dot_general(a, b, dims, preferred_element_type=F32)


def iota(shape, dim):
    return lax.broadcasted_iota(jnp.int32, shape, dim)


def call(kernel, outs, ins, scratch=(), hbm_at=(), outs_in=pltpu.VMEM, name=None):
    def spec(i):
        return pl.BlockSpec(memory_space=pltpu.HBM if i in hbm_at else pltpu.VMEM)

    ins = [pltpu.with_memory_space_constraint(x, pltpu.HBM) if i in hbm_at else x for i, x in enumerate(ins)]
    return pl.pallas_call(
        kernel,
        out_shape=tuple(jax.ShapeDtypeStruct(s, d) for s, d in outs),
        in_specs=[spec(i) for i in range(len(ins))],
        out_specs=tuple(pl.BlockSpec(memory_space=outs_in) for _ in outs),
        scratch_shapes=list(scratch),
        compiler_params=pltpu.CompilerParams(vmem_limit_bytes=VMEM_LIMIT),
        name=name,
    )(*ins)


def route_kernel(
    donors_hbm, stencil_hbm, cells_hbm, request_ref, local_ref, rim_ref, near_ref, keep_ref,
    donors_ref, stencil_ref, cells_ref, sems,
):
    pairs = [(donors_hbm, donors_ref), (stencil_hbm, stencil_ref), (cells_hbm, cells_ref)]
    copies = [pltpu.make_async_copy(a, b, sems.at[i]) for i, (a, b) in enumerate(pairs)]
    for c in copies:
        c.start()
    for c in copies:
        c.wait()
    donors = donors_ref[...]
    donors = (donors & 7) * 8 + (donors >> 3)
    member = (iota((MEMBERS, FRINGE), 0) == donors).astype(F32)
    before = (iota((FRINGE, FRINGE), 0) < iota((FRINGE, FRINGE), 1)).astype(BF16)
    member_b = member.astype(BF16)
    earlier = dot(member_b, before, NN)
    rank = jnp.sum(member * earlier, axis=0, keepdims=True).astype(jnp.int32)
    at_rank = (iota((CAP, FRINGE), 0) == rank).astype(F32)

    def place(values):
        stacked = jnp.concatenate([at_rank * v.astype(F32) for v in values], axis=0)
        return dot(member_b, stacked.astype(BF16), NT)

    row = stencil_ref[0:1, :]
    col = stencil_ref[1:2, :]
    lane = iota((1, FRINGE), 1)
    grid = jnp.where(lane < NEAR, 1, 2)
    half = col >> 1
    sent = place([row, half, col - 2 * half, stencil_ref[2:3, :], stencil_ref[3:4, :], grid])
    request_ref[:, 0, :] = jnp.zeros((MEMBERS, 128), F32)
    request_ref[:, 0, 0:16] = sent[:, 0:16]
    request_ref[:, 0, 16:32] = 2.0 * sent[:, 16:32] + sent[:, 32:48]
    request_ref[:, 0, 32:80] = sent[:, 48:96]
    cells = jnp.concatenate([jnp.zeros((1, NEAR), jnp.int32), cells_ref[...]], axis=1)
    far = lane >= NEAR
    local_ref[...] = place(
        [
            jnp.where(far, (cells >> 7) + 1, 0),
            jnp.where(far, cells & 127, 0),
            jnp.where(far, 0, lane + 1),
        ]
    )
    landing(local_ref, rim_ref, near_ref, keep_ref)


def over_eight(x):
    return jnp.sum(x.reshape(MEMBERS // 8, 8, COLS), axis=0)


def kept(listed):
    return 1.0 - jnp.broadcast_to(jnp.sum(listed, axis=0, keepdims=True), (8, COLS))


def landing(local_ref, rim_ref, near_ref, keep_ref):
    lane = iota((MEMBERS, COLS), 1)
    places = local_ref[...].astype(jnp.int32)
    listed = [jnp.zeros((8, COLS), F32) for _ in range(3)]

    for s in range(CAP):
        at = slice(s * MEMBERS, (s + 1) * MEMBERS)
        row = jnp.broadcast_to(places[:, s : s + 1] - 1, (MEMBERS, COLS))
        col = jnp.broadcast_to(places[:, CAP + s : CAP + s + 1], (MEMBERS, COLS))
        hit = jnp.where(lane == col, 1.0, 0.0)
        for i, r in enumerate((0, ROWS - 1)):
            here = jnp.where(row == r, hit, 0.0)
            rim_ref[at, i * COLS : (i + 1) * COLS] = here.astype(BF16)
            listed[i] = listed[i] + over_eight(here)
        side = jnp.where(col == 0, row, jnp.where(col == COLS - 1, row + ROWS, -1))
        here = jnp.where((lane == side) & (row >= 0), 1.0, 0.0)
        rim_ref[at, 2 * COLS : 3 * COLS] = here.astype(BF16)
        listed[2] = listed[2] + over_eight(here)
        if s < NEAR:
            near = places[:, 2 * CAP + s : 2 * CAP + s + 1] - 1
            place = jnp.where(near >= 0, (near >> 1) * COLS + COLS - 2 + (near & 1), -1)
            place = jnp.broadcast_to(place, (MEMBERS, COLS))
            for r in range(DROWS):
                near_ref[at, r * COLS : (r + 1) * COLS] = jnp.where(lane + r * COLS == place, 1.0, 0.0).astype(BF16)
    for i in range(3):
        keep_ref[i] = kept(listed[i])


def split(x):
    high = x.astype(BF16)
    return high, (x - high.astype(F32)).astype(BF16)


def weights(request_ref, rows_ref, far_ref, near_ref):
    rows_ref[...] = request_ref[:, 0, :]
    request = rows_ref[...]
    whole = request.astype(jnp.int32)
    lane = iota((MEMBERS, COLS), 1)

    def wide(x, f, s):
        at = f * CAP + s
        return jnp.broadcast_to(x[:, at : at + 1], (MEMBERS, COLS))

    for s in range(CAP):
        at = slice(s * MEMBERS, (s + 1) * MEMBERS)
        col = wide(whole, R_COL, s)
        fx = wide(request, R_FX, s) * (1.0 / 16.0)
        fy = wide(request, R_FY, s) * (1.0 / 16.0)
        grid = wide(request, R_GRID, s)
        on_deck = jnp.where(grid == 2.0, 1.0, 0.0)
        first, second = on_deck * (1.0 - fx), on_deck * fx
        share = [first * (1.0 - fy), first * fy, second * (1.0 - fy), second * fy]
        for t in range(DCOLS // COLS):
            low, high = lane + t * COLS == col, lane + t * COLS == col + 1
            for r in range(DROWS):
                here = jnp.where(low, share[2 * r], jnp.where(high, share[2 * r + 1], 0.0))
                start = r * DCOLS + t * COLS
                far_ref[at, start : start + COLS] = here.astype(BF16)
        if s < NEAR:
            row = wide(whole, R_ROW, s)
            on_back = jnp.where(grid == 1.0, 1.0, 0.0)
            across = jnp.where(lane == col, on_back * (1.0 - fy), jnp.where(lane == col + 1, on_back * fy, 0.0))
            first, second = (1.0 - fx) * across, fx * across
            for r in range(ROWS):
                here = jnp.where(row == r, first, jnp.where(row + 1 == r, second, 0.0))
                near_ref[at, r * COLS : (r + 1) * COLS] = here.astype(BF16)


def stack_deck(pieces, r, value):
    high, low = split(value)
    pieces[0:PLANES, r * DCOLS : (r + 1) * DCOLS] = high
    pieces[128 : 128 + PLANES, r * DCOLS : (r + 1) * DCOLS] = low


def stack_back(pieces, r, value):
    high, low = split(value)
    pieces[0:PLANES, r * COLS : (r + 1) * COLS] = high
    pieces[128 : 128 + PLANES, r * COLS : (r + 1) * COLS] = low


def clear_pieces(deck_pieces, back_pieces):
    for pieces in (deck_pieces, back_pieces):
        gap = jnp.zeros((128 - PLANES, pieces.shape[1]), BF16)
        pieces[PLANES:128, :] = gap
        pieces[128 + PLANES : 256, :] = gap


def answer(far_ref, near_ref, deck_pieces, back_pieces, out_ref, quarters=range(CAP // 4)):
    lane = iota((MEMBERS, 128), 1)
    for q in quarters:
        got = dot(far_ref[q * 256 : (q + 1) * 256, :], deck_pieces[...], NT)
        if q == 0:
            got = got + dot(near_ref[...], back_pieces[...], NT)
        got = got[:, 0:128] + got[:, 128:256]
        a = [got[i * MEMBERS : (i + 1) * MEMBERS, :] for i in range(4)]
        base = q * 4 * PLANES
        out_ref[:, 0, base : base + 128] = jnp.where(lane < 96, a[0], pltpu.roll(a[1], 96, 1))
        out_ref[:, 0, base + 128 : base + 256] = jnp.where(
            lane < 64, pltpu.roll(a[1], 96, 1), pltpu.roll(a[2], 64, 1)
        )
        out_ref[:, 0, base + 256 : base + 384] = jnp.where(
            lane < 32, pltpu.roll(a[2], 64, 1), pltpu.roll(a[3], 32, 1)
        )


def first_answer_kernel(
    request_ref, deck_hbm, back_hbm, deck_out, back_out, far_ref, near_ref, out_ref,
    rows_ref, deck_pieces, back_pieces, deck_sems, back_sems,
):
    copies = [
        pltpu.make_async_copy(deck_hbm.at[:, r, :], deck_out.at[r], deck_sems.at[r]) for r in range(DROWS)
    ] + [pltpu.make_async_copy(back_hbm.at[:, r, :], back_out.at[r], back_sems.at[r]) for r in range(ROWS)]
    for c in copies:
        c.start()
    clear_pieces(deck_pieces, back_pieces)
    weights(request_ref, rows_ref, far_ref, near_ref)
    for c in copies:
        c.wait()
    for r in range(DROWS):
        stack_deck(deck_pieces, r, deck_out[r])
    for r in range(ROWS):
        stack_back(back_pieces, r, back_out[r])
    answer(far_ref, near_ref, deck_pieces, back_pieces, out_ref)


def rim_kernel(
    got_ref, rim_ref, near_ref, keep_ref, deck_ref, back_ref,
    got_pieces, deck_out, column_first, column_second, row_first, row_second, plain_ref,
):
    plain_ref[...] = got_ref[:, 0, :]
    lane = iota((MEMBERS, 128), 1)
    for q in range(CAP // 4):
        base = q * 4 * PLANES
        c0 = plain_ref[:, base : base + 128]
        c1 = plain_ref[:, base + 128 : base + 256]
        c2 = plain_ref[:, base + 256 : base + 384]
        a0 = jnp.where(lane < 96, c0, 0.0)
        a1 = jnp.where(lane < 32, pltpu.roll(c0, 32, 1), jnp.where(lane < 96, pltpu.roll(c1, 32, 1), 0.0))
        a2 = jnp.where(lane < 64, pltpu.roll(c1, 64, 1), jnp.where(lane < 96, pltpu.roll(c2, 64, 1), 0.0))
        a3 = jnp.where(lane < 96, pltpu.roll(c2, 96, 1), 0.0)
        across = jnp.concatenate([a0, a1, a2, a3], axis=0).T
        high, low = split(across[0:PLANES, :])
        got_pieces[0:PLANES, q * 256 : (q + 1) * 256] = high
        got_pieces[PLANES : 2 * PLANES, q * 256 : (q + 1) * 256] = low
    near = dot(got_pieces[:, 0:256], near_ref[...], NN)
    near = near[0:PLANES] + near[PLANES : 2 * PLANES]
    lane = iota((PLANES, 128), 1)
    column, line, tile = position()
    odd = lax.rem(tile, 2) == 0
    odd_line = lax.rem(line, 2) == 0
    deck = []
    for r in range(DROWS):
        outer = jnp.where(lane >= 126, near[:, r * 128 : (r + 1) * 128], deck_ref[r, :, 256:384])
        deck.append(jnp.concatenate([deck_ref[r, :, 0:256], outer], axis=1))
        deck_out[r] = deck[r]
    row_first[0:PLANES, :] = jnp.where(odd, deck[0], deck[1])
    row_second[0:PLANES, :] = jnp.where(odd, deck[1], deck[0])
    rim = dot(got_pieces[...], rim_ref[...], NN)
    rim = rim[0:PLANES] + rim[PLANES : 2 * PLANES]
    north = back_ref[0] * keep_ref[0, 0:1, :] + rim[:, 0:COLS]
    south = back_ref[ROWS - 1] * keep_ref[1, 0:1, :] + rim[:, COLS : 2 * COLS]
    column_first[...] = jnp.where(odd_line, north, south)
    column_second[...] = jnp.where(odd_line, south, north)
    ends = jnp.zeros((PLANES, COLS), F32)
    for r in range(ROWS):
        ends = jnp.where(lane == r, back_ref[r, :, 0:1], ends)
        ends = jnp.where(lane == ROWS + r, back_ref[r, :, COLS - 1 : COLS], ends)
    ends = ends * keep_ref[2, 0:1, :] + rim[:, 2 * COLS : 3 * COLS]
    ends = jnp.concatenate([ends, jnp.zeros((COLS - PLANES, COLS), F32)], axis=0).T
    parts = [ends[i * 8 : (i + 1) * 8, :] for i in range(4)]
    for side, flag in ((row_first, odd), (row_second, jnp.logical_not(odd))):
        for i in range(2):
            side[PLANES : PLANES + 8, i * COLS : (i + 1) * COLS] = jnp.where(flag, parts[i], parts[2 + i])
        side[PLANES : PLANES + 8, 2 * COLS : 3 * COLS] = jnp.zeros((8, COLS), F32)


def fill_rows(got_pieces, fill_ref, keep_ref, back_ref, back_out):
    for c in range(ROWS // 2):
        new = dot(got_pieces[...], fill_ref[:, c * 256 : (c + 1) * 256], NN)
        new = new[0:PLANES] + new[PLANES : 2 * PLANES]
        for half in range(2):
            r = 2 * c + half
            back_out[r] = back_ref[r] * keep_ref[r, 0:1, :] + new[:, half * 128 : (half + 1) * 128]


def fill_kernel(
    section, got_pieces, fill_ref, keep_ref, back_ref, deck_ref, metric_ref, base_deck, base_back, back_out, *inner
):
    fill_rows(got_pieces, fill_ref, keep_ref, back_ref, back_out)
    inner_rows(section, back_out, keep_ref, base_back, *inner[:3])
    deck_inner(section, deck_ref, metric_ref, base_deck, *inner[3:])


def first_fill_kernel(
    got_pieces, local_ref, back_ref, deck_ref, metric_ref, back_out, fill_ref, keep_ref, *inner
):
    lane = iota((MEMBERS, COLS), 1)
    places = local_ref[...].astype(jnp.int32)
    listed = [jnp.zeros((8, COLS), F32) for _ in range(ROWS)]
    for s in range(CAP):
        at = slice(s * MEMBERS, (s + 1) * MEMBERS)
        row = jnp.broadcast_to(places[:, s : s + 1] - 1, (MEMBERS, COLS))
        col = jnp.broadcast_to(places[:, CAP + s : CAP + s + 1], (MEMBERS, COLS))
        hit = jnp.where(lane == col, 1.0, 0.0)
        for r in range(ROWS):
            here = jnp.where(row == r, hit, 0.0)
            fill_ref[at, r * COLS : (r + 1) * COLS] = here.astype(BF16)
            listed[r] = listed[r] + over_eight(here)
    for r in range(ROWS):
        keep_ref[r] = kept(listed[r])
    fill_rows(got_pieces, fill_ref, keep_ref, back_ref, back_out)
    inner_rows(0, back_out, keep_ref, None, *inner[:3])
    deck_inner(0, deck_ref, metric_ref, None, *inner[3:])


def deck_metric(metric_ref, r):
    return [metric_ref[i, r : r + 1, :] for i in range(4)]


def deck_keep():
    return jnp.where(iota((1, DCOLS), 1) < DCOLS - 2, 1.0, 0.0)


def deck_inner(section, deck_ref, metric_ref, base_ref, strain_out, lap_out, rest_out):
    lane = iota((SPAN, DCOLS), 1)
    half = (0.5 * WEIGHTS[section] * TIME_STEP) * deck_keep()
    for r in range(DROWS):
        here = fields(deck_ref, (r,))
        base = None if base_ref is None else fields(base_ref, (r,))
        m = deck_metric(metric_ref, r)
        g1, g2 = m[0] * m[0] + m[1] * m[1], m[2] * m[2] + m[3] * m[3]
        speed_eta, speed_span = half * (m[2] * here[0] + m[3] * here[1]), half * here[2]
        strain = None
        for c in range(3):
            f = here[c]
            plus_eta = jnp.where(lane == DCOLS - 1, 0.0, pltpu.roll(f, DCOLS - 1, 1))
            minus_eta = jnp.where(lane == 0, 0.0, pltpu.roll(f, 1, 1))
            plus_span = pltpu.roll(f, SPAN - 1, 0)
            minus_span = pltpu.roll(f, 1, 0)
            b, s = plus_eta - minus_eta, plus_span - minus_span
            square = b * b + s * s
            strain = square if strain is None else strain + square
            doubled = 2.0 * f
            at = slice(c * SPAN, (c + 1) * SPAN)
            lap_out[r, at, :] = g2 * (plus_eta - doubled + minus_eta) + (plus_span - doubled + minus_span) - g1 * doubled
            rest_out[r, at, :] = carried(section, f, base, c) - (speed_eta * b + speed_span * s)
        strain_out[r] = strain


def deck_outer(section, here, minus_xi, plus_xi, m, part):
    strain, lap, rest = part
    step = (WEIGHTS[section] * TIME_STEP) * deck_keep()
    a = [plus_xi[c] - minus_xi[c] for c in range(3)]
    strain = strain + (a[0] * a[0] + a[1] * a[1] + a[2] * a[2])
    stretched = 1.0 + 0.25 * strain
    viscosity = (SMAGORINSKY * step) * (stretched * lax.rsqrt(stretched))
    speed_xi = (0.5 * step) * (m[0] * here[0] + m[1] * here[1])
    g1 = m[0] * m[0] + m[1] * m[1]
    return [
        rest[c] + (viscosity * (lap[c] + g1 * (plus_xi[c] + minus_xi[c])) - speed_xi * a[c])
        for c in range(3)
    ]


def carried(section, f, base, c):
    if section == 0:
        return f
    if section == 1:
        return 0.75 * base[c] + 0.25 * f
    return base[c] * (1.0 / 3.0) + (2.0 / 3.0) * f


def inner_part(here, minus_xi, plus_xi, keep, base, section):
    half = (0.5 * WEIGHTS[section] * TIME_STEP) * keep
    speed_xi, speed_span = half * here[0], half * here[2]
    strain, lap, rest = None, [], []
    for c in range(3):
        f = here[c]
        plus_span = pltpu.roll(f, SPAN - 1, 0)
        minus_span = pltpu.roll(f, 1, 0)
        a = plus_xi[c] - minus_xi[c]
        s = plus_span - minus_span
        square = a * a + s * s
        strain = square if strain is None else strain + square
        lap.append((plus_xi[c] + minus_xi[c]) + (plus_span + minus_span) - 6.0 * f)
        advection = speed_xi * a + speed_span * s
        rest.append(carried(section, f, base, c) - advection)
    return strain, lap, rest


def outer_part(here, minus_eta, plus_eta, part, keep, section):
    strain, lap, rest = part
    step = (WEIGHTS[section] * TIME_STEP) * keep
    b = [plus_eta[c] - minus_eta[c] for c in range(3)]
    strain = strain + (b[0] * b[0] + b[1] * b[1] + b[2] * b[2])
    stretched = 1.0 + 0.25 * strain
    viscosity = (SMAGORINSKY * step) * (stretched * lax.rsqrt(stretched))
    speed_eta = (0.5 * step) * here[1]
    return [
        rest[c] + (viscosity * (lap[c] + (plus_eta[c] + minus_eta[c])) - speed_eta * b[c])
        for c in range(3)
    ]


def inner_rows(section, back_ref, keep_ref, base_ref, strain_out, lap_out, rest_out):
    for r in range(1, ROWS - 1):
        strain, lap, rest = inner_part(
            fields(back_ref, (r,)),
            fields(back_ref, (r - 1,)),
            fields(back_ref, (r + 1,)),
            keep_ref[r, 0:1, :],
            None if base_ref is None else fields(base_ref, (r,)),
            section,
        )
        strain_out[r - 1] = strain
        for c in range(3):
            lap_out[r - 1, c * SPAN : (c + 1) * SPAN, :] = lap[c]
            rest_out[r - 1, c * SPAN : (c + 1) * SPAN, :] = rest[c]


def fields(ref, at):
    return [ref[at + (slice(c * SPAN, (c + 1) * SPAN), slice(None))] for c in range(3)]


def section_kernel(section, *refs):
    refs = list(refs)
    deck_ref, back_ref, column_first, column_second, row_first, row_second, metric_ref, keep_ref = refs[:8]
    strain_ref, lap_ref, rest_ref, deck_strain, deck_lap, deck_rest = refs[8:14]
    del refs[:14]
    base_back = None
    if section > 0:
        base_back = refs[0]
        del refs[0]
    last = section == 2
    if last:
        deck_hbm, back_hbm, deck_out, back_out, deck_sems, back_sems = refs
        copies = []

        def send(rows, r, whole, sems):
            copies.append(pltpu.make_async_copy(rows.at[r], whole.at[:, r, :], sems.at[r]))
            copies[-1].start()

    else:
        far_ref, near_ref, deck_out, back_out, answer_out, deck_pieces, back_pieces = refs
        clear_pieces(deck_pieces, back_pieces)
    column, line, tile = position()
    odd = lax.rem(tile, 2) == 0
    odd_line = lax.rem(line, 2) == 0
    west_end = (column > 0).astype(F32)
    east_end = (column < lax.axis_size("gy") - 1).astype(F32)

    def ordered(flag, first, second, at):
        a, b = first[at], second[at]
        return jnp.where(flag, a, b), jnp.where(flag, b, a)

    spans = [slice(c * SPAN, (c + 1) * SPAN) for c in range(3)]
    across = [ordered(odd, row_first, row_second, (at, slice(None))) for at in spans]
    beside = []
    halves = [
        ordered(odd, row_first, row_second, (slice(PLANES, PLANES + 8), slice(i * COLS, (i + 1) * COLS)))
        for i in range(2)
    ]
    for side in range(2):
        cells = jnp.concatenate([halves[0][side], halves[1][side], jnp.zeros((COLS - 16, COLS), F32)], axis=0)
        beside.append(cells.T)
    north_end = (line > 0).astype(F32)
    south_end = (line < lax.axis_size("grid") * lax.axis_size("gx") - 1).astype(F32)
    along = [ordered(odd_line, column_first, column_second, (at, slice(None))) for at in spans]
    along = [(before * north_end, after * south_end) for before, after in along]
    for r in range(DROWS):
        if r == 0:
            minus = [a[0] for a in across]
            plus = fields(deck_ref, (1,))
        else:
            minus = fields(deck_ref, (0,))
            plus = [a[1] for a in across]
        part = deck_strain[r], fields(deck_lap, (r,)), fields(deck_rest, (r,))
        new = deck_outer(section, fields(deck_ref, (r,)), minus, plus, deck_metric(metric_ref, r), part)
        for c in range(3):
            deck_out[r, c * SPAN : (c + 1) * SPAN, :] = new[c]
        if last:
            send(deck_out, r, deck_hbm, deck_sems)
        else:
            stack_deck(deck_pieces, r, jnp.concatenate(new, axis=0))
    lane = iota((SPAN, COLS), 1)
    for r in range(ROWS):
        here = fields(back_ref, (r,))
        plus_eta, minus_eta = [], []
        for c in range(3):
            from_west = beside[0][spans[c], r : r + 1] * west_end
            from_east = beside[1][spans[c], r : r + 1] * east_end
            plus_eta.append(jnp.where(lane == COLS - 1, from_east, pltpu.roll(here[c], COLS - 1, 1)))
            minus_eta.append(jnp.where(lane == 0, from_west, pltpu.roll(here[c], 1, 1)))
        keep = keep_ref[r, 0:1, :]
        if 0 < r < ROWS - 1:
            part = strain_ref[r - 1], fields(lap_ref, (r - 1,)), fields(rest_ref, (r - 1,))
        else:
            minus = fields(back_ref, (r - 1,)) if r > 0 else [a[0] for a in along]
            plus = fields(back_ref, (r + 1,)) if r < ROWS - 1 else [a[1] for a in along]
            base = fields(base_back, (r,)) if section > 0 else None
            part = inner_part(here, minus, plus, keep, base, section)
        new = outer_part(here, minus_eta, plus_eta, part, keep, section)
        for c in range(3):
            back_out[r, c * SPAN : (c + 1) * SPAN, :] = new[c]
        if last:
            send(back_out, r, back_hbm, back_sems)
        else:
            stack_back(back_pieces, r, jnp.concatenate(new, axis=0))
            if r in (1, 5, 9):
                answer(far_ref, near_ref, deck_pieces, back_pieces, answer_out, [(r + 3) // 4])
    if last:
        for c in copies:
            c.wait()
    else:
        answer(far_ref, near_ref, deck_pieces, back_pieces, answer_out, [0])


def local(deck_fields, back_fields, metrics, donors, stencil, fringe_cells):
    group = ("gy", "gx")
    everyone = ("grid", "gx", "gy")

    def exchange(x):
        return lax.all_to_all(x, group, split_axis=0, concat_axis=0, tiled=True)

    count = lax.axis_size("grid") * lax.axis_size("gx") * lax.axis_size("gy")
    across_y = lax.axis_size("gy")

    def pairs(step, first, periodic=False):
        out = []
        for t in range(count):
            if (t // step) % 2 == first:
                other = (t + step) % count
                if periodic or t + step < count:
                    out += [(t, other), (other, t)]
                else:
                    out += [(t, t ^ 2), (other, other ^ 2)]
        return out

    deck_in = deck_fields.reshape(PLANES, DROWS, DCOLS)
    back_in = back_fields.reshape(PLANES, ROWS, COLS)
    request, placing, rim_map, near_map, rim_keep = call(
        route_kernel,
        [
            ((MEMBERS, 1, 128), F32),
            ((MEMBERS, 3 * CAP), F32),
            ((SLOTS, 3 * COLS), BF16),
            ((NEAR * MEMBERS, 2 * COLS), BF16),
            ((3, 8, COLS), F32),
        ],
        [donors.reshape(1, FRINGE), stencil.reshape(FRINGE, 4).T, fringe_cells],
        scratch=[
            pltpu.VMEM((1, FRINGE), jnp.int32),
            pltpu.VMEM((4, FRINGE), jnp.int32),
            pltpu.VMEM((1, FRINGE - NEAR), jnp.int32),
            pltpu.SemaphoreType.DMA((3,)),
        ],
        hbm_at=(0, 1, 2),
        name="route",
    )
    request = exchange(request)
    pieces = [pltpu.VMEM((256, DROWS * DCOLS), BF16), pltpu.VMEM((256, ROWS * COLS), BF16)]
    deck, back_state, far, near, answers = call(
        first_answer_kernel,
        [
            ((DROWS, PLANES, DCOLS), F32),
            ((ROWS, PLANES, COLS), F32),
            ((SLOTS, DROWS * DCOLS), BF16),
            ((NEAR * MEMBERS, ROWS * COLS), BF16),
            ((MEMBERS, 1, PACKED), F32),
        ],
        [request, deck_in, back_in],
        scratch=[pltpu.VMEM((MEMBERS, 128), F32)]
        + pieces
        + [
            pltpu.SemaphoreType.DMA((DROWS,)),
            pltpu.SemaphoreType.DMA((ROWS,)),
        ],
        hbm_at=(1, 2),
        name="first_answer",
    )
    base = None
    for section in range(3):
        got = exchange(answers)
        got_pieces, deck, column_first, column_second, row_first, row_second = call(
            rim_kernel,
            [
                ((2 * PLANES, SLOTS), BF16),
                ((DROWS, PLANES, DCOLS), F32),
                ((PLANES, COLS), F32),
                ((PLANES, COLS), F32),
                ((PLANES + 8, DCOLS), F32),
                ((PLANES + 8, DCOLS), F32),
            ],
            [got, rim_map, near_map, rim_keep, deck, back_state],
            scratch=[pltpu.VMEM((MEMBERS, PACKED), F32)],
            name="rim",
        )
        row_first = lax.ppermute(row_first, everyone, pairs(1, 1, True))
        row_second = lax.ppermute(row_second, everyone, pairs(1, 0, True))
        column_first = lax.ppermute(column_first, everyone, pairs(across_y, 1))
        column_second = lax.ppermute(column_second, everyone, pairs(across_y, 0))
        inner = [
            ((ROWS - 2, SPAN, COLS), F32),
            ((ROWS - 2, PLANES, COLS), F32),
            ((ROWS - 2, PLANES, COLS), F32),
            ((DROWS, SPAN, DCOLS), F32),
            ((DROWS, PLANES, DCOLS), F32),
            ((DROWS, PLANES, DCOLS), F32),
        ]
        if section == 0:
            back_state, fill_map, keep, *inner = call(
                first_fill_kernel,
                [((ROWS, PLANES, COLS), F32), ((SLOTS, ROWS * COLS), BF16), ((ROWS, 8, COLS), F32)] + inner,
                [got_pieces, placing, back_state, deck, metrics],
                name="fill",
            )
            base = [deck, back_state]
        else:
            back_state, *inner = call(
                functools.partial(fill_kernel, section),
                [((ROWS, PLANES, COLS), F32)] + inner,
                [got_pieces, fill_map, keep, back_state, deck, metrics] + base,
                name="fill",
            )
        ins = [deck, back_state, column_first, column_second, row_first, row_second, metrics, keep] + inner
        if section > 0:
            ins.append(base[1])
        kernel = functools.partial(section_kernel, section)
        if section < 2:
            deck, back_state, answers = call(
                kernel,
                [
                    ((DROWS, PLANES, DCOLS), F32),
                    ((ROWS, PLANES, COLS), F32),
                    ((MEMBERS, 1, PACKED), F32),
                ],
                ins + [far, near],
                scratch=pieces,
                name="section",
            )
        else:
            deck, back_state = call(
                kernel,
                [((PLANES, DROWS, DCOLS), F32), ((PLANES, ROWS, COLS), F32)],
                ins,
                scratch=[
                    pltpu.VMEM((DROWS, PLANES, DCOLS), F32),
                    pltpu.VMEM((ROWS, PLANES, COLS), F32),
                    pltpu.SemaphoreType.DMA((DROWS,)),
                    pltpu.SemaphoreType.DMA((ROWS,)),
                ],
                outs_in=pl.ANY,
                name="section",
            )
    return deck.reshape(deck_fields.shape), back_state.reshape(back_fields.shape)


def solution(mesh):
    return jax.shard_map(
        local,
        mesh=mesh,
        in_specs=(
            P(None, None, ("grid", "gx", "gy"), None),
            P(None, None, ("grid", "gx"), "gy"),
            P(None, ("grid", "gx", "gy"), None),
            P(("grid", "gx", "gy"), None, None),
            P(("grid", "gx", "gy"), None, None),
            P(("grid", "gx", "gy"), None),
        ),
        out_specs=(P(None, None, ("grid", "gx", "gy"), None), P(None, None, ("grid", "gx"), "gy")),
        check_vma=False,
    )
```

```python
import functools

import jax
import jax.numpy as jnp
from jax import lax
from jax.experimental import pallas as pl
from jax.experimental.pallas import tpu as pltpu
from jax.sharding import PartitionSpec as P

SPAN = 32
PLANES = 96
MEMBERS = 64
CAP = 16
SLOTS = MEMBERS * CAP
ROWS = 16
COLS = 128
DROWS = 2
DCOLS = 384
FRINGE = 512
NEAR = 4
TIME_STEP = 0.05
SMAGORINSKY = 0.02
WEIGHTS = (1.0, 0.25, 2.0 / 3.0)
F32 = jnp.float32
BF16 = jnp.bfloat16
NT = (((1,), (1,)), ((), ()))
NN = (((1,), (0,)), ((), ()))
VMEM_LIMIT = 24 * 1024 * 1024
PACKED = CAP * PLANES
R_ROW, R_COL, R_FX, R_FY, R_GRID = range(5)


def position():
    column = lax.axis_index("gy")
    line = lax.axis_index("grid") * lax.axis_size("gx") + lax.axis_index("gx")
    tile = line * lax.axis_size("gy") + column
    return column, line, tile


def dot(a, b, dims):
    return lax.dot_general(a, b, dims, preferred_element_type=F32)


def iota(shape, dim):
    return lax.broadcasted_iota(jnp.int32, shape, dim)


def call(kernel, outs, ins, scratch=(), hbm_at=(), outs_in=pltpu.VMEM, name=None):
    def spec(i):
        return pl.BlockSpec(memory_space=pltpu.HBM if i in hbm_at else pltpu.VMEM)

    ins = [pltpu.with_memory_space_constraint(x, pltpu.HBM) if i in hbm_at else x for i, x in enumerate(ins)]
    return pl.pallas_call(
        kernel,
        out_shape=tuple(jax.ShapeDtypeStruct(s, d) for s, d in outs),
        in_specs=[spec(i) for i in range(len(ins))],
        out_specs=tuple(pl.BlockSpec(memory_space=outs_in) for _ in outs),
        scratch_shapes=list(scratch),
        compiler_params=pltpu.CompilerParams(vmem_limit_bytes=VMEM_LIMIT),
        name=name,
    )(*ins)


def route_kernel(
    donors_hbm, stencil_hbm, cells_hbm, request_ref, local_ref, rim_ref, near_ref, keep_ref,
    donors_ref, stencil_ref, cells_ref, sems,
):
    pairs = [(donors_hbm, donors_ref), (stencil_hbm, stencil_ref), (cells_hbm, cells_ref)]
    copies = [pltpu.make_async_copy(a, b, sems.at[i]) for i, (a, b) in enumerate(pairs)]
    for c in copies:
        c.start()
    for c in copies:
        c.wait()
    donors = donors_ref[...]
    donors = (donors & 7) * 8 + (donors >> 3)
    member = (iota((MEMBERS, FRINGE), 0) == donors).astype(F32)
    before = (iota((FRINGE, FRINGE), 0) < iota((FRINGE, FRINGE), 1)).astype(BF16)
    member_b = member.astype(BF16)
    earlier = dot(member_b, before, NN)
    rank = jnp.sum(member * earlier, axis=0, keepdims=True).astype(jnp.int32)
    at_rank = (iota((CAP, FRINGE), 0) == rank).astype(F32)

    def place(values):
        stacked = jnp.concatenate([at_rank * v.astype(F32) for v in values], axis=0)
        return dot(member_b, stacked.astype(BF16), NT)

    row = stencil_ref[0:1, :]
    col = stencil_ref[1:2, :]
    lane = iota((1, FRINGE), 1)
    grid = jnp.where(lane < NEAR, 1, 2)
    half = col >> 1
    sent = place([row, half, col - 2 * half, stencil_ref[2:3, :], stencil_ref[3:4, :], grid])
    request_ref[:, 0, :] = jnp.zeros((MEMBERS, 128), F32)
    request_ref[:, 0, 0:16] = sent[:, 0:16]
    request_ref[:, 0, 16:32] = 2.0 * sent[:, 16:32] + sent[:, 32:48]
    request_ref[:, 0, 32:80] = sent[:, 48:96]
    cells = jnp.concatenate([jnp.zeros((1, NEAR), jnp.int32), cells_ref[...]], axis=1)
    far = lane >= NEAR
    local_ref[...] = place(
        [
            jnp.where(far, (cells >> 7) + 1, 0),
            jnp.where(far, cells & 127, 0),
            jnp.where(far, 0, lane + 1),
        ]
    )
    landing(local_ref, rim_ref, near_ref, keep_ref)


def over_eight(x):
    return jnp.sum(x.reshape(MEMBERS // 8, 8, COLS), axis=0)


def kept(listed):
    return 1.0 - jnp.broadcast_to(jnp.sum(listed, axis=0, keepdims=True), (8, COLS))


def landing(local_ref, rim_ref, near_ref, keep_ref):
    lane = iota((MEMBERS, COLS), 1)
    places = local_ref[...].astype(jnp.int32)
    listed = [jnp.zeros((8, COLS), F32) for _ in range(3)]

    for s in range(CAP):
        at = slice(s * MEMBERS, (s + 1) * MEMBERS)
        row = jnp.broadcast_to(places[:, s : s + 1] - 1, (MEMBERS, COLS))
        col = jnp.broadcast_to(places[:, CAP + s : CAP + s + 1], (MEMBERS, COLS))
        hit = jnp.where(lane == col, 1.0, 0.0)
        for i, r in enumerate((0, ROWS - 1)):
            here = jnp.where(row == r, hit, 0.0)
            rim_ref[at, i * COLS : (i + 1) * COLS] = here.astype(BF16)
            listed[i] = listed[i] + over_eight(here)
        side = jnp.where(col == 0, row, jnp.where(col == COLS - 1, row + ROWS, -1))
        here = jnp.where((lane == side) & (row >= 0), 1.0, 0.0)
        rim_ref[at, 2 * COLS : 3 * COLS] = here.astype(BF16)
        listed[2] = listed[2] + over_eight(here)
        if s < NEAR:
            near = places[:, 2 * CAP + s : 2 * CAP + s + 1] - 1
            place = jnp.where(near >= 0, (near >> 1) * COLS + COLS - 2 + (near & 1), -1)
            place = jnp.broadcast_to(place, (MEMBERS, COLS))
            for r in range(DROWS):
                near_ref[at, r * COLS : (r + 1) * COLS] = jnp.where(lane + r * COLS == place, 1.0, 0.0).astype(BF16)
    for i in range(3):
        keep_ref[i] = kept(listed[i])


def split(x):
    high = x.astype(BF16)
    return high, (x - high.astype(F32)).astype(BF16)


def weights(request_ref, rows_ref, far_ref, near_ref):
    rows_ref[...] = request_ref[:, 0, :]
    request = rows_ref[...]
    whole = request.astype(jnp.int32)
    lane = iota((MEMBERS, COLS), 1)

    def wide(x, f, s):
        at = f * CAP + s
        return jnp.broadcast_to(x[:, at : at + 1], (MEMBERS, COLS))

    for s in range(CAP):
        at = slice(s * MEMBERS, (s + 1) * MEMBERS)
        col = wide(whole, R_COL, s)
        fx = wide(request, R_FX, s) * (1.0 / 16.0)
        fy = wide(request, R_FY, s) * (1.0 / 16.0)
        grid = wide(request, R_GRID, s)
        on_deck = jnp.where(grid == 2.0, 1.0, 0.0)
        first, second = on_deck * (1.0 - fx), on_deck * fx
        share = [first * (1.0 - fy), first * fy, second * (1.0 - fy), second * fy]
        for t in range(DCOLS // COLS):
            low, high = lane + t * COLS == col, lane + t * COLS == col + 1
            for r in range(DROWS):
                here = jnp.where(low, share[2 * r], jnp.where(high, share[2 * r + 1], 0.0))
                start = r * DCOLS + t * COLS
                far_ref[at, start : start + COLS] = here.astype(BF16)
        if s < NEAR:
            row = wide(whole, R_ROW, s)
            on_back = jnp.where(grid == 1.0, 1.0, 0.0)
            across = jnp.where(lane == col, on_back * (1.0 - fy), jnp.where(lane == col + 1, on_back * fy, 0.0))
            first, second = (1.0 - fx) * across, fx * across
            for r in range(ROWS):
                here = jnp.where(row == r, first, jnp.where(row + 1 == r, second, 0.0))
                near_ref[at, r * COLS : (r + 1) * COLS] = here.astype(BF16)


def stack_deck(pieces, r, value):
    high, low = split(value)
    pieces[0:PLANES, r * DCOLS : (r + 1) * DCOLS] = high
    pieces[128 : 128 + PLANES, r * DCOLS : (r + 1) * DCOLS] = low


def stack_back(pieces, r, value):
    high, low = split(value)
    pieces[0:PLANES, r * COLS : (r + 1) * COLS] = high
    pieces[128 : 128 + PLANES, r * COLS : (r + 1) * COLS] = low


def clear_pieces(deck_pieces, back_pieces):
    for pieces in (deck_pieces, back_pieces):
        gap = jnp.zeros((128 - PLANES, pieces.shape[1]), BF16)
        pieces[PLANES:128, :] = gap
        pieces[128 + PLANES : 256, :] = gap


def answer(far_ref, near_ref, deck_pieces, back_pieces, out_ref):
    lane = iota((MEMBERS, 128), 1)
    for q in range(CAP // 4):
        got = dot(far_ref[q * 256 : (q + 1) * 256, :], deck_pieces[...], NT)
        if q == 0:
            got = got + dot(near_ref[...], back_pieces[...], NT)
        got = got[:, 0:128] + got[:, 128:256]
        a = [got[i * MEMBERS : (i + 1) * MEMBERS, :] for i in range(4)]
        base = q * 4 * PLANES
        out_ref[:, 0, base : base + 128] = jnp.where(lane < 96, a[0], pltpu.roll(a[1], 96, 1))
        out_ref[:, 0, base + 128 : base + 256] = jnp.where(
            lane < 64, pltpu.roll(a[1], 96, 1), pltpu.roll(a[2], 64, 1)
        )
        out_ref[:, 0, base + 256 : base + 384] = jnp.where(
            lane < 32, pltpu.roll(a[2], 64, 1), pltpu.roll(a[3], 32, 1)
        )


def first_answer_kernel(
    request_ref, deck_hbm, back_hbm, deck_out, back_out, far_ref, near_ref, out_ref,
    rows_ref, deck_pieces, back_pieces, deck_sems, back_sems,
):
    copies = [
        pltpu.make_async_copy(deck_hbm.at[:, r, :], deck_out.at[r], deck_sems.at[r]) for r in range(DROWS)
    ] + [pltpu.make_async_copy(back_hbm.at[:, r, :], back_out.at[r], back_sems.at[r]) for r in range(ROWS)]
    for c in copies:
        c.start()
    clear_pieces(deck_pieces, back_pieces)
    weights(request_ref, rows_ref, far_ref, near_ref)
    for c in copies:
        c.wait()
    for r in range(DROWS):
        stack_deck(deck_pieces, r, deck_out[r])
    for r in range(ROWS):
        stack_back(back_pieces, r, back_out[r])
    answer(far_ref, near_ref, deck_pieces, back_pieces, out_ref)


def rim_kernel(
    got_ref, rim_ref, near_ref, keep_ref, deck_ref, back_ref,
    got_pieces, deck_out, column_first, column_second, row_first, row_second, plain_ref,
):
    plain_ref[...] = got_ref[:, 0, :]
    lane = iota((MEMBERS, 128), 1)
    for q in range(CAP // 4):
        base = q * 4 * PLANES
        c0 = plain_ref[:, base : base + 128]
        c1 = plain_ref[:, base + 128 : base + 256]
        c2 = plain_ref[:, base + 256 : base + 384]
        a0 = jnp.where(lane < 96, c0, 0.0)
        a1 = jnp.where(lane < 32, pltpu.roll(c0, 32, 1), jnp.where(lane < 96, pltpu.roll(c1, 32, 1), 0.0))
        a2 = jnp.where(lane < 64, pltpu.roll(c1, 64, 1), jnp.where(lane < 96, pltpu.roll(c2, 64, 1), 0.0))
        a3 = jnp.where(lane < 96, pltpu.roll(c2, 96, 1), 0.0)
        across = jnp.concatenate([a0, a1, a2, a3], axis=0).T
        high, low = split(across[0:PLANES, :])
        got_pieces[0:PLANES, q * 256 : (q + 1) * 256] = high
        got_pieces[PLANES : 2 * PLANES, q * 256 : (q + 1) * 256] = low
    near = dot(got_pieces[:, 0:256], near_ref[...], NN)
    near = near[0:PLANES] + near[PLANES : 2 * PLANES]
    lane = iota((PLANES, 128), 1)
    column, line, tile = position()
    odd = lax.rem(tile, 2) == 0
    odd_line = lax.rem(line, 2) == 0
    deck = []
    for r in range(DROWS):
        outer = jnp.where(lane >= 126, near[:, r * 128 : (r + 1) * 128], deck_ref[r, :, 256:384])
        deck.append(jnp.concatenate([deck_ref[r, :, 0:256], outer], axis=1))
        deck_out[r] = deck[r]
    row_first[0:PLANES, :] = jnp.where(odd, deck[0], deck[1])
    row_second[0:PLANES, :] = jnp.where(odd, deck[1], deck[0])
    rim = dot(got_pieces[...], rim_ref[...], NN)
    rim = rim[0:PLANES] + rim[PLANES : 2 * PLANES]
    north = back_ref[0] * keep_ref[0, 0:1, :] + rim[:, 0:COLS]
    south = back_ref[ROWS - 1] * keep_ref[1, 0:1, :] + rim[:, COLS : 2 * COLS]
    column_first[...] = jnp.where(odd_line, north, south)
    column_second[...] = jnp.where(odd_line, south, north)
    ends = jnp.zeros((PLANES, COLS), F32)
    for r in range(ROWS):
        ends = jnp.where(lane == r, back_ref[r, :, 0:1], ends)
        ends = jnp.where(lane == ROWS + r, back_ref[r, :, COLS - 1 : COLS], ends)
    ends = ends * keep_ref[2, 0:1, :] + rim[:, 2 * COLS : 3 * COLS]
    ends = jnp.concatenate([ends, jnp.zeros((COLS - PLANES, COLS), F32)], axis=0).T
    parts = [ends[i * 8 : (i + 1) * 8, :] for i in range(4)]
    for side, flag in ((row_first, odd), (row_second, jnp.logical_not(odd))):
        for i in range(2):
            side[PLANES : PLANES + 8, i * COLS : (i + 1) * COLS] = jnp.where(flag, parts[i], parts[2 + i])
        side[PLANES : PLANES + 8, 2 * COLS : 3 * COLS] = jnp.zeros((8, COLS), F32)


def fill_rows(got_pieces, fill_ref, keep_ref, back_ref, back_out):
    for c in range(ROWS // 2):
        new = dot(got_pieces[...], fill_ref[:, c * 256 : (c + 1) * 256], NN)
        new = new[0:PLANES] + new[PLANES : 2 * PLANES]
        for half in range(2):
            r = 2 * c + half
            back_out[r] = back_ref[r] * keep_ref[r, 0:1, :] + new[:, half * 128 : (half + 1) * 128]


def fill_kernel(
    section, got_pieces, fill_ref, keep_ref, back_ref, deck_ref, metric_ref, base_deck, base_back, back_out, *inner
):
    fill_rows(got_pieces, fill_ref, keep_ref, back_ref, back_out)
    inner_rows(section, back_out, keep_ref, base_back, *inner[:4])
    deck_inner(section, deck_ref, metric_ref, base_deck, *inner[4:])


def first_fill_kernel(
    got_pieces, local_ref, back_ref, deck_ref, metric_ref, back_out, fill_ref, keep_ref, *inner
):
    lane = iota((MEMBERS, COLS), 1)
    places = local_ref[...].astype(jnp.int32)
    listed = [jnp.zeros((8, COLS), F32) for _ in range(ROWS)]
    for s in range(CAP):
        at = slice(s * MEMBERS, (s + 1) * MEMBERS)
        row = jnp.broadcast_to(places[:, s : s + 1] - 1, (MEMBERS, COLS))
        col = jnp.broadcast_to(places[:, CAP + s : CAP + s + 1], (MEMBERS, COLS))
        hit = jnp.where(lane == col, 1.0, 0.0)
        for r in range(ROWS):
            here = jnp.where(row == r, hit, 0.0)
            fill_ref[at, r * COLS : (r + 1) * COLS] = here.astype(BF16)
            listed[r] = listed[r] + over_eight(here)
    for r in range(ROWS):
        keep_ref[r] = kept(listed[r])
    fill_rows(got_pieces, fill_ref, keep_ref, back_ref, back_out)
    inner_rows(0, back_out, keep_ref, None, *inner[:4])
    deck_inner(0, deck_ref, metric_ref, None, *inner[4:])


def deck_metric(metric_ref, r):
    return [metric_ref[i, r : r + 1, :] for i in range(4)]


def deck_keep():
    return jnp.where(iota((1, DCOLS), 1) < DCOLS - 2, 1.0, 0.0)


def deck_inner(section, deck_ref, metric_ref, base_ref, strain_out, lap_out, rest_out):
    lane = iota((SPAN, DCOLS), 1)
    half = (0.5 * WEIGHTS[section] * TIME_STEP) * deck_keep()
    for r in range(DROWS):
        here = fields(deck_ref, (r,))
        base = None if base_ref is None else fields(base_ref, (r,))
        m = deck_metric(metric_ref, r)
        g1, g2 = m[0] * m[0] + m[1] * m[1], m[2] * m[2] + m[3] * m[3]
        speed_eta, speed_span = half * (m[2] * here[0] + m[3] * here[1]), half * here[2]
        strain = None
        for c in range(3):
            f = here[c]
            plus_eta = jnp.where(lane == DCOLS - 1, 0.0, pltpu.roll(f, DCOLS - 1, 1))
            minus_eta = jnp.where(lane == 0, 0.0, pltpu.roll(f, 1, 1))
            plus_span = pltpu.roll(f, SPAN - 1, 0)
            minus_span = pltpu.roll(f, 1, 0)
            b, s = plus_eta - minus_eta, plus_span - minus_span
            square = b * b + s * s
            strain = square if strain is None else strain + square
            doubled = 2.0 * f
            at = slice(c * SPAN, (c + 1) * SPAN)
            lap_out[r, at, :] = g2 * (plus_eta - doubled + minus_eta) + (plus_span - doubled + minus_span) - g1 * doubled
            rest_out[r, at, :] = carried(section, f, base, c) - (speed_eta * b + speed_span * s)
        strain_out[r] = strain


def deck_outer(section, here, minus_xi, plus_xi, m, part):
    strain, lap, rest = part
    step = (WEIGHTS[section] * TIME_STEP) * deck_keep()
    a = [plus_xi[c] - minus_xi[c] for c in range(3)]
    strain = strain + (a[0] * a[0] + a[1] * a[1] + a[2] * a[2])
    stretched = 1.0 + 0.25 * strain
    viscosity = (SMAGORINSKY * step) * (stretched * lax.rsqrt(stretched))
    speed_xi = (0.5 * step) * (m[0] * here[0] + m[1] * here[1])
    g1 = m[0] * m[0] + m[1] * m[1]
    return [
        rest[c] + (viscosity * (lap[c] + g1 * (plus_xi[c] + minus_xi[c])) - speed_xi * a[c])
        for c in range(3)
    ]


def carried(section, f, base, c):
    if section == 0:
        return f
    if section == 1:
        return 0.75 * base[c] + 0.25 * f
    return base[c] * (1.0 / 3.0) + (2.0 / 3.0) * f


def inner_part(here, minus_xi, plus_xi, keep, base, section):
    half = (0.5 * WEIGHTS[section] * TIME_STEP) * keep
    speed_xi, speed_span = half * here[0], half * here[2]
    strain, lap, rest = None, [], []
    for c in range(3):
        f = here[c]
        plus_span = pltpu.roll(f, SPAN - 1, 0)
        minus_span = pltpu.roll(f, 1, 0)
        a = plus_xi[c] - minus_xi[c]
        s = plus_span - minus_span
        square = a * a + s * s
        strain = square if strain is None else strain + square
        lap.append((plus_xi[c] + minus_xi[c]) + (plus_span + minus_span) - 6.0 * f)
        advection = speed_xi * a + speed_span * s
        rest.append(carried(section, f, base, c) - advection)
    return strain, lap, rest


def outer_part(speed, b, around, part, keep, section):
    strain, lap, rest = part
    step = (WEIGHTS[section] * TIME_STEP) * keep
    strain = strain + (b[0] * b[0] + b[1] * b[1] + b[2] * b[2])
    stretched = 1.0 + 0.25 * strain
    viscosity = (SMAGORINSKY * step) * (stretched * lax.rsqrt(stretched))
    speed_eta = (0.5 * step) * speed
    return [
        rest[c] + (viscosity * (lap[c] + around[c]) - speed_eta * b[c])
        for c in range(3)
    ]


def inner_rows(section, back_ref, keep_ref, base_ref, strain_out, lap_out, rest_out, b_out):
    lane = iota((SPAN, COLS), 1)
    for r in range(1, ROWS - 1):
        strain, lap, rest = inner_part(
            fields(back_ref, (r,)),
            fields(back_ref, (r - 1,)),
            fields(back_ref, (r + 1,)),
            keep_ref[r, 0:1, :],
            None if base_ref is None else fields(base_ref, (r,)),
            section,
        )
        strain_out[r - 1] = strain
        for c in range(3):
            f = back_ref[r, c * SPAN : (c + 1) * SPAN, :]
            plus_eta = jnp.where(lane == COLS - 1, 0.0, pltpu.roll(f, COLS - 1, 1))
            minus_eta = jnp.where(lane == 0, 0.0, pltpu.roll(f, 1, 1))
            b_out[r - 1, c * SPAN : (c + 1) * SPAN, :] = plus_eta - minus_eta
            lap_out[r - 1, c * SPAN : (c + 1) * SPAN, :] = lap[c] + (plus_eta + minus_eta)
            rest_out[r - 1, c * SPAN : (c + 1) * SPAN, :] = rest[c]


def fields(ref, at):
    return [ref[at + (slice(c * SPAN, (c + 1) * SPAN), slice(None))] for c in range(3)]


def section_kernel(section, *refs):
    refs = list(refs)
    deck_ref, back_ref, column_first, column_second, row_first, row_second, metric_ref, keep_ref = refs[:8]
    strain_ref, lap_ref, rest_ref, b_ref, deck_strain, deck_lap, deck_rest = refs[8:15]
    del refs[:15]
    base_back = None
    if section > 0:
        base_back = refs[0]
        del refs[0]
    last = section == 2
    if last:
        deck_hbm, back_hbm, deck_out, back_out, deck_sems, back_sems = refs
        copies = []

        def send(rows, r, whole, sems):
            copies.append(pltpu.make_async_copy(rows.at[r], whole.at[:, r, :], sems.at[r]))
            copies[-1].start()

    else:
        far_ref, near_ref, deck_out, back_out, answer_out, deck_pieces, back_pieces = refs
        clear_pieces(deck_pieces, back_pieces)
    column, line, tile = position()
    odd = lax.rem(tile, 2) == 0
    odd_line = lax.rem(line, 2) == 0
    west_end = (column > 0).astype(F32)
    east_end = (column < lax.axis_size("gy") - 1).astype(F32)

    def ordered(flag, first, second, at):
        a, b = first[at], second[at]
        return jnp.where(flag, a, b), jnp.where(flag, b, a)

    spans = [slice(c * SPAN, (c + 1) * SPAN) for c in range(3)]
    across = [ordered(odd, row_first, row_second, (at, slice(None))) for at in spans]
    beside = []
    halves = [
        ordered(odd, row_first, row_second, (slice(PLANES, PLANES + 8), slice(i * COLS, (i + 1) * COLS)))
        for i in range(2)
    ]
    for side in range(2):
        cells = jnp.concatenate([halves[0][side], halves[1][side], jnp.zeros((COLS - 16, COLS), F32)], axis=0)
        beside.append(cells.T)
    north_end = (line > 0).astype(F32)
    south_end = (line < lax.axis_size("grid") * lax.axis_size("gx") - 1).astype(F32)
    along = [ordered(odd_line, column_first, column_second, (at, slice(None))) for at in spans]
    along = [(before * north_end, after * south_end) for before, after in along]
    for r in range(DROWS):
        if r == 0:
            minus = [a[0] for a in across]
            plus = fields(deck_ref, (1,))
        else:
            minus = fields(deck_ref, (0,))
            plus = [a[1] for a in across]
        part = deck_strain[r], fields(deck_lap, (r,)), fields(deck_rest, (r,))
        new = deck_outer(section, fields(deck_ref, (r,)), minus, plus, deck_metric(metric_ref, r), part)
        for c in range(3):
            deck_out[r, c * SPAN : (c + 1) * SPAN, :] = new[c]
        if last:
            send(deck_out, r, deck_hbm, deck_sems)
        else:
            stack_deck(deck_pieces, r, jnp.concatenate(new, axis=0))
    lane = iota((SPAN, COLS), 1)
    for r in range(ROWS):
        keep = keep_ref[r, 0:1, :]
        west = [beside[0][at, r : r + 1] * west_end for at in spans]
        east = [beside[1][at, r : r + 1] * east_end for at in spans]
        if 0 < r < ROWS - 1:
            part = strain_ref[r - 1], fields(lap_ref, (r - 1,)), fields(rest_ref, (r - 1,))
            inside = fields(b_ref, (r - 1,))
            b = [inside[c] + jnp.where(lane == COLS - 1, east[c], jnp.where(lane == 0, -west[c], 0.0)) for c in range(3)]
            around = [jnp.where(lane == COLS - 1, east[c], jnp.where(lane == 0, west[c], 0.0)) for c in range(3)]
        else:
            here = fields(back_ref, (r,))
            plus_eta = [jnp.where(lane == COLS - 1, east[c], pltpu.roll(here[c], COLS - 1, 1)) for c in range(3)]
            minus_eta = [jnp.where(lane == 0, west[c], pltpu.roll(here[c], 1, 1)) for c in range(3)]
            minus = fields(back_ref, (r - 1,)) if r > 0 else [a[0] for a in along]
            plus = fields(back_ref, (r + 1,)) if r < ROWS - 1 else [a[1] for a in along]
            base = fields(base_back, (r,)) if section > 0 else None
            part = inner_part(here, minus, plus, keep, base, section)
            b = [plus_eta[c] - minus_eta[c] for c in range(3)]
            around = [plus_eta[c] + minus_eta[c] for c in range(3)]
        new = outer_part(back_ref[r, spans[1], :], b, around, part, keep, section)
        for c in range(3):
            back_out[r, c * SPAN : (c + 1) * SPAN, :] = new[c]
        if last:
            send(back_out, r, back_hbm, back_sems)
        else:
            stack_back(back_pieces, r, jnp.concatenate(new, axis=0))
    if last:
        for c in copies:
            c.wait()
    else:
        answer(far_ref, near_ref, deck_pieces, back_pieces, answer_out)


def local(deck_fields, back_fields, metrics, donors, stencil, fringe_cells):
    group = ("gy", "gx")
    everyone = ("grid", "gx", "gy")

    def exchange(x):
        return lax.all_to_all(x, group, split_axis=0, concat_axis=0, tiled=True)

    count = lax.axis_size("grid") * lax.axis_size("gx") * lax.axis_size("gy")
    across_y = lax.axis_size("gy")

    def pairs(step, first, periodic=False):
        out = []
        for t in range(count):
            if (t // step) % 2 == first:
                other = (t + step) % count
                if periodic or t + step < count:
                    out += [(t, other), (other, t)]
                else:
                    out += [(t, t ^ 2), (other, other ^ 2)]
        return out

    deck_in = deck_fields.reshape(PLANES, DROWS, DCOLS)
    back_in = back_fields.reshape(PLANES, ROWS, COLS)
    request, placing, rim_map, near_map, rim_keep = call(
        route_kernel,
        [
            ((MEMBERS, 1, 128), F32),
            ((MEMBERS, 3 * CAP), F32),
            ((SLOTS, 3 * COLS), BF16),
            ((NEAR * MEMBERS, 2 * COLS), BF16),
            ((3, 8, COLS), F32),
        ],
        [donors.reshape(1, FRINGE), stencil.reshape(FRINGE, 4).T, fringe_cells],
        scratch=[
            pltpu.VMEM((1, FRINGE), jnp.int32),
            pltpu.VMEM((4, FRINGE), jnp.int32),
            pltpu.VMEM((1, FRINGE - NEAR), jnp.int32),
            pltpu.SemaphoreType.DMA((3,)),
        ],
        hbm_at=(0, 1, 2),
        name="route",
    )
    request = exchange(request)
    pieces = [pltpu.VMEM((256, DROWS * DCOLS), BF16), pltpu.VMEM((256, ROWS * COLS), BF16)]
    deck, back_state, far, near, answers = call(
        first_answer_kernel,
        [
            ((DROWS, PLANES, DCOLS), F32),
            ((ROWS, PLANES, COLS), F32),
            ((SLOTS, DROWS * DCOLS), BF16),
            ((NEAR * MEMBERS, ROWS * COLS), BF16),
            ((MEMBERS, 1, PACKED), F32),
        ],
        [request, deck_in, back_in],
        scratch=[pltpu.VMEM((MEMBERS, 128), F32)]
        + pieces
        + [
            pltpu.SemaphoreType.DMA((DROWS,)),
            pltpu.SemaphoreType.DMA((ROWS,)),
        ],
        hbm_at=(1, 2),
        name="first_answer",
    )
    base = None
    for section in range(3):
        got = exchange(answers)
        got_pieces, deck, column_first, column_second, row_first, row_second = call(
            rim_kernel,
            [
                ((2 * PLANES, SLOTS), BF16),
                ((DROWS, PLANES, DCOLS), F32),
                ((PLANES, COLS), F32),
                ((PLANES, COLS), F32),
                ((PLANES + 8, DCOLS), F32),
                ((PLANES + 8, DCOLS), F32),
            ],
            [got, rim_map, near_map, rim_keep, deck, back_state],
            scratch=[pltpu.VMEM((MEMBERS, PACKED), F32)],
            name="rim",
        )
        row_first = lax.ppermute(row_first, everyone, pairs(1, 1, True))
        row_second = lax.ppermute(row_second, everyone, pairs(1, 0, True))
        column_first = lax.ppermute(column_first, everyone, pairs(across_y, 1))
        column_second = lax.ppermute(column_second, everyone, pairs(across_y, 0))
        inner = [
            ((ROWS - 2, SPAN, COLS), F32),
            ((ROWS - 2, PLANES, COLS), F32),
            ((ROWS - 2, PLANES, COLS), F32),
            ((ROWS - 2, PLANES, COLS), F32),
            ((DROWS, SPAN, DCOLS), F32),
            ((DROWS, PLANES, DCOLS), F32),
            ((DROWS, PLANES, DCOLS), F32),
        ]
        if section == 0:
            back_state, fill_map, keep, *inner = call(
                first_fill_kernel,
                [((ROWS, PLANES, COLS), F32), ((SLOTS, ROWS * COLS), BF16), ((ROWS, 8, COLS), F32)] + inner,
                [got_pieces, placing, back_state, deck, metrics],
                name="fill",
            )
            base = [deck, back_state]
        else:
            back_state, *inner = call(
                functools.partial(fill_kernel, section),
                [((ROWS, PLANES, COLS), F32)] + inner,
                [got_pieces, fill_map, keep, back_state, deck, metrics] + base,
                name="fill",
            )
        ins = [deck, back_state, column_first, column_second, row_first, row_second, metrics, keep] + inner
        if section > 0:
            ins.append(base[1])
        kernel = functools.partial(section_kernel, section)
        if section < 2:
            deck, back_state, answers = call(
                kernel,
                [
                    ((DROWS, PLANES, DCOLS), F32),
                    ((ROWS, PLANES, COLS), F32),
                    ((MEMBERS, 1, PACKED), F32),
                ],
                ins + [far, near],
                scratch=pieces,
                name="section",
            )
        else:
            deck, back_state = call(
                kernel,
                [((PLANES, DROWS, DCOLS), F32), ((PLANES, ROWS, COLS), F32)],
                ins,
                scratch=[
                    pltpu.VMEM((DROWS, PLANES, DCOLS), F32),
                    pltpu.VMEM((ROWS, PLANES, COLS), F32),
                    pltpu.SemaphoreType.DMA((DROWS,)),
                    pltpu.SemaphoreType.DMA((ROWS,)),
                ],
                outs_in=pl.ANY,
                name="section",
            )
    return deck.reshape(deck_fields.shape), back_state.reshape(back_fields.shape)


def solution(mesh):
    return jax.shard_map(
        local,
        mesh=mesh,
        in_specs=(
            P(None, None, ("grid", "gx", "gy"), None),
            P(None, None, ("grid", "gx"), "gy"),
            P(None, ("grid", "gx", "gy"), None),
            P(("grid", "gx", "gy"), None, None),
            P(("grid", "gx", "gy"), None, None),
            P(("grid", "gx", "gy"), None),
        ),
        out_specs=(P(None, None, ("grid", "gx", "gy"), None), P(None, None, ("grid", "gx"), "gy")),
        check_vma=False,
    )
```
